32 devices in a mesh: band: 2 (over x), tile: 8 (over z, y), bin: 2 (over core).
Axes of the slice: x: 2, y: 2, z: 4, core: 2. Of those that a mesh axis runs over, the one named last changes fastest.
Arguments:
- spectra: float32 [1296, 8192], P(None, ('band', 'tile', 'bin')), parts along dimension 1, may hold values from 0.25 to 2
- wind: float32 [2, 8192], P(None, ('band', 'tile', 'bin')), parts along dimension 1, may hold values from -5 to 5
- mask: int32 [64, 256], P(None, 'band'), parts along dimension 1, may hold values from 0 to 1, as said below
- dia_index: int32 [2, 2, 4, 1296], replicated, may hold values from 0 to 1295, as said below
- dia_weight: bfloat16 [2, 2, 4, 1296], replicated, may hold values from 0.099609375 to 0.5
- nl_coef: float32 [1296], replicated, may hold values from 0.01 to 0.1
Outputs:
- propagated: float32 [1296, 64, 256], P('bin', 'tile', 'band'), parts along dimension 2
The draws below stay inside these ranges and needn't reach their ends.
There are 2 independent parts, one for each index of `band`. The reference program is written for one: setup_inputs(seed, part) draws one part's arguments, and reference() takes and returns one part's arrays. A program takes and returns all parts, laid end to end along the dimension named above; an argument that names none is the same for every part. Nothing has to cross between parts.
Inputs may be any that keep to these rules, and one draw needn't show every extreme that they name: `mask`: exactly 4096 cells are sea; at least one tile of 8 columns is entirely sea. `dia_index`: for each mirror, member and bin, the corners are frequencies f and f + 1 with f in 0..34 and directions d and d + 1 modulo 36: four different bins.
All inputs are finite; a program needn't handle non-finite values.
Results may differ from the reference program's by a relative error of at most 0.0011.
Values sent between devices are 32-bit elements; how exact they have to be, the bound alone decides.
No kernel may reach another device: no remote copies, remote signals or barrier semaphores. Data moves between devices by JAX's collectives and lax.ppermute only.
A program may use at most 128 MiB of HBM per device.

```python
import math
import jax
import jax.numpy as jnp
from jax import lax

NF = 36
NTH = 36
NB = 1296
CX = 8
NY = 128
STEPS = 2
NX = 64
GROUP = 16
PTS_DEV = 256
SEA = 4096


def draw_mask(key, part):
    cell_total = NX * NY
    tile_cells = CX * NY
    tile_count = NX // CX
    first_key, second_key, third_key = jax.random.split(key, 3)
    sea_order = jax.random.permutation(first_key, cell_total).astype(jnp.int32)
    tile_bias = jax.random.randint(second_key, (tile_count,), 0, 4)
    full_tile = jax.random.randint(third_key, (), 0, tile_count)
    tile_of = jnp.arange(cell_total) // tile_cells
    score = sea_order + tile_bias[tile_of] * (cell_total // 4) + jnp.where(tile_of == full_tile, 2 * cell_total, 0)
    ordering = jnp.argsort(score, stable=True)
    chosen = ordering[cell_total - SEA:]
    flat_mask = jnp.zeros((cell_total,), jnp.int32).at[chosen].set(1)
    return flat_mask.reshape(NX, NY)


def draw_dia_index(key, part):
    first_key, second_key = jax.random.split(key)
    freq_step = jax.random.randint(first_key, (2, 2, NF * NTH), 1, 4)
    turning = jax.random.randint(second_key, (2, 2, NF * NTH), 0, 4)
    bin_range = jnp.arange(NF * NTH)
    frequency = bin_range // NTH
    direction = bin_range % NTH
    member_sign = jnp.array([1, -1])[None, :, None]
    mirror_sign = jnp.array([1, -1])[:, None, None]
    lower_freq = jnp.clip(frequency[None, None, :] + member_sign * freq_step, 0, NF - 2)
    direction_base = direction[None, None, :] + member_sign * mirror_sign * turning
    corner_list = []
    for corner in range(4):
        freq_corner = lower_freq + corner // 2
        dir_corner = (direction_base + corner % 2) % NTH
        corner_list.append(freq_corner * NTH + dir_corner)
    return jnp.stack(corner_list, axis=2).astype(jnp.int32)


def steps_of(rng, shape, pieces, low, high):
    level = 1.0
    for dim, blocks in pieces:
        steps = jax.random.uniform(jax.random.fold_in(jax.random.fold_in(rng, 6), dim), (blocks,), jnp.float32, low / len(pieces), high / len(pieces))
        level = level * jnp.repeat(jnp.exp(steps), shape[dim] // blocks).reshape((-1,) + (1,) * (len(shape) - 1 - dim))
    return level


def normal_values(stream_key, shape, deviation, most, cuts=(), dtype=jnp.bfloat16):
    loudness = steps_of(stream_key, shape, cuts, -0.22, 0.18) if cuts else 1.0
    values = jax.random.normal(stream_key, shape, jnp.float32) * deviation * loudness
    return jnp.minimum(jnp.maximum(values, -most), most).astype(dtype)


def setup_inputs(seed: int = 0, part: int = 0) -> dict:
    arg_keys = jax.random.split(jax.random.key(seed), 7)
    part_keys = jax.random.split(jax.random.fold_in(arg_keys[6], part), 7)
    return {
        "spectra": jnp.clip(jnp.exp(math.log(2.0) - 2.0794415 * jax.random.uniform(part_keys[0], (NB, SEA), jnp.float32) ** steps_of(part_keys[0], (NB, SEA), ((1, 16),), -0.2, 0.2)), 0.25, 2.0),
        "wind": normal_values(part_keys[1], (2, SEA), 1.0, 5.0, ((1, 16),), jnp.float32),
        "mask": draw_mask(jax.random.fold_in(jax.random.fold_in(arg_keys[6], part), 71), part),
        "dia_index": draw_dia_index(jax.random.fold_in(arg_keys[6], 71), part),
        "dia_weight": jnp.clip(jax.random.uniform(arg_keys[4], (2, 2, 4, NB), jnp.float32, 0.099609375, 0.5), 0.099609375, 0.5).astype(jnp.bfloat16),
        "nl_coef": jnp.clip(jnp.exp(jax.random.uniform(arg_keys[5], (NB,), jnp.float32, math.log(0.01), math.log(0.1))), 0.01, 0.1),
    }


LAMBDA = 0.25
COEF_THREE = (1.0 + LAMBDA) ** -4
COEF_FOUR = (1.0 - LAMBDA) ** -4
COEF_BOTH = (1.0 - LAMBDA * LAMBDA) ** -4
CFL_LIMIT = 0.8
WIND_RATE = 0.2


def bin_tables(count_bins):
    bin_range = jnp.arange(count_bins)
    theta = 2.0 * math.pi * (bin_range % NTH).astype(jnp.float32) / NTH
    group_speed = CFL_LIMIT * 1.1 ** (-(bin_range // NTH).astype(jnp.float32))
    return jnp.cos(theta), jnp.sin(theta), group_speed


def interpolate(values, table, weight):
    accumulated = jnp.zeros(values.shape, jnp.float32)
    for corner in range(4):
        accumulated = accumulated + weight[corner].astype(jnp.float32)[:, None] * values[table[corner]].astype(jnp.float32)
    return accumulated


def spread_back(values, table, weight):
    accumulated = jnp.zeros(values.shape, jnp.float32)
    for corner in range(4):
        accumulated = accumulated.at[table[corner]].add(weight[corner].astype(jnp.float32)[:, None] * values.astype(jnp.float32))
    return accumulated


def coupling(spectra, third_member, fourth_member, nl_coef):
    return nl_coef[:, None] * (spectra * spectra * (COEF_THREE * third_member + COEF_FOUR * fourth_member) - 2.0 * COEF_BOTH * spectra * third_member * fourth_member)


def upwind(padded, courant, axis, length):
    def window(offset, amount):
        return lax.slice_in_dim(padded, offset, offset + amount, axis=axis)
    faces = length + 1
    left_two = window(0, faces)
    left_one = window(1, faces)
    right_one = window(2, faces)
    right_two = window(3, faces)
    curvature = jnp.where(courant >= 0.0, right_one - 2.0 * left_one + left_two, right_two - 2.0 * right_one + left_one)
    face_value = 0.5 * (left_one + right_one) - 0.5 * courant * (right_one - left_one) - (1.0 - courant * courant) / 6.0 * curvature
    face_flux = courant * face_value
    centre = window(2, length)
    return centre - (lax.slice_in_dim(face_flux, 1, faces, axis=axis) - lax.slice_in_dim(face_flux, 0, length, axis=axis))


def reference(spectra, wind, mask, dia_index, dia_weight, nl_coef):
    rounded = spectra.astype(jnp.bfloat16)
    nonlinear = jnp.zeros(spectra.shape, jnp.float32)
    for mirror in range(2):
        third_member = interpolate(rounded, dia_index[mirror, 0], dia_weight[mirror, 0])
        fourth_member = interpolate(rounded, dia_index[mirror, 1], dia_weight[mirror, 1])
        interaction = coupling(spectra, third_member, fourth_member, nl_coef)
        interaction_low = interaction.astype(jnp.bfloat16)
        nonlinear = nonlinear - 2.0 * interaction + spread_back(interaction_low, dia_index[mirror, 0], dia_weight[mirror, 0]) + spread_back(interaction_low, dia_index[mirror, 1], dia_weight[mirror, 1])
    cosine, sine_theta, group_speed = bin_tables(NB)
    wind_drive = jnp.maximum(wind[0][None, :] * cosine[:, None] + wind[1][None, :] * sine_theta[:, None], 0.0)
    relaxed = spectra + nonlinear + WIND_RATE * wind_drive * spectra
    flat_mask = mask.reshape(-1)
    sea_cells = jnp.argsort(1 - flat_mask, stable=True)[:SEA].astype(jnp.int32)
    column = jnp.arange(SEA)
    number = ((column % PTS_DEV) * GROUP + column // PTS_DEV).astype(jnp.int32)
    cell_of = sea_cells[number]
    spectra_grid = jnp.zeros((NB, NX * NY), jnp.float32).at[:, cell_of].set(relaxed).reshape(NB, NX, NY)
    sea_factor = mask.astype(jnp.float32)
    courant_x = (group_speed * cosine)[:, None, None]
    courant_y = (group_speed * sine_theta)[:, None, None]
    for substep in range(STEPS):
        padded = jnp.concatenate([spectra_grid[:, NX - 2:], spectra_grid, spectra_grid[:, :2]], axis=1)
        spectra_grid = upwind(padded, courant_x, 1, NX) * sea_factor
        padded = jnp.pad(spectra_grid, ((0, 0), (0, 0), (2, 2)))
        spectra_grid = upwind(padded, courant_y, 2, NY) * sea_factor
    return spectra_grid
```

```python
import functools
import math

import jax
import jax.numpy as jnp
import numpy as np
from jax import lax
from jax.experimental import pallas as pl
from jax.experimental.pallas import tpu as pltpu
from jax.sharding import PartitionSpec as P

NTH = 36
STEPS = 2
LANES = 128
ROWS = 256

LAMBDA = 0.25
COEF_THREE = (1.0 + LAMBDA) ** (-4)
COEF_FOUR = (1.0 - LAMBDA) ** (-4)
COEF_BOTH = (1.0 - LAMBDA * LAMBDA) ** (-4)
CFL_LIMIT = 0.8
WIND_RATE = 0.2


def round_up(value, step):
    return -(-value // step) * step


def bin_tables(count_bins):
    bin_range = np.arange(count_bins)
    theta = 2.0 * math.pi * (bin_range % NTH) / NTH
    group_speed = CFL_LIMIT * 1.1 ** (-(bin_range // NTH).astype(np.float64))
    return np.cos(theta), np.sin(theta), group_speed


def stencil(courant):
    bend = (1.0 - courant * courant) / 6.0
    up = courant >= 0.0
    zero = np.zeros_like(courant)
    left = courant * np.where(up, -bend, zero)
    here = courant * (0.5 + 0.5 * courant + np.where(up, 2.0 * bend, -bend))
    right = courant * (0.5 - 0.5 * courant + np.where(up, -bend, 2.0 * bend))
    far = courant * np.where(up, zero, -bend)
    return np.stack([left, here - left, 1.0 + right - here, far - right, -far])


def source_kernel(owners, per, spectra, wind, index, weight, nl_coef, tables, out,
                  index_pad, weight_pad, nl_pad, flat_t, low_t, wind_t, matrix, inter, total):
    count_bins, points = spectra.shape
    padded = flat_t.shape[1]
    chunks = padded // LANES
    whole = count_bins // LANES
    rest = count_bins - whole * LANES
    index_pad[...] = jnp.full(index_pad.shape, -1, jnp.int32)
    index_pad[:, :count_bins] = index[...]
    weight_pad[...] = jnp.zeros(weight_pad.shape, jnp.float32)
    weight_pad[:, :count_bins] = weight[...].astype(jnp.float32)
    nl_pad[...] = jnp.zeros(nl_pad.shape, jnp.float32)
    nl_pad[:, :count_bins] = nl_coef[...]
    for half in range(points // LANES):
        span = slice(half * LANES, (half + 1) * LANES)
        for block in range(chunks):
            if block < whole:
                values = spectra[block * LANES:(block + 1) * LANES, span]
            else:
                values = jnp.concatenate(
                    [spectra[whole * LANES:, span], jnp.zeros((LANES - rest, LANES), jnp.float32)], axis=0
                )
            turned = values.T
            flat_t[span, block * LANES:(block + 1) * LANES] = turned
            low_t[span, block * LANES:(block + 1) * LANES] = turned.astype(jnp.bfloat16)
        drive = jnp.concatenate([wind[:, span], jnp.zeros((LANES - 2, LANES), jnp.float32)], axis=0)
        wind_t[span, :] = drive.T

    def chunk_step(chunk, carry):
        lane = pl.multiple_of(chunk * LANES, LANES)
        lanes = pl.ds(lane, LANES)
        wide = pl.multiple_of(chunk * 4 * LANES, 4 * LANES)
        rows_index = [index_pad[pl.ds(r, 1), lanes] for r in range(16)]
        rows_weight = [weight_pad[pl.ds(r, 1), lanes] for r in range(16)]
        members = [jnp.zeros((points, 2 * LANES), jnp.float32) for _ in range(2)]
        for start in range(0, padded, ROWS):
            size = min(ROWS, padded - start)
            place = lax.broadcasted_iota(jnp.int32, (size, LANES), 0) + start
            for mirror in range(2):
                for member in range(2):
                    block = jnp.zeros((size, LANES), jnp.float32)
                    for corner in range(4):
                        r = mirror * 8 + member * 4 + corner
                        block = jnp.where(place == rows_index[r], rows_weight[r], block)
                    matrix[start:start + size, pl.ds(wide + (mirror * 2 + member) * LANES, LANES)] = (
                        block.astype(jnp.bfloat16)
                    )
                members[mirror] = members[mirror] + jnp.dot(
                    low_t[:, start:start + size],
                    matrix[start:start + size, pl.ds(wide + mirror * 2 * LANES, 2 * LANES)],
                    preferred_element_type=jnp.float32,
                )
        values = flat_t[:, lanes]
        coef = nl_pad[:, lanes]
        drive = jnp.maximum(
            wind_t[:, 0:1] * tables[0:1, lanes] + wind_t[:, 1:2] * tables[1:2, lanes], 0.0
        )
        base = values + WIND_RATE * drive * values
        for mirror in range(2):
            third = members[mirror][:, :LANES]
            fourth = members[mirror][:, LANES:]
            interaction = coef * (
                values * values * (COEF_THREE * third + COEF_FOUR * fourth)
                - 2.0 * COEF_BOTH * values * third * fourth
            )
            base = base - 2.0 * interaction
            for half in range(points // LANES):
                span = slice(half * LANES, (half + 1) * LANES)
                turned = interaction[span].T.astype(jnp.bfloat16)
                for member in range(2):
                    inter[pl.ds(wide + (mirror * 2 + member) * LANES, LANES), span] = turned
        for half in range(points // LANES):
            span = slice(half * LANES, (half + 1) * LANES)
            total[lanes, span] = base[span].T
        return carry

    lax.fori_loop(0, chunks, chunk_step, 0)
    for start in range(0, padded, ROWS):
        size = min(ROWS, padded - start)
        total[start:start + size, :] += jnp.dot(
            matrix[start:start + size, :], inter[...], preferred_element_type=jnp.float32
        )
    tiles, halves = owners
    half_bins = count_bins // halves
    for tile in range(tiles):
        for side in range(halves):
            first = side * half_bins + tile * per
            valid = min(per, half_bins - tile * per)
            if valid <= 0:
                continue
            for half in range(points // LANES):
                out[tile * halves + side, half * per:half * per + valid, :] = total[
                    first:first + valid, half * LANES:(half + 1) * LANES
                ]


def source_terms(owners, per, spectra, wind, index, weight, nl_coef):
    count_bins, points = spectra.shape
    padded = round_up(count_bins, LANES)
    cosine, sine, _ = bin_tables(count_bins)
    tables = np.zeros((2, padded), np.float32)
    tables[0, :count_bins] = cosine
    tables[1, :count_bins] = sine
    group = owners[0] * owners[1]
    rows = per * (points // LANES)
    return pl.pallas_call(
        functools.partial(source_kernel, owners, per),
        out_shape=jax.ShapeDtypeStruct((group, rows, LANES), jnp.float32),
        scratch_shapes=[
            pltpu.VMEM((16, padded), jnp.int32),
            pltpu.VMEM((16, padded), jnp.float32),
            pltpu.VMEM((1, padded), jnp.float32),
            pltpu.VMEM((points, padded), jnp.float32),
            pltpu.VMEM((points, padded), jnp.bfloat16),
            pltpu.VMEM((points, LANES), jnp.float32),
            pltpu.VMEM((padded, 4 * padded), jnp.bfloat16),
            pltpu.VMEM((4 * padded, points), jnp.bfloat16),
            pltpu.VMEM((padded, points), jnp.float32),
        ],
        compiler_params=pltpu.CompilerParams(vmem_limit_bytes=52 * 1024 * 1024),
        name="source_terms",
    )(spectra, wind, index, weight, nl_coef, jnp.asarray(tables))


def propagate_kernel(per, columns_tile, base, got, rel, taps, out, ranked, split, first, second):
    group = got.shape[0]
    columns = rel.shape[0]
    halves = got.shape[1] // per
    padded = first.shape[1]
    split_rows = split.shape[0] // 2
    fill = jnp.zeros((LANES - per, LANES), jnp.float32) if per < LANES else None

    def order(owner, carry):
        for half in range(halves):
            values = got[owner, half * per:(half + 1) * per, :]
            if fill is not None:
                values = jnp.concatenate([values, fill], axis=0)
            ranked[pl.ds(half * LANES * group + owner, LANES, stride=group), :] = values.T
        return carry

    lax.fori_loop(0, group, order, 0)

    rank_tiles = ranked.shape[0] // LANES

    def halve(tile, carry):
        start = pl.multiple_of(tile * LANES, LANES)
        turned = ranked[pl.ds(start, LANES), :].T[:split_rows]
        high = turned.astype(jnp.bfloat16)
        split[:split_rows, pl.ds(start, LANES)] = high
        split[split_rows:, pl.ds(start, LANES)] = (turned - high.astype(jnp.float32)).astype(jnp.bfloat16)
        return carry

    lax.fori_loop(0, rank_tiles, halve, 0)
    split[:, rank_tiles * LANES:] = jnp.zeros((2 * split_rows, LANES), jnp.bfloat16)

    place = lax.broadcasted_iota(jnp.int32, (2 * LANES, LANES), 0)

    def expand(column, carry):
        start = pl.multiple_of(base[column], LANES)
        onehot = jnp.where(place == rel[pl.ds(column, 1), :], 1.0, 0.0).astype(jnp.bfloat16)
        both = jnp.dot(split[:, pl.ds(start, 2 * LANES)], onehot, preferred_element_type=jnp.float32)
        first[column] = both[:padded] + both[split_rows:split_rows + padded]
        return carry

    lax.fori_loop(0, columns, expand, 0)

    lane = lax.broadcasted_iota(jnp.int32, (8, LANES), 1)
    for tile in range(padded // 8):
        span = slice(tile * 8, (tile + 1) * 8)
        x_taps = [jnp.broadcast_to(taps[span, k:k + 1], (8, LANES)) for k in range(5)]
        y_taps = []
        for k in range(5):
            tap = jnp.broadcast_to(taps[span, 5 + k:6 + k], (8, LANES))
            shift = k - 2
            inside = (lane + shift >= 0) & (lane + shift < LANES)
            y_taps.append(jnp.where(inside, tap, 0.0))
        valid = min(8, per - tile * 8)

        def sweep(source, target, column):
            value = x_taps[2] * source[column, span, :]
            for k in (0, 1, 3, 4):
                if isinstance(column, int):
                    other = (column + k - 2) % columns
                else:
                    other = column + (k - 2)
                    other = jnp.where(other < 0, other + columns, other)
                    other = jnp.where(other >= columns, other - columns, other)
                value = value + x_taps[k] * source[other, span, :]
            sea = jnp.where(rel[pl.ds(column, 1), :] >= 0, 1.0, 0.0)
            value = value * sea
            moved = y_taps[2] * value
            for k in (0, 1, 3, 4):
                moved = moved + y_taps[k] * pltpu.roll(value, (2 - k) % LANES, 1)
            return moved * sea

        def one(column, carry):
            second[column, span, :] = sweep(first, second, column)
            return carry

        lax.fori_loop(0, columns, one, 0, unroll=8)

        def two(column, carry):
            result = sweep(second, None, column)
            owner = column // columns_tile
            start = (owner * per + tile * 8) * columns_tile + column % columns_tile
            if valid == 8:
                out[pl.ds(start, 8, stride=columns_tile), :] = result
            else:
                for row in range(valid):
                    out[pl.ds(start + row * columns_tile, 1), :] = result[row:row + 1]
            return carry

        lax.fori_loop(0, columns, two, 0, unroll=8)


def propagate(per, columns_tile, base, got, rel, taps):
    group, rows, _ = got.shape
    columns = rel.shape[0]
    points = rows // per * LANES
    padded = round_up(per, 8)
    split_rows = round_up(per, 16)
    smem = pl.BlockSpec(memory_space=pltpu.SMEM)
    vmem = pl.BlockSpec(memory_space=pltpu.VMEM)
    return pl.pallas_call(
        functools.partial(propagate_kernel, per, columns_tile),
        out_shape=jax.ShapeDtypeStruct((columns * per, LANES), jnp.float32),
        in_specs=[smem, vmem, vmem, vmem],
        out_specs=vmem,
        scratch_shapes=[
            pltpu.VMEM((group * points, LANES), jnp.float32),
            pltpu.VMEM((2 * split_rows, group * points + LANES), jnp.bfloat16),
            pltpu.VMEM((columns, padded, LANES), jnp.float32),
            pltpu.VMEM((columns, padded, LANES), jnp.float32),
        ],
        compiler_params=pltpu.CompilerParams(vmem_limit_bytes=52 * 1024 * 1024),
        name="propagate",
    )(base, got, rel, taps)


def shards(spectra, wind, mask, dia_index, dia_weight, nl_coef):
    count_bins = spectra.shape[0]
    tiles = lax.axis_size("tile")
    halves = lax.axis_size("bin")
    columns, latitudes = mask.shape
    columns_tile = columns // tiles
    half_bins = count_bins // halves
    per = -(-half_bins // tiles)
    padded = round_up(per, 8)

    payload = source_terms(
        (tiles, halves), per, spectra, wind, dia_index.reshape(16, count_bins),
        dia_weight.reshape(16, count_bins), nl_coef.reshape(1, count_bins),
    )
    got = lax.all_to_all(payload, ("tile", "bin"), split_axis=0, concat_axis=0, tiled=True)

    cosine, sine, speed = bin_tables(count_bins)
    weights = np.concatenate([stencil(speed * cosine), stencil(speed * sine)])
    table = np.zeros((halves, tiles, padded, LANES), np.float32)
    for side in range(halves):
        for tile in range(tiles):
            valid = max(0, min(per, half_bins - tile * per))
            begin = side * half_bins + tile * per
            table[side, tile, :valid, :10] = weights[:, begin:begin + valid].T
    taps = lax.dynamic_slice(
        jnp.asarray(table),
        (lax.axis_index("bin"), lax.axis_index("tile"), 0, 0),
        (1, 1, padded, LANES),
    ).reshape(padded, LANES)

    ones = mask.astype(jnp.bfloat16)
    upto = jnp.dot(ones, jnp.asarray(np.triu(np.ones((latitudes, latitudes))), jnp.bfloat16),
                   preferred_element_type=jnp.float32)
    before = jnp.dot(jnp.asarray(np.tril(np.ones((columns, columns)), -1), jnp.bfloat16), ones,
                     preferred_element_type=jnp.float32).sum(axis=1).astype(jnp.int32)
    total = payload.shape[0] * spectra.shape[1]
    base = jnp.minimum(before // LANES * LANES, total - LANES)
    rel = jnp.where(mask == 1, upto.astype(jnp.int32) - 1 + (before - base)[:, None], -1)

    moved = propagate(per, columns_tile, base, got, rel, taps)
    result = lax.all_to_all(
        moved.reshape(tiles, per, columns_tile, latitudes), "tile", split_axis=0, concat_axis=0, tiled=True
    ).reshape(tiles * per, columns_tile, latitudes)
    return result[:half_bins]


def solution(mesh):
    in_specs = (
        P(None, ("band", "tile", "bin")),
        P(None, ("band", "tile", "bin")),
        P(None, "band"),
        P(),
        P(),
        P(),
    )
    out_specs = P("bin", "tile", "band")
    return jax.shard_map(shards, mesh=mesh, in_specs=in_specs, out_specs=out_specs, check_vma=False)
```

```python
import functools
import math

import jax
import jax.numpy as jnp
import numpy as np
from jax import lax
from jax.experimental import pallas as pl
from jax.experimental.pallas import tpu as pltpu
from jax.sharding import PartitionSpec as P

NTH = 36
STEPS = 2
LANES = 128
ROWS = 256

LAMBDA = 0.25
COEF_THREE = (1.0 + LAMBDA) ** (-4)
COEF_FOUR = (1.0 - LAMBDA) ** (-4)
COEF_BOTH = (1.0 - LAMBDA * LAMBDA) ** (-4)
CFL_LIMIT = 0.8
WIND_RATE = 0.2


def round_up(value, step):
    return -(-value // step) * step


def bin_tables(count_bins):
    bin_range = np.arange(count_bins)
    theta = 2.0 * math.pi * (bin_range % NTH) / NTH
    group_speed = CFL_LIMIT * 1.1 ** (-(bin_range // NTH).astype(np.float64))
    return np.cos(theta), np.sin(theta), group_speed


def stencil(courant):
    bend = (1.0 - courant * courant) / 6.0
    up = courant >= 0.0
    zero = np.zeros_like(courant)
    left = courant * np.where(up, -bend, zero)
    here = courant * (0.5 + 0.5 * courant + np.where(up, 2.0 * bend, -bend))
    right = courant * (0.5 - 0.5 * courant + np.where(up, -bend, 2.0 * bend))
    far = courant * np.where(up, zero, -bend)
    return np.stack([left, here - left, 1.0 + right - here, far - right, -far])


def source_kernel(owners, per, spectra, wind, index, weight, nl_coef, tables, out,
                  index_pad, weight_pad, nl_pad, flat_t, low_t, wind_t, matrix, inter, total):
    count_bins, points = spectra.shape
    padded = flat_t.shape[1]
    chunks = padded // LANES
    whole = count_bins // LANES
    rest = count_bins - whole * LANES
    index_pad[...] = jnp.full(index_pad.shape, -1, jnp.int32)
    index_pad[:, :count_bins] = index[...]
    weight_pad[...] = jnp.zeros(weight_pad.shape, jnp.float32)
    weight_pad[:, :count_bins] = weight[...].astype(jnp.float32)
    nl_pad[...] = jnp.zeros(nl_pad.shape, jnp.float32)
    nl_pad[:, :count_bins] = nl_coef[...]
    for half in range(points // LANES):
        span = slice(half * LANES, (half + 1) * LANES)
        for block in range(chunks):
            if block < whole:
                values = spectra[block * LANES:(block + 1) * LANES, span]
            else:
                values = jnp.concatenate(
                    [spectra[whole * LANES:, span], jnp.zeros((LANES - rest, LANES), jnp.float32)], axis=0
                )
            turned = values.T
            flat_t[span, block * LANES:(block + 1) * LANES] = turned
            low_t[span, block * LANES:(block + 1) * LANES] = turned.astype(jnp.bfloat16)
        drive = jnp.concatenate([wind[:, span], jnp.zeros((LANES - 2, LANES), jnp.float32)], axis=0)
        wind_t[span, :] = drive.T

    def chunk_step(chunk, carry):
        lane = pl.multiple_of(chunk * LANES, LANES)
        lanes = pl.ds(lane, LANES)
        wide = pl.multiple_of(chunk * 4 * LANES, 4 * LANES)
        rows_index = [index_pad[pl.ds(r, 1), lanes] for r in range(16)]
        rows_weight = [weight_pad[pl.ds(r, 1), lanes] for r in range(16)]
        members = [jnp.zeros((points, 2 * LANES), jnp.float32) for _ in range(2)]
        for start in range(0, padded, ROWS):
            size = min(ROWS, padded - start)
            place = lax.broadcasted_iota(jnp.int32, (size, LANES), 0) + start
            for mirror in range(2):
                for member in range(2):
                    block = jnp.zeros((size, LANES), jnp.float32)
                    for corner in range(4):
                        r = mirror * 8 + member * 4 + corner
                        block = jnp.where(place == rows_index[r], rows_weight[r], block)
                    matrix[start:start + size, pl.ds(wide + (mirror * 2 + member) * LANES, LANES)] = (
                        block.astype(jnp.bfloat16)
                    )
                members[mirror] = members[mirror] + jnp.dot(
                    low_t[:, start:start + size],
                    matrix[start:start + size, pl.ds(wide + mirror * 2 * LANES, 2 * LANES)],
                    preferred_element_type=jnp.float32,
                )
        values = flat_t[:, lanes]
        coef = nl_pad[:, lanes]
        drive = jnp.maximum(
            wind_t[:, 0:1] * tables[0:1, lanes] + wind_t[:, 1:2] * tables[1:2, lanes], 0.0
        )
        base = values + WIND_RATE * drive * values
        for mirror in range(2):
            third = members[mirror][:, :LANES]
            fourth = members[mirror][:, LANES:]
            interaction = coef * (
                values * values * (COEF_THREE * third + COEF_FOUR * fourth)
                - 2.0 * COEF_BOTH * values * third * fourth
            )
            base = base - 2.0 * interaction
            for half in range(points // LANES):
                span = slice(half * LANES, (half + 1) * LANES)
                turned = interaction[span].T.astype(jnp.bfloat16)
                for member in range(2):
                    inter[pl.ds(wide + (mirror * 2 + member) * LANES, LANES), span] = turned
        for half in range(points // LANES):
            span = slice(half * LANES, (half + 1) * LANES)
            total[lanes, span] = base[span].T
        return carry

    lax.fori_loop(0, chunks, chunk_step, 0)
    for start in range(0, padded, ROWS):
        size = min(ROWS, padded - start)
        total[start:start + size, :] += jnp.dot(
            matrix[start:start + size, :], inter[...], preferred_element_type=jnp.float32
        )
    tiles, halves = owners
    half_bins = count_bins // halves
    for tile in range(tiles):
        for side in range(halves):
            first = side * half_bins + tile * per
            valid = min(per, half_bins - tile * per)
            if valid <= 0:
                continue
            for half in range(points // LANES):
                out[tile * halves + side, half * per:half * per + valid, :] = total[
                    first:first + valid, half * LANES:(half + 1) * LANES
                ]


def source_terms(owners, per, spectra, wind, index, weight, nl_coef):
    count_bins, points = spectra.shape
    padded = round_up(count_bins, LANES)
    cosine, sine, _ = bin_tables(count_bins)
    tables = np.zeros((2, padded), np.float32)
    tables[0, :count_bins] = cosine
    tables[1, :count_bins] = sine
    group = owners[0] * owners[1]
    rows = per * (points // LANES)
    return pl.pallas_call(
        functools.partial(source_kernel, owners, per),
        out_shape=jax.ShapeDtypeStruct((group, rows, LANES), jnp.float32),
        scratch_shapes=[
            pltpu.VMEM((16, padded), jnp.int32),
            pltpu.VMEM((16, padded), jnp.float32),
            pltpu.VMEM((1, padded), jnp.float32),
            pltpu.VMEM((points, padded), jnp.float32),
            pltpu.VMEM((points, padded), jnp.bfloat16),
            pltpu.VMEM((points, LANES), jnp.float32),
            pltpu.VMEM((padded, 4 * padded), jnp.bfloat16),
            pltpu.VMEM((4 * padded, points), jnp.bfloat16),
            pltpu.VMEM((padded, points), jnp.float32),
        ],
        compiler_params=pltpu.CompilerParams(vmem_limit_bytes=52 * 1024 * 1024),
        name="source_terms",
    )(spectra, wind, index, weight, nl_coef, jnp.asarray(tables))


def propagate_kernel(per, columns_tile, halo, base, got, rel, taps, out, ranked, lined, middle, pick, sea):
    group = got.shape[0]
    columns = rel.shape[0]
    halves = got.shape[1] // per
    fill = jnp.zeros((LANES - per, LANES), jnp.float32)

    def order(owner, carry):
        for half in range(halves):
            values = jnp.concatenate([got[owner, half * per:(half + 1) * per, :], fill], axis=0)
            ranked[pl.ds(half * LANES * group + owner, LANES, stride=group), :] = values.T
        return carry

    lax.fori_loop(0, group, order, 0, unroll=4)

    rank_tiles = ranked.shape[0] // LANES
    padded = lined.shape[0]

    def line_up(tile, carry):
        start = pl.multiple_of(tile * LANES, LANES)
        lined[:, pl.ds(start, LANES)] = ranked[pl.ds(start, LANES), :].T[:padded]
        return carry

    lax.fori_loop(0, rank_tiles, line_up, 0, unroll=4)
    lined[:, rank_tiles * LANES:] = jnp.zeros((padded, LANES), jnp.float32)

    for column in range(columns):
        row = jnp.broadcast_to(rel[column:column + 1, :], (8, LANES))
        pick[column] = row
        sea[column] = jnp.where(row >= 0, 1.0, 0.0)

    lane = lax.broadcasted_iota(jnp.int32, (8, LANES), 1)

    def bins_step(first_bin, valid):
        span = pl.ds(first_bin, 8)
        x_taps = [jnp.broadcast_to(taps[span, k:k + 1], (8, LANES)) for k in range(5)]
        y_taps = []
        for k in range(5):
            tap = jnp.broadcast_to(taps[span, 5 + k:6 + k], (8, LANES))
            inside = (lane + (k - 2) >= 0) & (lane + (k - 2) < LANES)
            y_taps.append(jnp.where(inside, tap, 0.0))

        def expanded(column):
            start = pl.multiple_of(base[column], LANES)
            chosen = pick[column]
            within = chosen & (LANES - 1)
            low = jnp.take_along_axis(lined[span, pl.ds(start, LANES)], within, axis=1)
            high = jnp.take_along_axis(lined[span, pl.ds(start + LANES, LANES)], within, axis=1)
            return jnp.where(chosen >= LANES, high, low) * sea[column]

        def sweep(values, column):
            value = x_taps[2] * values[2]
            for k in (0, 1, 3, 4):
                value = value + x_taps[k] * values[k]
            value = value * sea[column]
            moved = y_taps[2] * value
            for k in (0, 1, 3, 4):
                moved = moved + y_taps[k] * pltpu.roll(value, (2 - k) % LANES, 1)
            return moved * sea[column]

        reach = halo // STEPS
        first = {}
        for column in range(columns):
            first[column] = expanded(column)
        for column in range(reach, columns - reach):
            middle[column] = sweep([first[(column + k) % columns] for k in range(-2, 3)], column)
        for column in range(halo, columns - halo):
            result = sweep([middle[(column + k) % columns] for k in range(-2, 3)], column)
            owner, place = divmod(column - halo, columns_tile)
            start = (owner * per + first_bin) * columns_tile + place
            if valid == 8:
                out[pl.ds(start, 8, stride=columns_tile), :] = result
            else:
                for row in range(valid):
                    out[pl.ds(start + row * columns_tile, 1), :] = result[row:row + 1]

    def full_step(tile, carry):
        bins_step(pl.multiple_of(tile * 8, 8), 8)
        return carry

    lax.fori_loop(0, per // 8, full_step, 0)
    if per % 8:
        bins_step(per // 8 * 8, per % 8)


def propagate(per, columns_tile, halo, base, got, rel, taps):
    group, rows, _ = got.shape
    columns = rel.shape[0]
    points = rows // per * LANES
    padded = round_up(per, 8)
    smem = pl.BlockSpec(memory_space=pltpu.SMEM)
    vmem = pl.BlockSpec(memory_space=pltpu.VMEM)
    return pl.pallas_call(
        functools.partial(propagate_kernel, per, columns_tile, halo),
        out_shape=jax.ShapeDtypeStruct(((columns - 2 * halo) * per, LANES), jnp.float32),
        in_specs=[smem, vmem, vmem, vmem],
        out_specs=vmem,
        scratch_shapes=[
            pltpu.VMEM((group * points, LANES), jnp.float32),
            pltpu.VMEM((padded, group * points + LANES), jnp.float32),
            pltpu.VMEM((columns, 8, LANES), jnp.float32),
            pltpu.VMEM((columns, 8, LANES), jnp.int32),
            pltpu.VMEM((columns, 8, LANES), jnp.float32),
        ],
        compiler_params=pltpu.CompilerParams(vmem_limit_bytes=52 * 1024 * 1024),
        name="propagate",
    )(base, got, rel, taps)


def shards(spectra, wind, mask, dia_index, dia_weight, nl_coef):
    count_bins = spectra.shape[0]
    tiles = lax.axis_size("tile")
    halves = lax.axis_size("bin")
    columns, latitudes = mask.shape
    columns_tile = columns // tiles
    half_bins = count_bins // halves
    per = -(-half_bins // tiles)
    padded = round_up(per, 8)

    payload = source_terms(
        (tiles, halves), per, spectra, wind, dia_index.reshape(16, count_bins),
        dia_weight.reshape(16, count_bins), nl_coef.reshape(1, count_bins),
    )
    got = lax.all_to_all(payload, ("tile", "bin"), split_axis=0, concat_axis=0, tiled=True)

    cosine, sine, speed = bin_tables(count_bins)
    weights = np.concatenate([stencil(speed * cosine), stencil(speed * sine)])
    table = np.zeros((halves, tiles, padded, LANES), np.float32)
    for side in range(halves):
        for tile in range(tiles):
            valid = max(0, min(per, half_bins - tile * per))
            begin = side * half_bins + tile * per
            table[side, tile, :valid, :10] = weights[:, begin:begin + valid].T
    taps = lax.dynamic_slice(
        jnp.asarray(table),
        (lax.axis_index("bin"), lax.axis_index("tile"), 0, 0),
        (1, 1, padded, LANES),
    ).reshape(padded, LANES)

    ones = mask.astype(jnp.bfloat16)
    upto = jnp.dot(ones, jnp.asarray(np.triu(np.ones((latitudes, latitudes))), jnp.bfloat16),
                   preferred_element_type=jnp.float32)
    before = jnp.dot(jnp.asarray(np.tril(np.ones((columns, columns)), -1), jnp.bfloat16), ones,
                     preferred_element_type=jnp.float32).sum(axis=1).astype(jnp.int32)
    total = payload.shape[0] * spectra.shape[1]
    base = jnp.minimum(before // LANES * LANES, total - LANES)
    rel = jnp.where(mask == 1, upto.astype(jnp.int32) - 1 + (before - base)[:, None], -1)

    moved = propagate(per, columns_tile, 0, base, got, rel, taps)
    result = lax.all_to_all(
        moved.reshape(tiles, per, columns_tile, latitudes), "tile", split_axis=0, concat_axis=0, tiled=True
    ).reshape(tiles * per, columns_tile, latitudes)
    return result[:half_bins]


def solution(mesh):
    in_specs = (
        P(None, ("band", "tile", "bin")),
        P(None, ("band", "tile", "bin")),
        P(None, "band"),
        P(),
        P(),
        P(),
    )
    out_specs = P("bin", "tile", "band")
    return jax.shard_map(shards, mesh=mesh, in_specs=in_specs, out_specs=out_specs, check_vma=False)
```

```python
import functools
import math

import jax
import jax.numpy as jnp
import numpy as np
from jax import lax
from jax.experimental import pallas as pl
from jax.experimental.pallas import tpu as pltpu
from jax.sharding import PartitionSpec as P

NTH = 36
STEPS = 2
LANES = 128
ROWS = 256
RING = 40

LAMBDA = 0.25
COEF_THREE = (1.0 + LAMBDA) ** (-4)
COEF_FOUR = (1.0 - LAMBDA) ** (-4)
COEF_BOTH = (1.0 - LAMBDA * LAMBDA) ** (-4)
CFL_LIMIT = 0.8
WIND_RATE = 0.2


def round_up(value, step):
    return -(-value // step) * step


def bin_tables(count_bins):
    bin_range = np.arange(count_bins)
    theta = 2.0 * math.pi * (bin_range % NTH) / NTH
    group_speed = CFL_LIMIT * 1.1 ** (-(bin_range // NTH).astype(np.float64))
    return np.cos(theta), np.sin(theta), group_speed


def stencil(courant):
    bend = (1.0 - courant * courant) / 6.0
    up = courant >= 0.0
    zero = np.zeros_like(courant)
    left = courant * np.where(up, -bend, zero)
    here = courant * (0.5 + 0.5 * courant + np.where(up, 2.0 * bend, -bend))
    right = courant * (0.5 - 0.5 * courant + np.where(up, -bend, 2.0 * bend))
    far = courant * np.where(up, zero, -bend)
    return np.stack([left, here - left, 1.0 + right - here, far - right, -far])


def source_kernel(owners, per, spectra, wind, index, weight, nl_coef, tables, out,
                  code, weight_pad, nl_pad, spaced, flat_t, low_t, wind_t, matrix, inter, total):
    count_bins, points = spectra.shape
    padded = flat_t.shape[1]
    chunks = padded // LANES
    rings = count_bins // NTH
    depth = spaced.shape[0]
    whole = count_bins // LANES
    rest = count_bins - whole * LANES

    code[...] = jnp.zeros(code.shape, jnp.int32)
    weight_pad[...] = jnp.zeros(weight_pad.shape, jnp.float32)
    nl_pad[...] = jnp.zeros(nl_pad.shape, jnp.float32)
    nl_pad[:, :count_bins] = nl_coef[...].reshape(1, count_bins)
    for mirror in range(2):
        for member in range(2):
            row = (mirror * 2 + member) * 4
            bins = index[mirror, member]
            ring = ((bins.astype(jnp.float32) + 0.5) * (1.0 / NTH)).astype(jnp.int32)
            lowest = jnp.minimum(jnp.minimum(ring[0:1], ring[1:2]), jnp.minimum(ring[2:3], ring[3:4]))
            direction = bins - ring * NTH
            code[row:row + 4, :count_bins] = jnp.where(ring == lowest, direction, direction + RING)
            code[16 + mirror * 2 + member:17 + mirror * 2 + member, :count_bins] = lowest
            weight_pad[row:row + 4, :count_bins] = weight[mirror, member].astype(jnp.float32)

    gap = jnp.zeros((RING - NTH, points), jnp.float32)
    for ring in range(rings):
        spaced[ring * RING:ring * RING + NTH, :] = spectra[ring * NTH:(ring + 1) * NTH, :]
        spaced[ring * RING + NTH:(ring + 1) * RING, :] = gap
    spaced[rings * RING:, :] = jnp.zeros((depth - rings * RING, points), jnp.float32)
    for half in range(points // LANES):
        span = slice(half * LANES, (half + 1) * LANES)
        for block in range(depth // LANES):
            lanes = slice(block * LANES, (block + 1) * LANES)
            low_t[span, lanes] = spaced[lanes, span].T.astype(jnp.bfloat16)
        for block in range(chunks):
            lanes = slice(block * LANES, (block + 1) * LANES)
            if block < whole:
                values = spectra[lanes, span]
            else:
                values = jnp.concatenate(
                    [spectra[whole * LANES:, span], jnp.zeros((LANES - rest, LANES), jnp.float32)], axis=0
                )
            flat_t[span, lanes] = values.T
        drive = jnp.concatenate([wind[:, span], jnp.zeros((LANES - 2, LANES), jnp.float32)], axis=0)
        wind_t[span, :] = drive.T

    used = rings * RING
    matrix[used:, :] = jnp.zeros((depth - used, matrix.shape[1]), jnp.bfloat16)

    def chunk_step(chunk, carry):
        lane = pl.multiple_of(chunk * LANES, LANES)
        lanes = pl.ds(lane, LANES)
        wide = pl.multiple_of(chunk * 4 * LANES, 4 * LANES)
        place = lax.broadcasted_iota(jnp.int32, (RING, LANES), 0)
        nothing = jnp.zeros((RING, LANES), jnp.float32)
        patterns = []
        for pair in range(4):
            low = nothing
            high = nothing
            for corner in range(4):
                r = pair * 4 + corner
                where = code[pl.ds(r, 1), lanes]
                amount = jnp.broadcast_to(weight_pad[pl.ds(r, 1), lanes], (RING, LANES))
                low = jnp.where(place == where, amount, low)
                high = jnp.where(place + RING == where, amount, high)
            lowest = jnp.broadcast_to(code[pl.ds(16 + pair, 1), lanes], (8, LANES))
            patterns.append((low, high, lowest))
        members = [jnp.zeros((points, 2 * LANES), jnp.float32) for _ in range(2)]
        done = 0
        for ring in range(0, rings, 2):
            for pair in range(4):
                low, high, lowest = patterns[pair]
                parts = []
                for offset in range(2):
                    first = lowest == ring + offset
                    second = lowest == ring + offset - 1
                    for sub in range(0, RING, 8):
                        parts.append(
                            jnp.where(first, low[sub:sub + 8], jnp.where(second, high[sub:sub + 8], 0.0))
                        )
                matrix[ring * RING:(ring + 2) * RING, pl.ds(wide + pair * LANES, LANES)] = jnp.concatenate(
                    parts, axis=0
                ).astype(jnp.bfloat16)
            ready = (ring + 2) * RING
            while done < depth and (ready >= done + ROWS or ready == used):
                size = min(ROWS, depth - done)
                for mirror in range(2):
                    members[mirror] = members[mirror] + jnp.dot(
                        low_t[:, done:done + size],
                        matrix[done:done + size, pl.ds(wide + mirror * 2 * LANES, 2 * LANES)],
                        preferred_element_type=jnp.float32,
                    )
                done += size
        values = flat_t[:, lanes]
        coef = nl_pad[:, lanes]
        drive = jnp.maximum(
            wind_t[:, 0:1] * tables[0:1, lanes] + wind_t[:, 1:2] * tables[1:2, lanes], 0.0
        )
        base = values + WIND_RATE * drive * values
        for mirror in range(2):
            third = members[mirror][:, :LANES]
            fourth = members[mirror][:, LANES:]
            interaction = coef * (
                values * values * (COEF_THREE * third + COEF_FOUR * fourth)
                - 2.0 * COEF_BOTH * values * third * fourth
            )
            base = base - 2.0 * interaction
            for half in range(points // LANES):
                span = slice(half * LANES, (half + 1) * LANES)
                turned = interaction[span].T.astype(jnp.bfloat16)
                for member in range(2):
                    inter[pl.ds(wide + (mirror * 2 + member) * LANES, LANES), span] = turned
        for half in range(points // LANES):
            span = slice(half * LANES, (half + 1) * LANES)
            total[lanes, span] = base[span].T
        return carry

    lax.fori_loop(0, chunks, chunk_step, 0)
    for start in range(0, depth, ROWS):
        size = min(ROWS, depth - start)
        spaced[start:start + size, :] = jnp.dot(
            matrix[start:start + size, :], inter[...], preferred_element_type=jnp.float32
        )
    for ring in range(rings):
        total[ring * NTH:(ring + 1) * NTH, :] += spaced[ring * RING:ring * RING + NTH, :]
    tiles, halves = owners
    half_bins = count_bins // halves
    for tile in range(tiles):
        for side in range(halves):
            first = side * half_bins + tile * per
            valid = min(per, half_bins - tile * per)
            if valid <= 0:
                continue
            for half in range(points // LANES):
                out[tile * halves + side, half * per:half * per + valid, :] = total[
                    first:first + valid, half * LANES:(half + 1) * LANES
                ]


def source_terms(owners, per, spectra, wind, index, weight, nl_coef):
    count_bins, points = spectra.shape
    padded = round_up(count_bins, LANES)
    depth = round_up(count_bins // NTH * RING, LANES)
    cosine, sine, _ = bin_tables(count_bins)
    tables = np.zeros((2, padded), np.float32)
    tables[0, :count_bins] = cosine
    tables[1, :count_bins] = sine
    group = owners[0] * owners[1]
    rows = per * (points // LANES)
    return pl.pallas_call(
        functools.partial(source_kernel, owners, per),
        out_shape=jax.ShapeDtypeStruct((group, rows, LANES), jnp.float32),
        scratch_shapes=[
            pltpu.VMEM((24, padded), jnp.int32),
            pltpu.VMEM((16, padded), jnp.float32),
            pltpu.VMEM((1, padded), jnp.float32),
            pltpu.VMEM((depth, points), jnp.float32),
            pltpu.VMEM((points, padded), jnp.float32),
            pltpu.VMEM((points, depth), jnp.bfloat16),
            pltpu.VMEM((points, LANES), jnp.float32),
            pltpu.VMEM((depth, 4 * padded), jnp.bfloat16),
            pltpu.VMEM((4 * padded, points), jnp.bfloat16),
            pltpu.VMEM((padded, points), jnp.float32),
        ],
        compiler_params=pltpu.CompilerParams(vmem_limit_bytes=52 * 1024 * 1024),
        name="source_terms",
    )(spectra, wind, index, weight, nl_coef, jnp.asarray(tables))


def propagate_kernel(per, columns_tile, halo, base, got, rel, taps, out, ranked, lined, middle, pick, sea):
    group = got.shape[0]
    columns = rel.shape[0]
    halves = got.shape[1] // per
    fill = jnp.zeros((LANES - per, LANES), jnp.float32)

    def order(owner, carry):
        for half in range(halves):
            values = jnp.concatenate([got[owner, half * per:(half + 1) * per, :], fill], axis=0)
            ranked[pl.ds(half * LANES * group + owner, LANES, stride=group), :] = values.T
        return carry

    lax.fori_loop(0, group, order, 0, unroll=4)

    rank_tiles = ranked.shape[0] // LANES
    padded = lined.shape[0]

    def line_up(tile, carry):
        start = pl.multiple_of(tile * LANES, LANES)
        lined[:, pl.ds(start, LANES)] = ranked[pl.ds(start, LANES), :].T[:padded]
        return carry

    lax.fori_loop(0, rank_tiles, line_up, 0, unroll=4)
    lined[:, rank_tiles * LANES:] = jnp.zeros((padded, LANES), jnp.float32)

    for column in range(columns):
        row = jnp.broadcast_to(rel[column:column + 1, :], (8, LANES))
        pick[column] = row
        sea[column] = jnp.where(row >= 0, 1.0, 0.0)

    lane = lax.broadcasted_iota(jnp.int32, (8, LANES), 1)

    def bins_step(first_bin, valid):
        span = pl.ds(first_bin, 8)
        x_taps = [jnp.broadcast_to(taps[span, k:k + 1], (8, LANES)) for k in range(5)]
        y_taps = []
        for k in range(5):
            tap = jnp.broadcast_to(taps[span, 5 + k:6 + k], (8, LANES))
            inside = (lane + (k - 2) >= 0) & (lane + (k - 2) < LANES)
            y_taps.append(jnp.where(inside, tap, 0.0))

        def expanded(column):
            start = pl.multiple_of(base[column], LANES)
            chosen = pick[column]
            within = chosen & (LANES - 1)
            low = jnp.take_along_axis(lined[span, pl.ds(start, LANES)], within, axis=1)
            high = jnp.take_along_axis(lined[span, pl.ds(start + LANES, LANES)], within, axis=1)
            return jnp.where(chosen >= LANES, high, low) * sea[column]

        def sweep(values, column):
            value = x_taps[2] * values[2]
            for k in (0, 1, 3, 4):
                value = value + x_taps[k] * values[k]
            value = value * sea[column]
            moved = y_taps[2] * value
            for k in (0, 1, 3, 4):
                moved = moved + y_taps[k] * pltpu.roll(value, (2 - k) % LANES, 1)
            return moved * sea[column]

        reach = halo // STEPS
        first = {}
        for column in range(columns):
            first[column] = expanded(column)
        for column in range(reach, columns - reach):
            middle[column] = sweep([first[(column + k) % columns] for k in range(-2, 3)], column)
        for column in range(halo, columns - halo):
            result = sweep([middle[(column + k) % columns] for k in range(-2, 3)], column)
            owner, place = divmod(column - halo, columns_tile)
            start = (owner * per + first_bin) * columns_tile + place
            if valid == 8:
                out[pl.ds(start, 8, stride=columns_tile), :] = result
            else:
                for row in range(valid):
                    out[pl.ds(start + row * columns_tile, 1), :] = result[row:row + 1]

    def full_step(tile, carry):
        bins_step(pl.multiple_of(tile * 8, 8), 8)
        return carry

    lax.fori_loop(0, per // 8, full_step, 0)
    if per % 8:
        bins_step(per // 8 * 8, per % 8)


def propagate(per, columns_tile, halo, base, got, rel, taps):
    group, rows, _ = got.shape
    columns = rel.shape[0]
    points = rows // per * LANES
    padded = round_up(per, 8)
    smem = pl.BlockSpec(memory_space=pltpu.SMEM)
    vmem = pl.BlockSpec(memory_space=pltpu.VMEM)
    return pl.pallas_call(
        functools.partial(propagate_kernel, per, columns_tile, halo),
        out_shape=jax.ShapeDtypeStruct(((columns - 2 * halo) * per, LANES), jnp.float32),
        in_specs=[smem, vmem, vmem, vmem],
        out_specs=vmem,
        scratch_shapes=[
            pltpu.VMEM((group * points, LANES), jnp.float32),
            pltpu.VMEM((padded, group * points + LANES), jnp.float32),
            pltpu.VMEM((columns, 8, LANES), jnp.float32),
            pltpu.VMEM((columns, 8, LANES), jnp.int32),
            pltpu.VMEM((columns, 8, LANES), jnp.float32),
        ],
        compiler_params=pltpu.CompilerParams(vmem_limit_bytes=52 * 1024 * 1024),
        name="propagate",
    )(base, got, rel, taps)


def shards(spectra, wind, mask, dia_index, dia_weight, nl_coef):
    count_bins = spectra.shape[0]
    tiles = lax.axis_size("tile")
    halves = lax.axis_size("bin")
    columns, latitudes = mask.shape
    columns_tile = columns // tiles
    half_bins = count_bins // halves
    per = -(-half_bins // tiles)
    padded = round_up(per, 8)

    payload = source_terms(
        (tiles, halves), per, spectra, wind, dia_index, dia_weight, nl_coef
    )
    got = lax.all_to_all(payload, ("tile", "bin"), split_axis=0, concat_axis=0, tiled=True)

    cosine, sine, speed = bin_tables(count_bins)
    weights = np.concatenate([stencil(speed * cosine), stencil(speed * sine)])
    table = np.zeros((halves, tiles, padded, LANES), np.float32)
    for side in range(halves):
        for tile in range(tiles):
            valid = max(0, min(per, half_bins - tile * per))
            begin = side * half_bins + tile * per
            table[side, tile, :valid, :10] = weights[:, begin:begin + valid].T
    taps = lax.dynamic_slice(
        jnp.asarray(table),
        (lax.axis_index("bin"), lax.axis_index("tile"), 0, 0),
        (1, 1, padded, LANES),
    ).reshape(padded, LANES)

    ones = mask.astype(jnp.bfloat16)
    upto = jnp.dot(ones, jnp.asarray(np.triu(np.ones((latitudes, latitudes))), jnp.bfloat16),
                   preferred_element_type=jnp.float32)
    before = jnp.dot(jnp.asarray(np.tril(np.ones((columns, columns)), -1), jnp.bfloat16), ones,
                     preferred_element_type=jnp.float32).sum(axis=1).astype(jnp.int32)
    total = payload.shape[0] * spectra.shape[1]
    base = jnp.minimum(before // LANES * LANES, total - LANES)
    rel = jnp.where(mask == 1, upto.astype(jnp.int32) - 1 + (before - base)[:, None], -1)

    moved = propagate(per, columns_tile, 0, base, got, rel, taps)
    result = lax.all_to_all(
        moved.reshape(tiles, per, columns_tile, latitudes), "tile", split_axis=0, concat_axis=0, tiled=True
    ).reshape(tiles * per, columns_tile, latitudes)
    return result[:half_bins]


def solution(mesh):
    in_specs = (
        P(None, ("band", "tile", "bin")),
        P(None, ("band", "tile", "bin")),
        P(None, "band"),
        P(),
        P(),
        P(),
    )
    out_specs = P("bin", "tile", "band")
    return jax.shard_map(shards, mesh=mesh, in_specs=in_specs, out_specs=out_specs, check_vma=False)
```

```python
import dataclasses
import functools
import math

import jax
import jax.numpy as jnp
import numpy as np
from jax import lax
from jax.experimental import pallas as pl
from jax.experimental.pallas import tpu as pltpu
from jax.sharding import PartitionSpec as P

NTH = 36
STEPS = 2
LANES = 128
ROWS = 256
RING = 40
COMMON = 192
SIZES = (160, 176, 192, 208, 224)

LAMBDA = 0.25
COEF_THREE = (1.0 + LAMBDA) ** (-4)
COEF_FOUR = (1.0 - LAMBDA) ** (-4)
COEF_BOTH = (1.0 - LAMBDA * LAMBDA) ** (-4)
CFL_LIMIT = 0.8
WIND_RATE = 0.2


def round_up(value, step):
    return -(-value // step) * step


def bin_tables(count_bins):
    bin_range = np.arange(count_bins)
    theta = 2.0 * math.pi * (bin_range % NTH) / NTH
    group_speed = CFL_LIMIT * 1.1 ** (-(bin_range // NTH).astype(np.float64))
    return np.cos(theta), np.sin(theta), group_speed


def stencil(courant):
    bend = (1.0 - courant * courant) / 6.0
    up = courant >= 0.0
    zero = np.zeros_like(courant)
    left = courant * np.where(up, -bend, zero)
    here = courant * (0.5 + 0.5 * courant + np.where(up, 2.0 * bend, -bend))
    right = courant * (0.5 - 0.5 * courant + np.where(up, -bend, 2.0 * bend))
    far = courant * np.where(up, zero, -bend)
    return np.stack([left, here - left, 1.0 + right - here, far - right, -far])


def source_kernel(plan, first_point, spectra, wind, index, weight, nl_coef, tables, out,
                  code, weight_pad, nl_pad, spaced, flat_t, low_t, wind_t, matrix, inter, total, twice):
    count_bins, points = spectra.shape
    padded = flat_t.shape[1]
    chunks = padded // LANES
    rings = count_bins // NTH
    depth = spaced.shape[0]
    whole = count_bins // LANES
    rest = count_bins - whole * LANES

    code[...] = jnp.zeros(code.shape, jnp.int32)
    weight_pad[...] = jnp.zeros(weight_pad.shape, jnp.float32)
    nl_pad[...] = jnp.zeros(nl_pad.shape, jnp.float32)
    nl_pad[:, :count_bins] = nl_coef[...].reshape(1, count_bins)
    for mirror in range(2):
        for member in range(2):
            row = (mirror * 2 + member) * 4
            bins = index[mirror, member]
            ring = ((bins.astype(jnp.float32) + 0.5) * (1.0 / NTH)).astype(jnp.int32)
            lowest = jnp.minimum(jnp.minimum(ring[0:1], ring[1:2]), jnp.minimum(ring[2:3], ring[3:4]))
            direction = bins - ring * NTH
            code[row:row + 4, :count_bins] = jnp.where(ring == lowest, direction, direction + RING)
            code[16 + mirror * 2 + member:17 + mirror * 2 + member, :count_bins] = lowest
            weight_pad[row:row + 4, :count_bins] = weight[mirror, member].astype(jnp.float32)

    gap = jnp.zeros((RING - NTH, points), jnp.float32)
    for ring in range(rings):
        spaced[ring * RING:ring * RING + NTH, :] = spectra[ring * NTH:(ring + 1) * NTH, :]
        spaced[ring * RING + NTH:(ring + 1) * RING, :] = gap
    spaced[rings * RING:, :] = jnp.zeros((depth - rings * RING, points), jnp.float32)
    for half in range(points // LANES):
        span = slice(half * LANES, (half + 1) * LANES)
        for block in range(depth // LANES):
            lanes = slice(block * LANES, (block + 1) * LANES)
            low_t[span, lanes] = spaced[lanes, span].T.astype(jnp.bfloat16)
        for block in range(chunks):
            lanes = slice(block * LANES, (block + 1) * LANES)
            if block < whole:
                values = spectra[lanes, span]
            else:
                values = jnp.concatenate(
                    [spectra[whole * LANES:, span], jnp.zeros((LANES - rest, LANES), jnp.float32)], axis=0
                )
            flat_t[span, lanes] = values.T
        drive = jnp.concatenate([wind[:, span], jnp.zeros((LANES - 2, LANES), jnp.float32)], axis=0)
        wind_t[span, :] = drive.T

    used = rings * RING
    matrix[used:, :] = jnp.zeros((depth - used, matrix.shape[1]), jnp.bfloat16)

    def chunk_step(chunk, carry):
        lane = pl.multiple_of(chunk * LANES, LANES)
        lanes = pl.ds(lane, LANES)
        wide = pl.multiple_of(chunk * 4 * LANES, 4 * LANES)
        place = lax.broadcasted_iota(jnp.int32, (RING, LANES), 0)
        nothing = jnp.zeros((RING, LANES), jnp.float32)
        patterns = []
        for pair in range(4):
            low = nothing
            high = nothing
            for corner in range(4):
                r = pair * 4 + corner
                where = code[pl.ds(r, 1), lanes]
                amount = jnp.broadcast_to(weight_pad[pl.ds(r, 1), lanes], (RING, LANES))
                low = jnp.where(place == where, amount, low)
                high = jnp.where(place + RING == where, amount, high)
            lowest = jnp.broadcast_to(code[pl.ds(16 + pair, 1), lanes], (8, LANES))
            patterns.append((low, high, lowest))
        members = [jnp.zeros((points, 2 * LANES), jnp.float32) for _ in range(2)]
        done = 0
        for ring in range(0, rings, 2):
            for pair in range(4):
                low, high, lowest = patterns[pair]
                parts = []
                for offset in range(2):
                    first = lowest == ring + offset
                    second = lowest == ring + offset - 1
                    for sub in range(0, RING, 8):
                        parts.append(
                            jnp.where(first, low[sub:sub + 8], jnp.where(second, high[sub:sub + 8], 0.0))
                        )
                matrix[ring * RING:(ring + 2) * RING, pl.ds(wide + pair * LANES, LANES)] = jnp.concatenate(
                    parts, axis=0
                ).astype(jnp.bfloat16)
            ready = (ring + 2) * RING
            while done < depth and (ready >= done + ROWS or ready == used):
                size = min(ROWS, depth - done)
                for mirror in range(2):
                    members[mirror] = members[mirror] + jnp.dot(
                        low_t[:, done:done + size],
                        matrix[done:done + size, pl.ds(wide + mirror * 2 * LANES, 2 * LANES)],
                        preferred_element_type=jnp.float32,
                    )
                done += size
        values = flat_t[:, lanes]
        coef = nl_pad[:, lanes]
        drive = jnp.maximum(
            wind_t[:, 0:1] * tables[0:1, lanes] + wind_t[:, 1:2] * tables[1:2, lanes], 0.0
        )
        base = values + WIND_RATE * drive * values
        for mirror in range(2):
            third = members[mirror][:, :LANES]
            fourth = members[mirror][:, LANES:]
            interaction = coef * (
                values * values * (COEF_THREE * third + COEF_FOUR * fourth)
                - 2.0 * COEF_BOTH * values * third * fourth
            )
            base = base - 2.0 * interaction
            for half in range(points // LANES):
                span = slice(half * LANES, (half + 1) * LANES)
                turned = interaction[span].T.astype(jnp.bfloat16)
                for member in range(2):
                    inter[pl.ds(wide + (mirror * 2 + member) * LANES, LANES), span] = turned
        for half in range(points // LANES):
            span = slice(half * LANES, (half + 1) * LANES)
            total[lanes, span] = base[span].T
        return carry

    lax.fori_loop(0, chunks, chunk_step, 0)
    for start in range(0, depth, ROWS):
        size = min(ROWS, depth - start)
        spaced[start:start + size, :] = jnp.dot(
            matrix[start:start + size, :], inter[...], preferred_element_type=jnp.float32
        )
    for ring in range(rings):
        total[ring * NTH:(ring + 1) * NTH, :] += spaced[ring * RING:ring * RING + NTH, :]
    pack_payload(plan, first_point, total, out, twice)


def pack_payload(plan, first_point, total, out, twice):
    points = total.shape[1]
    main, rest, fold = plan.main, plan.rest, plan.fold
    lane = lax.broadcasted_iota(jnp.int32, (1, LANES), 1)
    for side in range(plan.halves):
        for member in range(plan.members):
            first = side * plan.half_bins + member * plan.per
            valid = min(main, plan.half_bins - member * plan.per)
            slot = (side * plan.members + member) % 2
            for half in range(points // LANES):
                values = total[first:first + valid, half * LANES:(half + 1) * LANES]
                if valid < LANES:
                    values = jnp.concatenate([values, jnp.zeros((LANES - valid, LANES), jnp.float32)], axis=0)
                turned = values.T
                twice[slot, half * LANES:(half + 1) * LANES, :] = turned
                twice[slot, points + half * LANES:points + (half + 1) * LANES, :] = turned
            for part in range(plan.parts):
                owner = (part * plan.members + member) * plan.halves + side
                begin = first_point[part]
                out[owner, rest + fold:rest + fold + COMMON, :] = twice[slot, pl.ds(begin, COMMON), :]
                out[owner, rest + 2 * fold + COMMON:rest + 2 * fold + points, :] = twice[
                    slot, pl.ds(begin + COMMON, points - COMMON), :
                ]
                if not rest:
                    continue
                shift = lax.rem(begin, LANES)
                swapped = begin >= LANES
                near = pltpu.roll(total[first + main:first + main + rest, :LANES], lax.rem(LANES - shift, LANES), 1)
                away = pltpu.roll(total[first + main:first + main + rest, LANES:], lax.rem(LANES - shift, LANES), 1)
                keep = (lane < LANES - shift) != swapped
                lead = jnp.where(keep, near, away)
                tail = jnp.where(keep, away, near)
                moved = pltpu.roll(tail, LANES // 2, 1)
                out[owner, :rest, :] = lead
                out[owner, rest:rest + fold, :] = jnp.where(lane < LANES // 2, tail[:fold], moved[rest - fold:])
                out[owner, rest + fold + COMMON:rest + 2 * fold + COMMON, :] = jnp.where(
                    lane < LANES // 2, moved[:fold], tail[rest - fold:]
                )


def source_terms(plan, first_point, spectra, wind, index, weight, nl_coef):
    count_bins, points = spectra.shape
    padded = round_up(count_bins, LANES)
    depth = round_up(count_bins // NTH * RING, LANES)
    cosine, sine, _ = bin_tables(count_bins)
    tables = np.zeros((2, padded), np.float32)
    tables[0, :count_bins] = cosine
    tables[1, :count_bins] = sine
    smem = pl.BlockSpec(memory_space=pltpu.SMEM)
    vmem = pl.BlockSpec(memory_space=pltpu.VMEM)
    return pl.pallas_call(
        functools.partial(source_kernel, plan),
        out_shape=jax.ShapeDtypeStruct((plan.group, plan.rows(points), LANES), jnp.float32),
        in_specs=[smem] + [vmem] * 6,
        out_specs=vmem,
        scratch_shapes=[
            pltpu.VMEM((24, padded), jnp.int32),
            pltpu.VMEM((16, padded), jnp.float32),
            pltpu.VMEM((1, padded), jnp.float32),
            pltpu.VMEM((depth, points), jnp.float32),
            pltpu.VMEM((points, padded), jnp.float32),
            pltpu.VMEM((points, depth), jnp.bfloat16),
            pltpu.VMEM((points, LANES), jnp.float32),
            pltpu.VMEM((depth, 4 * padded), jnp.bfloat16),
            pltpu.VMEM((4 * padded, points), jnp.bfloat16),
            pltpu.VMEM((padded, points), jnp.float32),
            pltpu.VMEM((2, 2 * points, LANES), jnp.float32),
        ],
        compiler_params=pltpu.CompilerParams(vmem_limit_bytes=52 * 1024 * 1024),
        name="source_terms",
    )(first_point, spectra, wind, index, weight, nl_coef, jnp.asarray(tables))


def propagate_kernel(plan, slots, base, got, rel, taps, out, ranked, extra, lined, middle, pick, sea):
    group = got.shape[0]
    columns = rel.shape[0]
    per, columns_tile, halo = plan.per, plan.columns_tile, plan.halo
    main, rest, fold = plan.main, plan.rest, plan.fold
    half_lanes = lax.broadcasted_iota(jnp.int32, (1, LANES), 1) < LANES // 2
    rest_rows = round_up(rest, 8)

    def order(owner, carry):
        common = min(slots, COMMON)
        ranked[pl.ds(owner, common, stride=group), :] = got[owner, rest + fold:rest + fold + common, :]
        if slots > COMMON:
            ranked[pl.ds(owner + COMMON * group, slots - COMMON, stride=group), :] = got[
                owner, rest + 2 * fold + COMMON:rest + 2 * fold + slots, :
            ]
        if rest:
            lead = got[owner, :rest, :]
            near = got[owner, rest:rest + fold, :]
            first = near
            second = pltpu.roll(near, LANES // 2, 1)
            if slots > COMMON:
                away = got[owner, rest + fold + COMMON:rest + 2 * fold + COMMON, :]
                first = jnp.where(half_lanes, first, pltpu.roll(away, LANES // 2, 1))
                second = jnp.where(half_lanes, second, away)
            tail = jnp.concatenate([first[:rest - fold], second], axis=0)
            fill = jnp.zeros((LANES - rest, LANES), jnp.float32)
            extra[pl.ds(owner, LANES, stride=group), :] = jnp.concatenate([lead, fill], axis=0).T
            turned = jnp.concatenate([tail, fill], axis=0).T
            extra[pl.ds(owner + LANES * group, slots - LANES, stride=group), :] = turned[:slots - LANES]
        return carry

    lax.fori_loop(0, group, order, 0, unroll=4)

    rank_tiles = ranked.shape[0] // LANES
    padded = lined.shape[0]

    def line_up(tile, carry):
        start = pl.multiple_of(tile * LANES, LANES)
        lined[:round_up(main, 8), pl.ds(start, LANES)] = ranked[pl.ds(start, LANES), :].T[:round_up(main, 8)]
        if rest:
            lined[main:main + rest_rows, pl.ds(start, LANES)] = extra[pl.ds(start, LANES), :].T[:rest_rows]
        return carry

    lax.fori_loop(0, rank_tiles, line_up, 0, unroll=4)
    lined[:, rank_tiles * LANES:] = jnp.zeros((padded, 2 * LANES), jnp.float32)

    for column in range(columns):
        row = jnp.broadcast_to(rel[column:column + 1, :], (8, LANES))
        pick[column] = row
        sea[column] = jnp.where(row >= 0, 1.0, 0.0)

    lane = lax.broadcasted_iota(jnp.int32, (8, LANES), 1)

    def bins_step(first_bin, valid):
        span = pl.ds(first_bin, 8)
        x_taps = [jnp.broadcast_to(taps[span, k:k + 1], (8, LANES)) for k in range(5)]
        y_taps = []
        for k in range(5):
            tap = jnp.broadcast_to(taps[span, 5 + k:6 + k], (8, LANES))
            inside = (lane + (k - 2) >= 0) & (lane + (k - 2) < LANES)
            y_taps.append(jnp.where(inside, tap, 0.0))

        def expanded(column):
            start = pl.multiple_of(base[column], LANES)
            chosen = pick[column]
            within = chosen & (LANES - 1)
            low = jnp.take_along_axis(lined[span, pl.ds(start, LANES)], within, axis=1)
            high = jnp.take_along_axis(lined[span, pl.ds(start + LANES, LANES)], within, axis=1)
            return jnp.where(chosen >= LANES, high, low) * sea[column]

        def sweep(values, column):
            value = x_taps[2] * values[2]
            for k in (0, 1, 3, 4):
                value = value + x_taps[k] * values[k]
            value = value * sea[column]
            moved = y_taps[2] * value
            for k in (0, 1, 3, 4):
                moved = moved + y_taps[k] * pltpu.roll(value, (2 - k) % LANES, 1)
            return moved * sea[column]

        reach = halo // STEPS
        first = {}
        for column in range(columns):
            first[column] = expanded(column)
        for column in range(reach, columns - reach):
            middle[column] = sweep([first[(column + k) % columns] for k in range(-2, 3)], column)
        for column in range(halo, columns - halo):
            result = sweep([middle[(column + k) % columns] for k in range(-2, 3)], column)
            owner, place = divmod(column - halo, columns_tile)
            start = (owner * per + first_bin) * columns_tile + place
            if valid == 8:
                out[pl.ds(start, 8, stride=columns_tile), :] = result
            else:
                for row in range(valid):
                    out[pl.ds(start + row * columns_tile, 1), :] = result[row:row + 1]

    def full_step(tile, carry):
        bins_step(pl.multiple_of(tile * 8, 8), 8)
        return carry

    lax.fori_loop(0, per // 8, full_step, 0)
    if per % 8:
        bins_step(per // 8 * 8, per % 8)


def propagate(plan, slots, base, got, rel, taps):
    columns = rel.shape[0]
    padded = round_up(plan.per, 8)
    ranks = plan.group * slots
    smem = pl.BlockSpec(memory_space=pltpu.SMEM)
    vmem = pl.BlockSpec(memory_space=pltpu.VMEM)
    return pl.pallas_call(
        functools.partial(propagate_kernel, plan, slots),
        out_shape=jax.ShapeDtypeStruct(((columns - 2 * plan.halo) * plan.per, LANES), jnp.float32),
        in_specs=[smem, vmem, vmem, vmem],
        out_specs=vmem,
        scratch_shapes=[
            pltpu.VMEM((ranks, LANES), jnp.float32),
            pltpu.VMEM((ranks if plan.rest else 8, LANES), jnp.float32),
            pltpu.VMEM((padded, ranks + 2 * LANES), jnp.float32),
            pltpu.VMEM((columns, 8, LANES), jnp.float32),
            pltpu.VMEM((columns, 8, LANES), jnp.int32),
            pltpu.VMEM((columns, 8, LANES), jnp.float32),
        ],
        compiler_params=pltpu.CompilerParams(vmem_limit_bytes=52 * 1024 * 1024),
        name="propagate",
    )(base, got, rel, taps)


@dataclasses.dataclass(frozen=True)
class Plan:
    tiles: int
    halves: int
    parts: int
    half_bins: int
    columns: int

    @property
    def group(self):
        return self.tiles * self.halves

    @property
    def members(self):
        return self.tiles // self.parts

    @property
    def per(self):
        return -(-self.half_bins // self.members)

    @property
    def main(self):
        return min(self.per, LANES)

    @property
    def rest(self):
        return self.per - self.main

    @property
    def fold(self):
        return -(-self.rest // 2)

    @property
    def columns_tile(self):
        return self.columns // self.tiles

    @property
    def halo(self):
        return 2 * STEPS if self.parts > 1 else 0

    @property
    def window(self):
        return self.columns // self.parts + 2 * self.halo

    def rows(self, slots):
        return self.rest + (2 if slots > COMMON else 1) * self.fold + slots


def shards(spectra, wind, mask, dia_index, dia_weight, nl_coef):
    count_bins, points = spectra.shape
    columns, latitudes = mask.shape
    plan = Plan(
        tiles=lax.axis_size("tile"), halves=lax.axis_size("bin"), parts=2,
        half_bins=count_bins // lax.axis_size("bin"), columns=columns,
    )
    group, members, parts, halo, window = plan.group, plan.members, plan.parts, plan.halo, plan.window
    sea_total = group * points
    tile_rank = lax.axis_index("tile")

    ones = mask.astype(jnp.bfloat16)
    counts = jnp.sum(mask, axis=1)
    before = jnp.sum(
        jnp.where(np.tril(np.ones((columns, columns), bool), -1), counts[None, :], 0), axis=1
    )
    reach = np.zeros((parts, columns), bool)
    for part in range(parts):
        reach[part, (part * (columns // parts) - halo + np.arange(window)) % columns] = True
    held = jnp.sum(jnp.where(reach, counts[None, :], 0), axis=1)
    starts = jnp.stack([before[(part * (columns // parts) - halo) % columns] for part in range(parts)])
    need = -(-(held + starts % group) // group)
    first_point = jnp.where(need <= points, starts // group, 0)
    wanted = lax.pmax(jnp.max(need), "band")

    payload = source_terms(plan, first_point, spectra, wind, dia_index, dia_weight, nl_coef)

    cosine, sine, speed = bin_tables(count_bins)
    weights = np.concatenate([stencil(speed * cosine), stencil(speed * sine)])
    table = np.zeros((plan.halves, members, round_up(plan.per, 8), LANES), np.float32)
    for side in range(plan.halves):
        for member in range(members):
            valid = max(0, min(plan.per, plan.half_bins - member * plan.per))
            begin = side * plan.half_bins + member * plan.per
            table[side, member, :valid, :10] = weights[:, begin:begin + valid].T
    taps = lax.dynamic_slice(
        jnp.asarray(table), (lax.axis_index("bin"), tile_rank % members, 0, 0), (1, 1) + table.shape[2:]
    ).reshape(table.shape[2:])

    part = tile_rank // members
    begin = (part * (columns // parts) - halo) % columns
    upto = jnp.dot(ones, jnp.asarray(np.triu(np.ones((latitudes, latitudes))), jnp.bfloat16),
                   preferred_element_type=jnp.float32).astype(jnp.int32)
    place = (before - first_point[part] * group) % sea_total
    floor = place // LANES * LANES
    rel = jnp.where(mask == 1, upto - 1 + (place - floor)[:, None], -1)
    floor = lax.dynamic_slice(jnp.concatenate([floor, floor]), (begin,), (window,))
    rel = lax.dynamic_slice(jnp.concatenate([rel, rel]), (begin, 0), (window, latitudes))

    def with_slots(slots):
        def run(payload, floor, rel, taps):
            got = lax.all_to_all(
                payload[:, :plan.rows(slots)], ("tile", "bin"), split_axis=0, concat_axis=0, tiled=True
            )
            return propagate(plan, slots, floor, got, rel, taps)

        return run

    sizes = [size for size in SIZES if size < points] + [points]
    choice = sum((wanted > size).astype(jnp.int32) for size in sizes[:-1])
    moved = lax.switch(choice, [with_slots(size) for size in sizes], payload, floor, rel, taps)
    result = lax.all_to_all(
        moved.reshape(members, plan.per, plan.columns_tile, latitudes), "tile", split_axis=0, concat_axis=0,
        axis_index_groups=[list(range(p * members, (p + 1) * members)) for p in range(parts)], tiled=True,
    ).reshape(members * plan.per, plan.columns_tile, latitudes)
    return result[:plan.half_bins]


def solution(mesh):
    in_specs = (
        P(None, ("band", "tile", "bin")),
        P(None, ("band", "tile", "bin")),
        P(None, "band"),
        P(),
        P(),
        P(),
    )
    out_specs = P("bin", "tile", "band")
    return jax.shard_map(shards, mesh=mesh, in_specs=in_specs, out_specs=out_specs, check_vma=False)
```

```python
import dataclasses
import functools
import math

import jax
import jax.numpy as jnp
import numpy as np
from jax import lax
from jax.experimental import pallas as pl
from jax.experimental.pallas import tpu as pltpu
from jax.sharding import PartitionSpec as P

NTH = 36
STEPS = 2
LANES = 128
ROWS = 256
RING = 40
COMMON = 192
VMEM_BYTES = 58 * 1024 * 1024
SIZES = (160, 176, 192, 208, 224)

LAMBDA = 0.25
COEF_THREE = (1.0 + LAMBDA) ** (-4)
COEF_FOUR = (1.0 - LAMBDA) ** (-4)
COEF_BOTH = (1.0 - LAMBDA * LAMBDA) ** (-4)
CFL_LIMIT = 0.8
WIND_RATE = 0.2


def round_up(value, step):
    return -(-value // step) * step


def bin_tables(count_bins):
    bin_range = np.arange(count_bins)
    theta = 2.0 * math.pi * (bin_range % NTH) / NTH
    group_speed = CFL_LIMIT * 1.1 ** (-(bin_range // NTH).astype(np.float64))
    return np.cos(theta), np.sin(theta), group_speed


def stencil(courant):
    bend = (1.0 - courant * courant) / 6.0
    up = courant >= 0.0
    zero = np.zeros_like(courant)
    left = courant * np.where(up, -bend, zero)
    here = courant * (0.5 + 0.5 * courant + np.where(up, 2.0 * bend, -bend))
    right = courant * (0.5 - 0.5 * courant + np.where(up, -bend, 2.0 * bend))
    far = courant * np.where(up, zero, -bend)
    return np.stack([left, here - left, 1.0 + right - here, far - right, -far])


def source_kernel(plan, first_point, spectra_far, wind_far, index_far, weight_far, nl_far, tables_far, out,
                  spectra, wind, index, weight, nl_coef, tables, arrived, code, weight_pad, nl_pad, spaced, flat_t, low_t, wind_t, matrix, inter, total, twice):
    count_bins, points = spectra.shape
    padded = flat_t.shape[1]
    chunks = padded // LANES
    rings = count_bins // NTH
    depth = spaced.shape[0]
    whole = count_bins // LANES
    rest = count_bins - whole * LANES
    pairs = [(index_far, index), (weight_far, weight), (nl_far, nl_coef), (wind_far, wind),
             (tables_far, tables), (spectra_far, spectra)]
    copies = [pltpu.make_async_copy(far, near, arrived.at[k]) for k, (far, near) in enumerate(pairs)]
    for copy in copies:
        copy.start()

    code[...] = jnp.zeros(code.shape, jnp.int32)
    weight_pad[...] = jnp.zeros(weight_pad.shape, jnp.float32)
    nl_pad[...] = jnp.zeros(nl_pad.shape, jnp.float32)
    for copy in copies:
        copy.wait()
    nl_pad[:, :count_bins] = nl_coef[...].reshape(1, count_bins)
    for mirror in range(2):
        for member in range(2):
            row = (mirror * 2 + member) * 4
            bins = index[mirror, member]
            ring = ((bins.astype(jnp.float32) + 0.5) * (1.0 / NTH)).astype(jnp.int32)
            lowest = jnp.minimum(jnp.minimum(ring[0:1], ring[1:2]), jnp.minimum(ring[2:3], ring[3:4]))
            direction = bins - ring * NTH
            code[row:row + 4, :count_bins] = jnp.where(ring == lowest, direction, direction + RING)
            code[16 + mirror * 2 + member:17 + mirror * 2 + member, :count_bins] = lowest
            weight_pad[row:row + 4, :count_bins] = weight[mirror, member].astype(jnp.float32)

    gap = jnp.zeros((RING - NTH, points), jnp.float32)
    for ring in range(rings):
        spaced[ring * RING:ring * RING + NTH, :] = spectra[ring * NTH:(ring + 1) * NTH, :]
        spaced[ring * RING + NTH:(ring + 1) * RING, :] = gap
    spaced[rings * RING:, :] = jnp.zeros((depth - rings * RING, points), jnp.float32)
    for half in range(points // LANES):
        span = slice(half * LANES, (half + 1) * LANES)
        for block in range(depth // LANES):
            lanes = slice(block * LANES, (block + 1) * LANES)
            low_t[span, lanes] = spaced[lanes, span].T.astype(jnp.bfloat16)
        for block in range(chunks):
            lanes = slice(block * LANES, (block + 1) * LANES)
            if block < whole:
                values = spectra[lanes, span]
            else:
                values = jnp.concatenate(
                    [spectra[whole * LANES:, span], jnp.zeros((LANES - rest, LANES), jnp.float32)], axis=0
                )
            flat_t[span, lanes] = values.T
        drive = jnp.concatenate([wind[:, span], jnp.zeros((LANES - 2, LANES), jnp.float32)], axis=0)
        wind_t[span, :] = drive.T

    used = rings * RING
    matrix[used:, :] = jnp.zeros((depth - used, matrix.shape[1]), jnp.bfloat16)

    def chunk_step(chunk, carry):
        lane = pl.multiple_of(chunk * LANES, LANES)
        lanes = pl.ds(lane, LANES)
        wide = pl.multiple_of(chunk * 4 * LANES, 4 * LANES)
        place = lax.broadcasted_iota(jnp.int32, (RING, LANES), 0)
        nothing = jnp.zeros((RING, LANES), jnp.float32)
        patterns = []
        for pair in range(4):
            low = nothing
            high = nothing
            for corner in range(4):
                r = pair * 4 + corner
                where = code[pl.ds(r, 1), lanes]
                amount = jnp.broadcast_to(weight_pad[pl.ds(r, 1), lanes], (RING, LANES))
                low = jnp.where(place == where, amount, low)
                high = jnp.where(place + RING == where, amount, high)
            lowest = jnp.broadcast_to(code[pl.ds(16 + pair, 1), lanes], (8, LANES))
            patterns.append((low, high, lowest))
        members = [jnp.zeros((points, 2 * LANES), jnp.float32) for _ in range(2)]
        done = 0
        for ring in range(0, rings, 2):
            for pair in range(4):
                low, high, lowest = patterns[pair]
                parts = []
                for offset in range(2):
                    first = lowest == ring + offset
                    second = lowest == ring + offset - 1
                    for sub in range(0, RING, 8):
                        parts.append(
                            jnp.where(first, low[sub:sub + 8], jnp.where(second, high[sub:sub + 8], 0.0))
                        )
                matrix[ring * RING:(ring + 2) * RING, pl.ds(wide + pair * LANES, LANES)] = jnp.concatenate(
                    parts, axis=0
                ).astype(jnp.bfloat16)
            ready = (ring + 2) * RING
            while done < depth and (ready >= done + ROWS or ready == used):
                size = min(ROWS, depth - done)
                for mirror in range(2):
                    members[mirror] = members[mirror] + jnp.dot(
                        low_t[:, done:done + size],
                        matrix[done:done + size, pl.ds(wide + mirror * 2 * LANES, 2 * LANES)],
                        preferred_element_type=jnp.float32,
                    )
                done += size
        values = flat_t[:, lanes]
        coef = nl_pad[:, lanes]
        drive = jnp.maximum(
            wind_t[:, 0:1] * tables[0:1, lanes] + wind_t[:, 1:2] * tables[1:2, lanes], 0.0
        )
        base = values + WIND_RATE * drive * values
        for mirror in range(2):
            third = members[mirror][:, :LANES]
            fourth = members[mirror][:, LANES:]
            interaction = coef * (
                values * values * (COEF_THREE * third + COEF_FOUR * fourth)
                - 2.0 * COEF_BOTH * values * third * fourth
            )
            base = base - 2.0 * interaction
            for half in range(points // LANES):
                span = slice(half * LANES, (half + 1) * LANES)
                turned = interaction[span].T.astype(jnp.bfloat16)
                for member in range(2):
                    inter[pl.ds(wide + (mirror * 2 + member) * LANES, LANES), span] = turned
        for half in range(points // LANES):
            span = slice(half * LANES, (half + 1) * LANES)
            total[lanes, span] = base[span].T
        return carry

    lax.fori_loop(0, chunks, chunk_step, 0)
    for start in range(0, used, ROWS):
        size = min(ROWS, used - start)
        spaced[start:start + size, :] = jnp.dot(
            matrix[start:start + size, :], inter[...], preferred_element_type=jnp.float32
        )
    for ring in range(rings):
        total[ring * NTH:(ring + 1) * NTH, :] += spaced[ring * RING:ring * RING + NTH, :]
    pack_payload(plan, first_point, total, out, twice)


def pack_payload(plan, first_point, total, out, twice):
    points = total.shape[1]
    main, rest, fold = plan.main, plan.rest, plan.fold
    lane = lax.broadcasted_iota(jnp.int32, (1, LANES), 1)
    for side in range(plan.halves):
        for member in range(plan.members):
            first = side * plan.half_bins + member * plan.per
            valid = min(main, plan.half_bins - member * plan.per)
            slot = (side * plan.members + member) % 2
            for half in range(points // LANES):
                values = total[first:first + valid, half * LANES:(half + 1) * LANES]
                if valid < LANES:
                    values = jnp.concatenate([values, jnp.zeros((LANES - valid, LANES), jnp.float32)], axis=0)
                turned = values.T
                twice[slot, half * LANES:(half + 1) * LANES, :] = turned
                twice[slot, points + half * LANES:points + (half + 1) * LANES, :] = turned
            for part in range(plan.parts):
                owner = (part * plan.members + member) * plan.halves + side
                begin = lax.rem(first_point[part], points)
                out[owner, rest + fold:rest + fold + COMMON, :] = twice[slot, pl.ds(begin, COMMON), :]
                out[owner, rest + 2 * fold + COMMON:rest + 2 * fold + points, :] = twice[
                    slot, pl.ds(begin + COMMON, points - COMMON), :
                ]
                if not rest:
                    continue
                shift = lax.rem(begin, LANES)
                swapped = begin >= LANES
                near = pltpu.roll(total[first + main:first + main + rest, :LANES], lax.rem(LANES - shift, LANES), 1)
                away = pltpu.roll(total[first + main:first + main + rest, LANES:], lax.rem(LANES - shift, LANES), 1)
                keep = (lane < LANES - shift) != swapped
                lead = jnp.where(keep, near, away)
                tail = jnp.where(keep, away, near)
                moved = pltpu.roll(tail, LANES // 2, 1)
                out[owner, :rest, :] = lead
                out[owner, rest:rest + fold, :] = jnp.where(lane < LANES // 2, tail[:fold], moved[rest - fold:])
                out[owner, rest + fold + COMMON:rest + 2 * fold + COMMON, :] = jnp.where(
                    lane < LANES // 2, moved[:fold], tail[rest - fold:]
                )


def source_terms(plan, first_point, spectra, wind, index, weight, nl_coef):
    count_bins, points = spectra.shape
    padded = round_up(count_bins, LANES)
    depth = round_up(count_bins // NTH * RING, LANES)
    cosine, sine, _ = bin_tables(count_bins)
    tables = np.zeros((2, padded), np.float32)
    tables[0, :count_bins] = cosine
    tables[1, :count_bins] = sine
    smem = pl.BlockSpec(memory_space=pltpu.SMEM)
    vmem = pl.BlockSpec(memory_space=pltpu.VMEM)
    operands = (spectra, wind, index, weight, nl_coef, jnp.asarray(tables))
    return pl.pallas_call(
        functools.partial(source_kernel, plan),
        out_shape=jax.ShapeDtypeStruct((plan.group, plan.rows(points), LANES), jnp.float32),
        in_specs=[smem] + [pl.BlockSpec(memory_space=pl.ANY)] * len(operands),
        out_specs=vmem,
        scratch_shapes=[pltpu.VMEM(operand.shape, operand.dtype) for operand in operands] + [
            pltpu.SemaphoreType.DMA((len(operands),)),
            pltpu.VMEM((24, padded), jnp.int32),
            pltpu.VMEM((16, padded), jnp.float32),
            pltpu.VMEM((1, padded), jnp.float32),
            pltpu.VMEM((depth, points), jnp.float32),
            pltpu.VMEM((points, padded), jnp.float32),
            pltpu.VMEM((points, depth), jnp.bfloat16),
            pltpu.VMEM((points, LANES), jnp.float32),
            pltpu.VMEM((depth, 4 * padded), jnp.bfloat16),
            pltpu.VMEM((4 * padded, points), jnp.bfloat16),
            pltpu.VMEM((padded, points), jnp.float32),
            pltpu.VMEM((2, 2 * points, LANES), jnp.float32),
        ],
        compiler_params=pltpu.CompilerParams(vmem_limit_bytes=VMEM_BYTES),
        cost_estimate=pl.CostEstimate(
            flops=4 * depth * 4 * padded * points, bytes_accessed=8 * count_bins * points, transcendentals=0
        ),
        name="source_terms",
    )(first_point, *operands)


def ranks_kernel(plan, sea_total, part, mask, triangle, need, first_point, floor, rel):
    columns, latitudes = mask.shape
    sea = mask[...].astype(jnp.float32).astype(jnp.bfloat16)

    def product(left, right):
        return jnp.dot(left, right, preferred_element_type=jnp.float32)

    upto = product(sea, triangle[...])
    counts = lax.dot_general(
        jnp.ones((8, latitudes), jnp.bfloat16), sea, (((1,), (1,)), ((), ())), preferred_element_type=jnp.float32
    )
    row = lax.broadcasted_iota(jnp.int32, (columns, columns), 0)
    col = lax.broadcasted_iota(jnp.int32, (columns, columns), 1)
    before_row = product(counts.astype(jnp.bfloat16), jnp.where(row < col, 1.0, 0.0).astype(jnp.bfloat16))
    before_col = jnp.sum(product(jnp.where(col < row, 1.0, 0.0).astype(jnp.bfloat16), sea), axis=1, keepdims=True)
    lane = lax.broadcasted_iota(jnp.int32, (1, columns), 1)
    most = 0
    chosen = 0
    for p in range(plan.parts):
        begin = (p * (columns // plan.parts) - plan.halo) % columns
        inside = (lane + (columns - begin)) & (columns - 1)
        start = jnp.sum(jnp.where(lane == begin, before_row[:1], 0.0)).astype(jnp.int32)
        held = jnp.sum(jnp.where(inside < plan.window, counts[:1], 0.0)).astype(jnp.int32)
        wanted = (held + lax.rem(start, plan.group) + plan.group - 1) // plan.group
        first = jnp.where(wanted * plan.group <= sea_total, start // plan.group, 0)
        first_point[p] = first
        most = jnp.maximum(most, wanted)
        chosen = jnp.where(part[0] == p, first, chosen)
    need[0] = most

    def split(before):
        place = before.astype(jnp.int32) - chosen * plan.group
        place = jnp.where(place < 0, place + sea_total, place)
        within = place & (LANES - 1)
        return place - within, within

    floor[...] = split(before_row[:1])[0]
    rel[...] = jnp.where(mask[...] == 1, upto.astype(jnp.int32) - 1 + split(before_col)[1], -1)


def sea_ranks(plan, sea_total, part, mask):
    columns, latitudes = mask.shape
    smem = pl.BlockSpec(memory_space=pltpu.SMEM)
    vmem = pl.BlockSpec(memory_space=pltpu.VMEM)
    return pl.pallas_call(
        functools.partial(ranks_kernel, plan, sea_total),
        out_shape=[
            jax.ShapeDtypeStruct((1,), jnp.int32),
            jax.ShapeDtypeStruct((plan.parts,), jnp.int32),
            jax.ShapeDtypeStruct((1, columns), jnp.int32),
            jax.ShapeDtypeStruct((columns, latitudes), jnp.int32),
        ],
        in_specs=[smem, vmem, vmem],
        out_specs=[smem, smem, vmem, vmem],
        name="sea_ranks",
    )(part, mask, jnp.asarray(np.triu(np.ones((latitudes, latitudes))), jnp.bfloat16))


def propagate_kernel(plan, slots, part, base, got, rel, taps, out, ranked, extra, lined, pick, sea):
    group = got.shape[0]
    columns = plan.window
    all_columns = rel.shape[0]
    begin = part[0] * (all_columns // plan.parts) + (all_columns - plan.halo)
    per, columns_tile, halo = plan.per, plan.columns_tile, plan.halo
    main, rest, fold = plan.main, plan.rest, plan.fold
    half_lanes = lax.broadcasted_iota(jnp.int32, (1, LANES), 1) < LANES // 2
    rest_rows = round_up(rest, 8)

    def order(owner, carry):
        common = min(slots, COMMON)
        ranked[pl.ds(owner, common, stride=group), :] = got[owner, rest + fold:rest + fold + common, :]
        if slots > COMMON:
            ranked[pl.ds(owner + COMMON * group, slots - COMMON, stride=group), :] = got[
                owner, rest + 2 * fold + COMMON:rest + 2 * fold + slots, :
            ]
        if rest:
            lead = got[owner, :rest, :]
            near = got[owner, rest:rest + fold, :]
            first = near
            second = pltpu.roll(near, LANES // 2, 1)
            if slots > COMMON:
                away = got[owner, rest + fold + COMMON:rest + 2 * fold + COMMON, :]
                first = jnp.where(half_lanes, first, pltpu.roll(away, LANES // 2, 1))
                second = jnp.where(half_lanes, second, away)
            tail = jnp.concatenate([first[:rest - fold], second], axis=0)
            fill = jnp.zeros((LANES - rest, LANES), jnp.float32)
            extra[pl.ds(owner, LANES, stride=group), :] = jnp.concatenate([lead, fill], axis=0).T
            turned = jnp.concatenate([tail, fill], axis=0).T
            extra[pl.ds(owner + LANES * group, slots - LANES, stride=group), :] = turned[:slots - LANES]
        return carry

    lax.fori_loop(0, group, order, 0, unroll=4)

    rank_tiles = ranked.shape[0] // LANES
    padded = lined.shape[0]

    def line_up(tile, carry):
        start = pl.multiple_of(tile * LANES, LANES)
        lined[:round_up(main, 8), pl.ds(start, LANES)] = ranked[pl.ds(start, LANES), :].T[:round_up(main, 8)]
        if rest:
            lined[main:main + rest_rows, pl.ds(start, LANES)] = extra[pl.ds(start, LANES), :].T[:rest_rows]
        return carry

    lax.fori_loop(0, rank_tiles, line_up, 0, unroll=4)
    lined[:, rank_tiles * LANES:] = jnp.zeros((padded, 2 * LANES), jnp.float32)

    for column in range(columns):
        row = jnp.broadcast_to(rel[pl.ds(lax.rem(begin + column, all_columns), 1), :], (8, LANES))
        pick[column] = row
        sea[column] = jnp.where(row >= 0, 1.0, 0.0)

    lane = lax.broadcasted_iota(jnp.int32, (8, LANES), 1)

    def bins_step(first_bin, valid):
        span = pl.ds(first_bin, 8)
        x_taps = [jnp.broadcast_to(taps[span, k:k + 1], (8, LANES)) for k in range(5)]
        y_taps = []
        for k in range(5):
            tap = jnp.broadcast_to(taps[span, 5 + k:6 + k], (8, LANES))
            inside = (lane + (k - 2) >= 0) & (lane + (k - 2) < LANES)
            y_taps.append(jnp.where(inside, tap, 0.0))

        def expanded(column):
            start = pl.multiple_of(base[0, lax.rem(begin + column, all_columns)], LANES)
            chosen = pick[column]
            within = chosen & (LANES - 1)
            low = jnp.take_along_axis(lined[span, pl.ds(start, LANES)], within, axis=1)
            high = jnp.take_along_axis(lined[span, pl.ds(start + LANES, LANES)], within, axis=1)
            return jnp.where(chosen >= LANES, high, low) * sea[column]

        def store(result, column):
            owner, place = divmod(column - halo, columns_tile)
            start = (owner * per + first_bin) * columns_tile + place
            if valid == 8:
                out[pl.ds(start, 8, stride=columns_tile), :] = result
            else:
                for row in range(valid):
                    out[pl.ds(start + row * columns_tile, 1), :] = result[row:row + 1]

        def sweep(values, column):
            value = x_taps[2] * values[2]
            for k in (0, 1, 3, 4):
                value = value + x_taps[k] * values[k]
            value = value * sea[column]
            moved = y_taps[2] * value
            for k in (0, 1, 3, 4):
                moved = moved + y_taps[k] * pltpu.roll(value, (2 - k) % LANES, 1)
            return moved * sea[column]

        reach = halo // STEPS
        first = {}
        middle = {}

        def neighbours(values, column):
            return [values.get((column + k) % columns) for k in range(-2, 3)]

        waiting = list(range(reach, columns - reach))
        last = list(range(halo, columns - halo))
        for column in range(columns):
            first[column] = expanded(column)
            for ready in [c for c in waiting if all(v is not None for v in neighbours(first, c))]:
                middle[ready] = sweep(neighbours(first, ready), ready)
                waiting.remove(ready)
            for ready in [c for c in last if all(v is not None for v in neighbours(middle, c))]:
                store(sweep(neighbours(middle, ready), ready), ready)
                last.remove(ready)

    def full_step(tile, carry):
        bins_step(pl.multiple_of(tile * 8, 8), 8)
        return carry

    lax.fori_loop(0, per // 8, full_step, 0)
    if per % 8:
        bins_step(per // 8 * 8, per % 8)


def propagate(plan, slots, part, base, got, rel, taps):
    columns = plan.window
    padded = round_up(plan.per, 8)
    ranks = plan.group * slots
    smem = pl.BlockSpec(memory_space=pltpu.SMEM)
    vmem = pl.BlockSpec(memory_space=pltpu.VMEM)
    return pl.pallas_call(
        functools.partial(propagate_kernel, plan, slots),
        out_shape=jax.ShapeDtypeStruct(((columns - 2 * plan.halo) * plan.per, LANES), jnp.float32),
        in_specs=[smem, smem, vmem, vmem, vmem],
        out_specs=vmem,
        scratch_shapes=[
            pltpu.VMEM((ranks, LANES), jnp.float32),
            pltpu.VMEM((ranks if plan.rest else 8, LANES), jnp.float32),
            pltpu.VMEM((padded, ranks + 2 * LANES), jnp.float32),
            pltpu.VMEM((columns, 8, LANES), jnp.int32),
            pltpu.VMEM((columns, 8, LANES), jnp.float32),
        ],
        compiler_params=pltpu.CompilerParams(vmem_limit_bytes=VMEM_BYTES),
        name="propagate",
    )(part, base, got, rel, taps)


@dataclasses.dataclass(frozen=True)
class Plan:
    tiles: int
    halves: int
    parts: int
    half_bins: int
    columns: int

    @property
    def group(self):
        return self.tiles * self.halves

    @property
    def members(self):
        return self.tiles // self.parts

    @property
    def per(self):
        return -(-self.half_bins // self.members)

    @property
    def main(self):
        return min(self.per, LANES)

    @property
    def rest(self):
        return self.per - self.main

    @property
    def fold(self):
        return -(-self.rest // 2)

    @property
    def columns_tile(self):
        return self.columns // self.tiles

    @property
    def halo(self):
        return 2 * STEPS if self.parts > 1 else 0

    @property
    def window(self):
        return self.columns // self.parts + 2 * self.halo

    def rows(self, slots):
        return self.rest + (2 if slots > COMMON else 1) * self.fold + slots


def shards(spectra, wind, mask, dia_index, dia_weight, nl_coef):
    count_bins, points = spectra.shape
    columns, latitudes = mask.shape
    plan = Plan(
        tiles=lax.axis_size("tile"), halves=lax.axis_size("bin"), parts=2,
        half_bins=count_bins // lax.axis_size("bin"), columns=columns,
    )
    members, parts = plan.members, plan.parts
    sea_total = plan.group * points
    tile_rank = lax.axis_index("tile")

    part = (tile_rank // members).astype(jnp.int32).reshape(1)
    need, first_point, floor, rel = sea_ranks(plan, sea_total, part, mask)
    wanted = need
    bands = lax.axis_size("band")
    for step in range(1, bands):
        wanted = jnp.maximum(
            wanted, lax.ppermute(need, "band", [(band, (band + step) % bands) for band in range(bands)])
        )
    wanted = wanted[0]

    payload = source_terms(plan, first_point, spectra, wind, dia_index, dia_weight, nl_coef)

    cosine, sine, speed = bin_tables(count_bins)
    weights = np.concatenate([stencil(speed * cosine), stencil(speed * sine)])
    table = np.zeros((plan.halves, members, round_up(plan.per, 8), LANES), np.float32)
    for side in range(plan.halves):
        for member in range(members):
            valid = max(0, min(plan.per, plan.half_bins - member * plan.per))
            begin = side * plan.half_bins + member * plan.per
            table[side, member, :valid, :10] = weights[:, begin:begin + valid].T
    taps = lax.dynamic_slice(
        jnp.asarray(table), (lax.axis_index("bin"), tile_rank % members, 0, 0), (1, 1) + table.shape[2:]
    ).reshape(table.shape[2:])

    def with_slots(slots):
        def run(payload, part, floor, rel, taps):
            got = lax.all_to_all(
                payload[:, :plan.rows(slots)], ("tile", "bin"), split_axis=0, concat_axis=0, tiled=True
            )
            return propagate(plan, slots, part, floor, got, rel, taps)

        return run

    sizes = [size for size in SIZES if size < points] + [points]
    choice = sum((wanted > size).astype(jnp.int32) for size in sizes[:-1])
    moved = lax.switch(choice, [with_slots(size) for size in sizes], payload, part, floor, rel, taps)
    result = lax.all_to_all(
        moved.reshape(members, plan.per, plan.columns_tile, latitudes), "tile", split_axis=0, concat_axis=0,
        axis_index_groups=[list(range(p * members, (p + 1) * members)) for p in range(parts)], tiled=True,
    ).reshape(members * plan.per, plan.columns_tile, latitudes)
    return result[:plan.half_bins]


def solution(mesh):
    in_specs = (
        P(None, ("band", "tile", "bin")),
        P(None, ("band", "tile", "bin")),
        P(None, "band"),
        P(),
        P(),
        P(),
    )
    out_specs = P("bin", "tile", "band")
    return jax.shard_map(shards, mesh=mesh, in_specs=in_specs, out_specs=out_specs, check_vma=False)
```

```python
import dataclasses
import functools
import math

import jax
import jax.numpy as jnp
import numpy as np
from jax import lax
from jax.experimental import pallas as pl
from jax.experimental.pallas import tpu as pltpu
from jax.sharding import PartitionSpec as P

NTH = 36
STEPS = 2
LANES = 128
ROWS = 256
RING = 40
COMMON = 192
VMEM_BYTES = 58 * 1024 * 1024
SIZES = (160, 176, 192, 208, 224, 240)
BATCH = 8

LAMBDA = 0.25
COEF_THREE = (1.0 + LAMBDA) ** (-4)
COEF_FOUR = (1.0 - LAMBDA) ** (-4)
COEF_BOTH = (1.0 - LAMBDA * LAMBDA) ** (-4)
CFL_LIMIT = 0.8
WIND_RATE = 0.2


def round_up(value, step):
    return -(-value // step) * step


def bin_tables(count_bins):
    bin_range = np.arange(count_bins)
    theta = 2.0 * math.pi * (bin_range % NTH) / NTH
    group_speed = CFL_LIMIT * 1.1 ** (-(bin_range // NTH).astype(np.float64))
    return np.cos(theta), np.sin(theta), group_speed


def stencil(courant):
    bend = (1.0 - courant * courant) / 6.0
    up = courant >= 0.0
    zero = np.zeros_like(courant)
    left = courant * np.where(up, -bend, zero)
    here = courant * (0.5 + 0.5 * courant + np.where(up, 2.0 * bend, -bend))
    right = courant * (0.5 - 0.5 * courant + np.where(up, -bend, 2.0 * bend))
    far = courant * np.where(up, zero, -bend)
    return np.stack([left, here - left, 1.0 + right - here, far - right, -far])


def source_kernel(plan, first_point, spectra_far, wind_far, index_far, weight_far, nl_far, tables_far, out,
                  spectra, wind, index, weight, nl_coef, tables, arrived, code, weight_pad, nl_pad, spaced, flat_t, low_t, wind_t, matrix, inter, total, twice):
    count_bins, points = spectra.shape
    padded = flat_t.shape[1]
    chunks = padded // LANES
    rings = count_bins // NTH
    depth = spaced.shape[0]
    whole = count_bins // LANES
    rest = count_bins - whole * LANES
    pairs = [(index_far, index), (weight_far, weight), (nl_far, nl_coef), (wind_far, wind),
             (tables_far, tables), (spectra_far, spectra)]
    copies = [pltpu.make_async_copy(far, near, arrived.at[k]) for k, (far, near) in enumerate(pairs)]
    for copy in copies:
        copy.start()

    code[...] = jnp.zeros(code.shape, jnp.int32)
    weight_pad[...] = jnp.zeros(weight_pad.shape, jnp.float32)
    nl_pad[...] = jnp.zeros(nl_pad.shape, jnp.float32)
    for copy in copies:
        copy.wait()
    nl_pad[:, :count_bins] = nl_coef[...].reshape(1, count_bins)
    for mirror in range(2):
        for member in range(2):
            row = (mirror * 2 + member) * 4
            bins = index[mirror, member]
            ring = ((bins.astype(jnp.float32) + 0.5) * (1.0 / NTH)).astype(jnp.int32)
            lowest = jnp.minimum(jnp.minimum(ring[0:1], ring[1:2]), jnp.minimum(ring[2:3], ring[3:4]))
            direction = bins - ring * NTH
            code[row:row + 4, :count_bins] = jnp.where(ring == lowest, direction, direction + RING)
            code[16 + mirror * 2 + member:17 + mirror * 2 + member, :count_bins] = lowest
            weight_pad[row:row + 4, :count_bins] = weight[mirror, member].astype(jnp.float32)

    gap = jnp.zeros((RING - NTH, points), jnp.float32)
    for ring in range(rings):
        spaced[ring * RING:ring * RING + NTH, :] = spectra[ring * NTH:(ring + 1) * NTH, :]
        spaced[ring * RING + NTH:(ring + 1) * RING, :] = gap
    spaced[rings * RING:, :] = jnp.zeros((depth - rings * RING, points), jnp.float32)
    for half in range(points // LANES):
        span = slice(half * LANES, (half + 1) * LANES)
        for block in range(depth // LANES):
            lanes = slice(block * LANES, (block + 1) * LANES)
            low_t[span, lanes] = spaced[lanes, span].T.astype(jnp.bfloat16)
        for block in range(chunks):
            lanes = slice(block * LANES, (block + 1) * LANES)
            if block < whole:
                values = spectra[lanes, span]
            else:
                values = jnp.concatenate(
                    [spectra[whole * LANES:, span], jnp.zeros((LANES - rest, LANES), jnp.float32)], axis=0
                )
            flat_t[span, lanes] = values.T
        drive = jnp.concatenate([wind[:, span], jnp.zeros((LANES - 2, LANES), jnp.float32)], axis=0)
        wind_t[span, :] = drive.T

    used = rings * RING
    matrix[used:, :] = jnp.zeros((depth - used, matrix.shape[1]), jnp.bfloat16)

    def chunk_step(chunk, carry):
        lane = pl.multiple_of(chunk * LANES, LANES)
        lanes = pl.ds(lane, LANES)
        wide = pl.multiple_of(chunk * 4 * LANES, 4 * LANES)
        place = lax.broadcasted_iota(jnp.int32, (RING, LANES), 0)
        nothing = jnp.zeros((RING, LANES), jnp.float32)
        patterns = []
        for pair in range(4):
            low = nothing
            high = nothing
            for corner in range(4):
                r = pair * 4 + corner
                where = code[pl.ds(r, 1), lanes]
                amount = jnp.broadcast_to(weight_pad[pl.ds(r, 1), lanes], (RING, LANES))
                low = jnp.where(place == where, amount, low)
                high = jnp.where(place + RING == where, amount, high)
            lowest = jnp.broadcast_to(code[pl.ds(16 + pair, 1), lanes], (8, LANES))
            patterns.append((low, high, lowest))
        members = [jnp.zeros((points, 2 * LANES), jnp.float32) for _ in range(2)]
        done = 0
        for ring in range(0, rings, 2):
            for pair in range(4):
                low, high, lowest = patterns[pair]
                parts = []
                for offset in range(2):
                    first = lowest == ring + offset
                    second = lowest == ring + offset - 1
                    for sub in range(0, RING, 8):
                        parts.append(
                            jnp.where(first, low[sub:sub + 8], jnp.where(second, high[sub:sub + 8], 0.0))
                        )
                matrix[ring * RING:(ring + 2) * RING, pl.ds(wide + pair * LANES, LANES)] = jnp.concatenate(
                    parts, axis=0
                ).astype(jnp.bfloat16)
            ready = (ring + 2) * RING
            while done < depth and (ready >= done + ROWS or ready == used):
                size = min(ROWS, depth - done)
                for mirror in range(2):
                    members[mirror] = members[mirror] + jnp.dot(
                        low_t[:, done:done + size],
                        matrix[done:done + size, pl.ds(wide + mirror * 2 * LANES, 2 * LANES)],
                        preferred_element_type=jnp.float32,
                    )
                done += size
        values = flat_t[:, lanes]
        coef = nl_pad[:, lanes]
        drive = jnp.maximum(
            wind_t[:, 0:1] * tables[0:1, lanes] + wind_t[:, 1:2] * tables[1:2, lanes], 0.0
        )
        base = values + WIND_RATE * drive * values
        for mirror in range(2):
            third = members[mirror][:, :LANES]
            fourth = members[mirror][:, LANES:]
            interaction = coef * (
                values * values * (COEF_THREE * third + COEF_FOUR * fourth)
                - 2.0 * COEF_BOTH * values * third * fourth
            )
            base = base - 2.0 * interaction
            for half in range(points // LANES):
                span = slice(half * LANES, (half + 1) * LANES)
                turned = interaction[span].T.astype(jnp.bfloat16)
                for member in range(2):
                    inter[pl.ds(wide + (mirror * 2 + member) * LANES, LANES), span] = turned
        for half in range(points // LANES):
            span = slice(half * LANES, (half + 1) * LANES)
            total[lanes, span] = base[span].T
        return carry

    lax.fori_loop(0, chunks, chunk_step, 0)
    for start in range(0, used, ROWS):
        size = min(ROWS, used - start)
        spaced[start:start + size, :] = jnp.dot(
            matrix[start:start + size, :], inter[...], preferred_element_type=jnp.float32
        )
    for ring in range(rings):
        total[ring * NTH:(ring + 1) * NTH, :] += spaced[ring * RING:ring * RING + NTH, :]
    pack_payload(plan, first_point, total, out, twice)


def pack_payload(plan, first_point, total, out, twice):
    points = total.shape[1]
    main, rest, fold = plan.main, plan.rest, plan.fold
    lane = lax.broadcasted_iota(jnp.int32, (1, LANES), 1)
    for side in range(plan.halves):
        for member in range(plan.members):
            first = side * plan.half_bins + member * plan.per
            valid = min(main, plan.half_bins - member * plan.per)
            slot = (side * plan.members + member) % 2
            for half in range(points // LANES):
                values = total[first:first + valid, half * LANES:(half + 1) * LANES]
                if valid < LANES:
                    values = jnp.concatenate([values, jnp.zeros((LANES - valid, LANES), jnp.float32)], axis=0)
                turned = values.T
                twice[slot, half * LANES:(half + 1) * LANES, :] = turned
                twice[slot, points + half * LANES:points + (half + 1) * LANES, :] = turned
            for part in range(plan.parts):
                owner = (part * plan.members + member) * plan.halves + side
                begin = lax.rem(first_point[part], points)
                out[owner, rest + fold:rest + fold + COMMON, :] = twice[slot, pl.ds(begin, COMMON), :]
                out[owner, rest + 2 * fold + COMMON:rest + 2 * fold + points, :] = twice[
                    slot, pl.ds(begin + COMMON, points - COMMON), :
                ]
                if not rest:
                    continue
                shift = lax.rem(begin, LANES)
                swapped = begin >= LANES
                near = pltpu.roll(total[first + main:first + main + rest, :LANES], lax.rem(LANES - shift, LANES), 1)
                away = pltpu.roll(total[first + main:first + main + rest, LANES:], lax.rem(LANES - shift, LANES), 1)
                keep = (lane < LANES - shift) != swapped
                lead = jnp.where(keep, near, away)
                tail = jnp.where(keep, away, near)
                moved = pltpu.roll(tail, LANES // 2, 1)
                out[owner, :rest, :] = lead
                out[owner, rest:rest + fold, :] = jnp.where(lane < LANES // 2, tail[:fold], moved[rest - fold:])
                out[owner, rest + fold + COMMON:rest + 2 * fold + COMMON, :] = jnp.where(
                    lane < LANES // 2, moved[:fold], tail[rest - fold:]
                )


def source_terms(plan, first_point, spectra, wind, index, weight, nl_coef):
    count_bins, points = spectra.shape
    padded = round_up(count_bins, LANES)
    depth = round_up(count_bins // NTH * RING, LANES)
    cosine, sine, _ = bin_tables(count_bins)
    tables = np.zeros((2, padded), np.float32)
    tables[0, :count_bins] = cosine
    tables[1, :count_bins] = sine
    smem = pl.BlockSpec(memory_space=pltpu.SMEM)
    vmem = pl.BlockSpec(memory_space=pltpu.VMEM)
    operands = (spectra, wind, index, weight, nl_coef, jnp.asarray(tables))
    return pl.pallas_call(
        functools.partial(source_kernel, plan),
        out_shape=jax.ShapeDtypeStruct((plan.group, plan.rows(points), LANES), jnp.float32),
        in_specs=[smem] + [pl.BlockSpec(memory_space=pl.ANY)] * len(operands),
        out_specs=vmem,
        scratch_shapes=[pltpu.VMEM(operand.shape, operand.dtype) for operand in operands] + [
            pltpu.SemaphoreType.DMA((len(operands),)),
            pltpu.VMEM((24, padded), jnp.int32),
            pltpu.VMEM((16, padded), jnp.float32),
            pltpu.VMEM((1, padded), jnp.float32),
            pltpu.VMEM((depth, points), jnp.float32),
            pltpu.VMEM((points, padded), jnp.float32),
            pltpu.VMEM((points, depth), jnp.bfloat16),
            pltpu.VMEM((points, LANES), jnp.float32),
            pltpu.VMEM((depth, 4 * padded), jnp.bfloat16),
            pltpu.VMEM((4 * padded, points), jnp.bfloat16),
            pltpu.VMEM((padded, points), jnp.float32),
            pltpu.VMEM((2, 2 * points, LANES), jnp.float32),
        ],
        compiler_params=pltpu.CompilerParams(vmem_limit_bytes=VMEM_BYTES),
        cost_estimate=pl.CostEstimate(
            flops=4 * depth * 4 * padded * points, bytes_accessed=8 * count_bins * points, transcendentals=0
        ),
        name="source_terms",
    )(first_point, *operands)


def ranks_kernel(plan, sea_total, part, mask, triangle, need, first_point, floor, rel):
    columns, latitudes = mask.shape
    sea = mask[...].astype(jnp.float32).astype(jnp.bfloat16)

    def product(left, right):
        return jnp.dot(left, right, preferred_element_type=jnp.float32)

    upto = product(sea, triangle[...])
    counts = lax.dot_general(
        jnp.ones((8, latitudes), jnp.bfloat16), sea, (((1,), (1,)), ((), ())), preferred_element_type=jnp.float32
    )
    row = lax.broadcasted_iota(jnp.int32, (columns, columns), 0)
    col = lax.broadcasted_iota(jnp.int32, (columns, columns), 1)
    before_row = product(counts.astype(jnp.bfloat16), jnp.where(row < col, 1.0, 0.0).astype(jnp.bfloat16))
    before_col = jnp.sum(product(jnp.where(col < row, 1.0, 0.0).astype(jnp.bfloat16), sea), axis=1, keepdims=True)
    lane = lax.broadcasted_iota(jnp.int32, (1, columns), 1)
    most = 0
    chosen = 0
    for p in range(plan.parts):
        begin = (p * (columns // plan.parts) - plan.halo) % columns
        inside = (lane + (columns - begin)) & (columns - 1)
        start = jnp.sum(jnp.where(lane == begin, before_row[:1], 0.0)).astype(jnp.int32)
        held = jnp.sum(jnp.where(inside < plan.window, counts[:1], 0.0)).astype(jnp.int32)
        wanted = (held + lax.rem(start, plan.group) + plan.group - 1) // plan.group
        first = jnp.where(wanted * plan.group <= sea_total, start // plan.group, 0)
        first_point[p] = first
        most = jnp.maximum(most, wanted)
        chosen = jnp.where(part[0] == p, first, chosen)
    need[0] = most

    def split(before):
        place = before.astype(jnp.int32) - chosen * plan.group
        place = jnp.where(place < 0, place + sea_total, place)
        within = place & (LANES - 1)
        return place - within, within

    floor[...] = split(before_row[:1])[0]
    rel[...] = jnp.where(mask[...] == 1, upto.astype(jnp.int32) - 1 + split(before_col)[1], -1)


def sea_ranks(plan, sea_total, part, mask):
    columns, latitudes = mask.shape
    smem = pl.BlockSpec(memory_space=pltpu.SMEM)
    vmem = pl.BlockSpec(memory_space=pltpu.VMEM)
    return pl.pallas_call(
        functools.partial(ranks_kernel, plan, sea_total),
        out_shape=[
            jax.ShapeDtypeStruct((1,), jnp.int32),
            jax.ShapeDtypeStruct((plan.parts,), jnp.int32),
            jax.ShapeDtypeStruct((1, columns), jnp.int32),
            jax.ShapeDtypeStruct((columns, latitudes), jnp.int32),
        ],
        in_specs=[smem, vmem, vmem],
        out_specs=[smem, smem, vmem, vmem],
        name="sea_ranks",
    )(part, mask, jnp.asarray(np.triu(np.ones((latitudes, latitudes))), jnp.bfloat16))


def propagate_kernel(plan, slots, part, base, got, rel, taps, out, ranked, extra, lined, pick, sea):
    group = got.shape[0]
    columns = plan.window
    all_columns = rel.shape[0]
    begin = part[0] * (all_columns // plan.parts) + (all_columns - plan.halo)
    per, columns_tile, halo = plan.per, plan.columns_tile, plan.halo
    main, rest, fold = plan.main, plan.rest, plan.fold
    half_lanes = lax.broadcasted_iota(jnp.int32, (1, LANES), 1) < LANES // 2
    rest_rows = round_up(rest, 8)

    common = min(slots, COMMON)
    fill = jnp.zeros((LANES - rest, LANES), jnp.float32)

    def turned_rest(owner):
        near = got[owner, rest:rest + fold, :]
        first = near
        second = pltpu.roll(near, LANES // 2, 1)
        if slots > COMMON:
            away = got[owner, rest + fold + COMMON:rest + 2 * fold + COMMON, :]
            first = jnp.where(half_lanes, first, pltpu.roll(away, LANES // 2, 1))
            second = jnp.where(half_lanes, second, away)
        lead = jnp.concatenate([got[owner, :rest, :], fill], axis=0).T
        return lead, jnp.concatenate([first[:rest - fold], second, fill], axis=0).T

    def order(step, carry):
        owners = [step * BATCH + k for k in range(BATCH)]
        turned = [turned_rest(owner) for owner in owners] if rest else []
        for owner in owners:
            ranked[pl.ds(owner, common, stride=group), :] = got[owner, rest + fold:rest + fold + common, :]
            if slots > COMMON:
                ranked[pl.ds(owner + COMMON * group, slots - COMMON, stride=group), :] = got[
                    owner, rest + 2 * fold + COMMON:rest + 2 * fold + slots, :
                ]
        for owner, (lead, tail) in zip(owners, turned):
            extra[pl.ds(owner, LANES, stride=group), :] = lead
            extra[pl.ds(owner + LANES * group, slots - LANES, stride=group), :] = tail[:slots - LANES]
        return carry

    lax.fori_loop(0, group // BATCH, order, 0)

    rank_tiles = ranked.shape[0] // LANES
    padded = lined.shape[0]
    main_rows = round_up(main, 8)

    def line_up(step, carry):
        starts = [pl.multiple_of(step * (2 * LANES) + k * LANES, LANES) for k in range(2)]
        turned = [ranked[pl.ds(start, LANES), :].T[:main_rows] for start in starts]
        more = [extra[pl.ds(start, LANES), :].T[:rest_rows] for start in starts] if rest else []
        for start, values in zip(starts, turned):
            lined[:main_rows, pl.ds(start, LANES)] = values
        for start, values in zip(starts, more):
            lined[main:main + rest_rows, pl.ds(start, LANES)] = values
        return carry

    lax.fori_loop(0, rank_tiles // 2, line_up, 0)
    lined[:, rank_tiles * LANES:] = jnp.zeros((padded, 2 * LANES), jnp.float32)

    for column in range(columns):
        row = jnp.broadcast_to(rel[pl.ds(lax.rem(begin + column, all_columns), 1), :], (8, LANES))
        pick[column] = row
        sea[column] = jnp.where(row >= 0, 1.0, 0.0)

    lane = lax.broadcasted_iota(jnp.int32, (8, LANES), 1)

    def bins_step(first_bin, valid):
        span = pl.ds(first_bin, 8)
        x_taps = [jnp.broadcast_to(taps[span, k:k + 1], (8, LANES)) for k in range(5)]
        y_taps = []
        for k in range(5):
            tap = jnp.broadcast_to(taps[span, 5 + k:6 + k], (8, LANES))
            inside = (lane + (k - 2) >= 0) & (lane + (k - 2) < LANES)
            y_taps.append(jnp.where(inside, tap, 0.0))

        def expanded(column):
            start = pl.multiple_of(base[0, lax.rem(begin + column, all_columns)], LANES)
            chosen = pick[column]
            within = chosen & (LANES - 1)
            low = jnp.take_along_axis(lined[span, pl.ds(start, LANES)], within, axis=1)
            high = jnp.take_along_axis(lined[span, pl.ds(start + LANES, LANES)], within, axis=1)
            return jnp.where(chosen >= LANES, high, low) * sea[column]

        def store(result, column):
            owner, place = divmod(column - halo, columns_tile)
            start = (owner * per + first_bin) * columns_tile + place
            if valid == 8:
                out[pl.ds(start, 8, stride=columns_tile), :] = result
            else:
                for row in range(valid):
                    out[pl.ds(start + row * columns_tile, 1), :] = result[row:row + 1]

        def sweep(values, column):
            value = x_taps[2] * values[2]
            for k in (0, 1, 3, 4):
                value = value + x_taps[k] * values[k]
            value = value * sea[column]
            moved = y_taps[2] * value
            for k in (0, 1, 3, 4):
                moved = moved + y_taps[k] * pltpu.roll(value, (2 - k) % LANES, 1)
            return moved * sea[column]

        reach = halo // STEPS
        first = {}
        middle = {}

        def neighbours(values, column):
            return [values[(column + k) % columns] for k in range(-2, 3)]

        for column in range(columns):
            first[column] = expanded(column)
        for column in range(reach, columns - reach):
            middle[column] = sweep(neighbours(first, column), column)
        results = {}
        for column in range(halo, columns - halo):
            results[column] = sweep(neighbours(middle, column), column)
        for column, result in results.items():
            store(result, column)

    def full_step(tile, carry):
        bins_step(pl.multiple_of(tile * 8, 8), 8)
        return carry

    lax.fori_loop(0, per // 8, full_step, 0)
    if per % 8:
        bins_step(per // 8 * 8, per % 8)


def propagate(plan, slots, part, base, got, rel, taps):
    columns = plan.window
    padded = round_up(plan.per, 8)
    ranks = plan.group * slots
    smem = pl.BlockSpec(memory_space=pltpu.SMEM)
    vmem = pl.BlockSpec(memory_space=pltpu.VMEM)
    return pl.pallas_call(
        functools.partial(propagate_kernel, plan, slots),
        out_shape=jax.ShapeDtypeStruct(((columns - 2 * plan.halo) * plan.per, LANES), jnp.float32),
        in_specs=[smem, smem, vmem, vmem, vmem],
        out_specs=vmem,
        scratch_shapes=[
            pltpu.VMEM((ranks, LANES), jnp.float32),
            pltpu.VMEM((ranks if plan.rest else 8, LANES), jnp.float32),
            pltpu.VMEM((padded, ranks + 2 * LANES), jnp.float32),
            pltpu.VMEM((columns, 8, LANES), jnp.int32),
            pltpu.VMEM((columns, 8, LANES), jnp.float32),
        ],
        compiler_params=pltpu.CompilerParams(vmem_limit_bytes=VMEM_BYTES),
        name="propagate",
    )(part, base, got, rel, taps)


@dataclasses.dataclass(frozen=True)
class Plan:
    tiles: int
    halves: int
    parts: int
    half_bins: int
    columns: int

    @property
    def group(self):
        return self.tiles * self.halves

    @property
    def members(self):
        return self.tiles // self.parts

    @property
    def per(self):
        return -(-self.half_bins // self.members)

    @property
    def main(self):
        return min(self.per, LANES)

    @property
    def rest(self):
        return self.per - self.main

    @property
    def fold(self):
        return -(-self.rest // 2)

    @property
    def columns_tile(self):
        return self.columns // self.tiles

    @property
    def halo(self):
        return 2 * STEPS if self.parts > 1 else 0

    @property
    def window(self):
        return self.columns // self.parts + 2 * self.halo

    def rows(self, slots):
        return self.rest + (2 if slots > COMMON else 1) * self.fold + slots


def shards(spectra, wind, mask, dia_index, dia_weight, nl_coef):
    count_bins, points = spectra.shape
    columns, latitudes = mask.shape
    plan = Plan(
        tiles=lax.axis_size("tile"), halves=lax.axis_size("bin"), parts=2,
        half_bins=count_bins // lax.axis_size("bin"), columns=columns,
    )
    members, parts = plan.members, plan.parts
    sea_total = plan.group * points
    tile_rank = lax.axis_index("tile")

    part = (tile_rank // members).astype(jnp.int32).reshape(1)
    need, first_point, floor, rel = sea_ranks(plan, sea_total, part, mask)
    wanted = need
    bands = lax.axis_size("band")
    for step in range(1, bands):
        wanted = jnp.maximum(
            wanted, lax.ppermute(need, "band", [(band, (band + step) % bands) for band in range(bands)])
        )
    wanted = wanted[0]

    payload = source_terms(plan, first_point, spectra, wind, dia_index, dia_weight, nl_coef)

    cosine, sine, speed = bin_tables(count_bins)
    weights = np.concatenate([stencil(speed * cosine), stencil(speed * sine)])
    table = np.zeros((plan.halves, members, round_up(plan.per, 8), LANES), np.float32)
    for side in range(plan.halves):
        for member in range(members):
            valid = max(0, min(plan.per, plan.half_bins - member * plan.per))
            begin = side * plan.half_bins + member * plan.per
            table[side, member, :valid, :10] = weights[:, begin:begin + valid].T
    taps = lax.dynamic_slice(
        jnp.asarray(table), (lax.axis_index("bin"), tile_rank % members, 0, 0), (1, 1) + table.shape[2:]
    ).reshape(table.shape[2:])

    def with_slots(slots):
        def run(payload, part, floor, rel, taps):
            got = lax.all_to_all(
                payload[:, :plan.rows(slots)], ("tile", "bin"), split_axis=0, concat_axis=0, tiled=True
            )
            return propagate(plan, slots, part, floor, got, rel, taps)

        return run

    sizes = [size for size in SIZES if size < points] + [points]
    choice = sum((wanted > size).astype(jnp.int32) for size in sizes[:-1])
    moved = lax.switch(choice, [with_slots(size) for size in sizes], payload, part, floor, rel, taps)
    result = lax.all_to_all(
        moved.reshape(members, plan.per, plan.columns_tile, latitudes), "tile", split_axis=0, concat_axis=0,
        axis_index_groups=[list(range(p * members, (p + 1) * members)) for p in range(parts)], tiled=True,
    ).reshape(members * plan.per, plan.columns_tile, latitudes)
    return result[:plan.half_bins]


def solution(mesh):
    in_specs = (
        P(None, ("band", "tile", "bin")),
        P(None, ("band", "tile", "bin")),
        P(None, "band"),
        P(),
        P(),
        P(),
    )
    out_specs = P("bin", "tile", "band")
    return jax.shard_map(shards, mesh=mesh, in_specs=in_specs, out_specs=out_specs, check_vma=False)
```

```python
import dataclasses
import functools
import math

import jax
import jax.numpy as jnp
import numpy as np
from jax import lax
from jax.experimental import pallas as pl
from jax.experimental.pallas import tpu as pltpu
from jax.sharding import PartitionSpec as P

NTH = 36
STEPS = 2
LANES = 128
ROWS = 256
RING = 40
COMMON = 192
VMEM_BYTES = 58 * 1024 * 1024
SIZES = (160, 176, 192, 208, 224, 240)
BATCH = 8

LAMBDA = 0.25
COEF_THREE = (1.0 + LAMBDA) ** (-4)
COEF_FOUR = (1.0 - LAMBDA) ** (-4)
COEF_BOTH = (1.0 - LAMBDA * LAMBDA) ** (-4)
CFL_LIMIT = 0.8
WIND_RATE = 0.2


def round_up(value, step):
    return -(-value // step) * step


def bin_tables(count_bins):
    bin_range = np.arange(count_bins)
    theta = 2.0 * math.pi * (bin_range % NTH) / NTH
    group_speed = CFL_LIMIT * 1.1 ** (-(bin_range // NTH).astype(np.float64))
    return np.cos(theta), np.sin(theta), group_speed


def stencil(courant):
    bend = (1.0 - courant * courant) / 6.0
    up = courant >= 0.0
    zero = np.zeros_like(courant)
    left = courant * np.where(up, -bend, zero)
    here = courant * (0.5 + 0.5 * courant + np.where(up, 2.0 * bend, -bend))
    right = courant * (0.5 - 0.5 * courant + np.where(up, -bend, 2.0 * bend))
    far = courant * np.where(up, zero, -bend)
    return np.stack([left, here - left, 1.0 + right - here, far - right, -far])


def source_kernel(plan, first_point, spectra_far, wind_far, index_far, weight_far, nl_far, tables_far, out,
                  spectra, wind, index, weight, nl_coef, tables, arrived, code, weight_pad, nl_pad, spaced, flat_t, low_t, matrix, inter, total, twice):
    count_bins, points = spectra.shape
    padded = flat_t.shape[1]
    chunks = padded // LANES
    rings = count_bins // NTH
    depth = spaced.shape[0]
    whole = count_bins // LANES
    rest = count_bins - whole * LANES
    pairs = [(index_far, index), (weight_far, weight), (nl_far, nl_coef), (wind_far, wind),
             (tables_far, tables), (spectra_far, spectra)]
    copies = [pltpu.make_async_copy(far, near, arrived.at[k]) for k, (far, near) in enumerate(pairs)]
    for copy in copies:
        copy.start()

    code[...] = jnp.zeros(code.shape, jnp.int32)
    weight_pad[...] = jnp.zeros(weight_pad.shape, jnp.float32)
    nl_pad[...] = jnp.zeros(nl_pad.shape, jnp.float32)
    for copy in copies:
        copy.wait()
    nl_pad[:, :count_bins] = nl_coef[...].reshape(1, count_bins)
    for mirror in range(2):
        for member in range(2):
            row = (mirror * 2 + member) * 4
            bins = index[mirror, member]
            ring = ((bins.astype(jnp.float32) + 0.5) * (1.0 / NTH)).astype(jnp.int32)
            lowest = jnp.minimum(jnp.minimum(ring[0:1], ring[1:2]), jnp.minimum(ring[2:3], ring[3:4]))
            direction = bins - ring * NTH
            code[row:row + 4, :count_bins] = jnp.where(ring == lowest, direction, direction + RING)
            code[16 + mirror * 2 + member:17 + mirror * 2 + member, :count_bins] = lowest
            weight_pad[row:row + 4, :count_bins] = weight[mirror, member].astype(jnp.float32)

    gap = jnp.zeros((RING - NTH, points), jnp.float32)
    for ring in range(rings):
        spaced[ring * RING:ring * RING + NTH, :] = spectra[ring * NTH:(ring + 1) * NTH, :]
        spaced[ring * RING + NTH:(ring + 1) * RING, :] = gap
    spaced[rings * RING:, :] = jnp.zeros((depth - rings * RING, points), jnp.float32)
    for half in range(points // LANES):
        span = slice(half * LANES, (half + 1) * LANES)
        for block in range(depth // LANES):
            lanes = slice(block * LANES, (block + 1) * LANES)
            low_t[span, lanes] = spaced[lanes, span].T.astype(jnp.bfloat16)
        for block in range(chunks):
            lanes = slice(block * LANES, (block + 1) * LANES)
            if block < whole:
                values = spectra[lanes, span]
            else:
                values = jnp.concatenate(
                    [spectra[whole * LANES:, span], jnp.zeros((LANES - rest, LANES), jnp.float32)], axis=0
                )
            flat_t[span, lanes] = values.T

    used = rings * RING
    matrix[used:, :] = jnp.zeros((depth - used, matrix.shape[1]), jnp.bfloat16)

    def members_of(chunk):
        lanes = slice(chunk * LANES, (chunk + 1) * LANES)
        wide = chunk * 4 * LANES
        place = lax.broadcasted_iota(jnp.int32, (RING, LANES), 0)
        patterns = []
        for pair in range(4):
            low = jnp.zeros((RING, LANES), jnp.float32)
            high = low
            for corner in range(4):
                r = pair * 4 + corner
                where = code[r:r + 1, lanes]
                amount = jnp.broadcast_to(weight_pad[r:r + 1, lanes], (RING, LANES))
                low = jnp.where(place == where, amount, low)
                high = jnp.where(place + RING == where, amount, high)
            lowest = jnp.broadcast_to(code[16 + pair:17 + pair, lanes], (8, LANES))
            patterns.append((low, high, lowest))
        members = [jnp.zeros((points, 2 * LANES), jnp.float32) for _ in range(2)]
        done = 0
        for ring in range(0, rings, 2):
            for pair in range(4):
                low, high, lowest = patterns[pair]
                parts = []
                for offset in range(2):
                    first = lowest == ring + offset
                    second = lowest == ring + offset - 1
                    for sub in range(0, RING, 8):
                        parts.append(
                            jnp.where(first, low[sub:sub + 8], jnp.where(second, high[sub:sub + 8], 0.0))
                        )
                matrix[ring * RING:(ring + 2) * RING, wide + pair * LANES:wide + (pair + 1) * LANES] = (
                    jnp.concatenate(parts, axis=0).astype(jnp.bfloat16)
                )
            ready = (ring + 2) * RING
            while done < depth and (ready >= done + ROWS or ready == used):
                size = min(ROWS, depth - done)
                for mirror in range(2):
                    members[mirror] = members[mirror] + jnp.dot(
                        low_t[:, done:done + size],
                        matrix[done:done + size, wide + mirror * 2 * LANES:wide + (mirror + 1) * 2 * LANES],
                        preferred_element_type=jnp.float32,
                    )
                done += size
        return members

    def interact(chunk, members):
        lanes = slice(chunk * LANES, (chunk + 1) * LANES)
        wide = chunk * 4 * LANES
        valid = min(LANES, count_bins - chunk * LANES)
        rows = slice(chunk * LANES, chunk * LANES + valid)
        values = flat_t[:, lanes]
        coef = nl_pad[:, lanes]
        turned = []
        for mirror in range(2):
            third = members[mirror][:, :LANES]
            fourth = members[mirror][:, LANES:]
            interaction = coef * (
                values * values * (COEF_THREE * third + COEF_FOUR * fourth)
                - 2.0 * COEF_BOTH * values * third * fourth
            )
            turned.append([interaction[half * LANES:(half + 1) * LANES].T for half in range(points // LANES)])
        for half in range(points // LANES):
            span = slice(half * LANES, (half + 1) * LANES)
            for mirror in range(2):
                low = turned[mirror][half].astype(jnp.bfloat16)
                for member in range(2):
                    start = wide + (mirror * 2 + member) * LANES
                    inter[start:start + LANES, span] = low
            drive = jnp.maximum(
                wind[0:1, span] * tables[0, rows, :] + wind[1:2, span] * tables[1, rows, :], 0.0
            )
            here = spectra[rows, span]
            both = (turned[0][half] + turned[1][half])[:valid]
            total[rows, span] = here + WIND_RATE * drive * here - 2.0 * both

    previous = None
    for chunk in range(chunks):
        members = members_of(chunk)
        if previous is not None:
            interact(chunk - 1, previous)
        previous = members
    interact(chunks - 1, previous)
    added = 0
    packed = 0
    owners = [(side, member) for side in range(plan.halves) for member in range(plan.members)]
    for start in range(0, used, ROWS):
        size = min(ROWS, used - start)
        spaced[start:start + size, :] = jnp.dot(
            matrix[start:start + size, :], inter[...], preferred_element_type=jnp.float32
        )
        while added < rings and added * RING + NTH <= start + size:
            total[added * NTH:(added + 1) * NTH, :] += spaced[added * RING:added * RING + NTH, :]
            added += 1
        while packed < len(owners):
            side, member = owners[packed]
            if min(side * plan.half_bins + (member + 1) * plan.per, count_bins) > added * NTH:
                break
            pack_payload(plan, first_point, total, out, twice, side, member)
            packed += 1


def pack_payload(plan, first_point, total, out, twice, side, member):
    points = total.shape[1]
    main, rest, fold = plan.main, plan.rest, plan.fold
    lane = lax.broadcasted_iota(jnp.int32, (1, LANES), 1)
    first = side * plan.half_bins + member * plan.per
    valid = min(main, plan.half_bins - member * plan.per)
    slot = (side * plan.members + member) % 2
    for half in range(points // LANES):
        values = total[first:first + valid, half * LANES:(half + 1) * LANES]
        if valid < LANES:
            values = jnp.concatenate([values, jnp.zeros((LANES - valid, LANES), jnp.float32)], axis=0)
        turned = values.T
        twice[slot, half * LANES:(half + 1) * LANES, :] = turned
        twice[slot, points + half * LANES:points + (half + 1) * LANES, :] = turned
    for part in range(plan.parts):
        owner = (part * plan.members + member) * plan.halves + side
        begin = lax.rem(first_point[part], points)
        out[owner, rest + fold:rest + fold + COMMON, :] = twice[slot, pl.ds(begin, COMMON), :]
        out[owner, rest + 2 * fold + COMMON:rest + 2 * fold + points, :] = twice[
            slot, pl.ds(begin + COMMON, points - COMMON), :
        ]
        if not rest:
            continue
        shift = lax.rem(begin, LANES)
        swapped = begin >= LANES
        near = pltpu.roll(total[first + main:first + main + rest, :LANES], lax.rem(LANES - shift, LANES), 1)
        away = pltpu.roll(total[first + main:first + main + rest, LANES:], lax.rem(LANES - shift, LANES), 1)
        keep = (lane < LANES - shift) != swapped
        lead = jnp.where(keep, near, away)
        tail = jnp.where(keep, away, near)
        moved = pltpu.roll(tail, LANES // 2, 1)
        out[owner, :rest, :] = lead
        out[owner, rest:rest + fold, :] = jnp.where(lane < LANES // 2, tail[:fold], moved[rest - fold:])
        out[owner, rest + fold + COMMON:rest + 2 * fold + COMMON, :] = jnp.where(
            lane < LANES // 2, moved[:fold], tail[rest - fold:]
        )


def source_terms(plan, first_point, spectra, wind, index, weight, nl_coef):
    count_bins, points = spectra.shape
    padded = round_up(count_bins, LANES)
    depth = round_up(count_bins // NTH * RING, LANES)
    cosine, sine, _ = bin_tables(count_bins)
    tables = np.stack([cosine, sine]).astype(np.float32)[:, :, None] * np.ones((1, 1, LANES), np.float32)
    smem = pl.BlockSpec(memory_space=pltpu.SMEM)
    vmem = pl.BlockSpec(memory_space=pltpu.VMEM)
    operands = (spectra, wind, index, weight, nl_coef, jnp.asarray(tables))
    return pl.pallas_call(
        functools.partial(source_kernel, plan),
        out_shape=jax.ShapeDtypeStruct((plan.group, plan.rows(points), LANES), jnp.float32),
        in_specs=[smem] + [pl.BlockSpec(memory_space=pl.ANY)] * len(operands),
        out_specs=vmem,
        scratch_shapes=[pltpu.VMEM(operand.shape, operand.dtype) for operand in operands] + [
            pltpu.SemaphoreType.DMA((len(operands),)),
            pltpu.VMEM((24, padded), jnp.int32),
            pltpu.VMEM((16, padded), jnp.float32),
            pltpu.VMEM((1, padded), jnp.float32),
            pltpu.VMEM((depth, points), jnp.float32),
            pltpu.VMEM((points, padded), jnp.float32),
            pltpu.VMEM((points, depth), jnp.bfloat16),
            pltpu.VMEM((depth, 4 * padded), jnp.bfloat16),
            pltpu.VMEM((4 * padded, points), jnp.bfloat16),
            pltpu.VMEM((padded, points), jnp.float32),
            pltpu.VMEM((2, 2 * points, LANES), jnp.float32),
        ],
        compiler_params=pltpu.CompilerParams(vmem_limit_bytes=VMEM_BYTES),
        cost_estimate=pl.CostEstimate(
            flops=4 * depth * 4 * padded * points, bytes_accessed=8 * count_bins * points, transcendentals=0
        ),
        name="source_terms",
    )(first_point, *operands)


def ranks_kernel(plan, sea_total, part, mask, triangle, need, first_point, floor, rel):
    columns, latitudes = mask.shape
    sea = mask[...].astype(jnp.float32).astype(jnp.bfloat16)

    def product(left, right):
        return jnp.dot(left, right, preferred_element_type=jnp.float32)

    upto = product(sea, triangle[...])
    counts = lax.dot_general(
        jnp.ones((8, latitudes), jnp.bfloat16), sea, (((1,), (1,)), ((), ())), preferred_element_type=jnp.float32
    )
    row = lax.broadcasted_iota(jnp.int32, (columns, columns), 0)
    col = lax.broadcasted_iota(jnp.int32, (columns, columns), 1)
    before_row = product(counts.astype(jnp.bfloat16), jnp.where(row < col, 1.0, 0.0).astype(jnp.bfloat16))
    before_col = jnp.sum(product(jnp.where(col < row, 1.0, 0.0).astype(jnp.bfloat16), sea), axis=1, keepdims=True)
    lane = lax.broadcasted_iota(jnp.int32, (1, columns), 1)
    most = 0
    chosen = 0
    for p in range(plan.parts):
        begin = (p * (columns // plan.parts) - plan.halo) % columns
        inside = (lane + (columns - begin)) & (columns - 1)
        start = jnp.sum(jnp.where(lane == begin, before_row[:1], 0.0)).astype(jnp.int32)
        held = jnp.sum(jnp.where(inside < plan.window, counts[:1], 0.0)).astype(jnp.int32)
        wanted = (held + lax.rem(start, plan.group) + plan.group - 1) // plan.group
        first = jnp.where(wanted * plan.group <= sea_total, start // plan.group, 0)
        first_point[p] = first
        most = jnp.maximum(most, wanted)
        chosen = jnp.where(part[0] == p, first, chosen)
    need[0] = most

    def split(before):
        place = before.astype(jnp.int32) - chosen * plan.group
        place = jnp.where(place < 0, place + sea_total, place)
        within = place & (LANES - 1)
        return place - within, within

    floor[...] = split(before_row[:1])[0]
    rel[...] = jnp.where(mask[...] == 1, upto.astype(jnp.int32) - 1 + split(before_col)[1], -1)


def sea_ranks(plan, sea_total, part, mask):
    columns, latitudes = mask.shape
    smem = pl.BlockSpec(memory_space=pltpu.SMEM)
    vmem = pl.BlockSpec(memory_space=pltpu.VMEM)
    return pl.pallas_call(
        functools.partial(ranks_kernel, plan, sea_total),
        out_shape=[
            jax.ShapeDtypeStruct((1,), jnp.int32),
            jax.ShapeDtypeStruct((plan.parts,), jnp.int32),
            jax.ShapeDtypeStruct((1, columns), jnp.int32),
            jax.ShapeDtypeStruct((columns, latitudes), jnp.int32),
        ],
        in_specs=[smem, vmem, vmem],
        out_specs=[smem, smem, vmem, vmem],
        name="sea_ranks",
    )(part, mask, jnp.asarray(np.triu(np.ones((latitudes, latitudes))), jnp.bfloat16))


def propagate_kernel(plan, slots, part, base, got, rel, taps, out, ranked, extra, lined, pick, sea, starts):
    group = got.shape[0]
    columns = plan.window
    all_columns = rel.shape[0]
    begin = part[0] * (all_columns // plan.parts) + (all_columns - plan.halo)
    per, columns_tile, halo = plan.per, plan.columns_tile, plan.halo
    main, rest, fold = plan.main, plan.rest, plan.fold
    half_lanes = lax.broadcasted_iota(jnp.int32, (1, LANES), 1) < LANES // 2
    rest_rows = round_up(rest, 8)

    common = min(slots, COMMON)
    fill = jnp.zeros((LANES - rest, LANES), jnp.float32)

    def turned_rest(owner):
        near = got[owner, rest:rest + fold, :]
        first = near
        second = pltpu.roll(near, LANES // 2, 1)
        if slots > COMMON:
            away = got[owner, rest + fold + COMMON:rest + 2 * fold + COMMON, :]
            first = jnp.where(half_lanes, first, pltpu.roll(away, LANES // 2, 1))
            second = jnp.where(half_lanes, second, away)
        lead = jnp.concatenate([got[owner, :rest, :], fill], axis=0).T
        return lead, jnp.concatenate([first[:rest - fold], second, fill], axis=0).T

    def order(step, carry):
        owners = [step * BATCH + k for k in range(BATCH)]
        turned = [turned_rest(owner) for owner in owners] if rest else []
        for owner in owners:
            ranked[pl.ds(owner, common, stride=group), :] = got[owner, rest + fold:rest + fold + common, :]
            if slots > COMMON:
                ranked[pl.ds(owner + COMMON * group, slots - COMMON, stride=group), :] = got[
                    owner, rest + 2 * fold + COMMON:rest + 2 * fold + slots, :
                ]
        for owner, (lead, tail) in zip(owners, turned):
            extra[pl.ds(owner, LANES, stride=group), :] = lead
            extra[pl.ds(owner + LANES * group, slots - LANES, stride=group), :] = tail[:slots - LANES]
        return carry

    lax.fori_loop(0, group // BATCH, order, 0)

    rank_tiles = ranked.shape[0] // LANES
    padded = lined.shape[0]
    main_rows = round_up(main, 8)

    def line_up(step, carry):
        starts = [pl.multiple_of(step * (2 * LANES) + k * LANES, LANES) for k in range(2)]
        turned = [ranked[pl.ds(start, LANES), :].T[:main_rows] for start in starts]
        more = [extra[pl.ds(start, LANES), :].T[:rest_rows] for start in starts] if rest else []
        for start, values in zip(starts, turned):
            lined[:main_rows, pl.ds(start, LANES)] = values
        for start, values in zip(starts, more):
            lined[main:main + rest_rows, pl.ds(start, LANES)] = values
        return carry

    lax.fori_loop(0, rank_tiles // 2, line_up, 0)
    lined[:, rank_tiles * LANES:] = jnp.zeros((padded, 2 * LANES), jnp.float32)

    for column in range(columns):
        source = (begin + column) & (all_columns - 1)
        starts[column] = base[0, source]
        row = jnp.broadcast_to(rel[pl.ds(source, 1), :], (8, LANES))
        pick[column] = row
        sea[column] = jnp.where(row >= 0, 1.0, 0.0)

    lane = lax.broadcasted_iota(jnp.int32, (8, LANES), 1)

    def bins_step(first_bin, valid):
        span = pl.ds(first_bin, 8)
        x_taps = [jnp.broadcast_to(taps[span, k:k + 1], (8, LANES)) for k in range(5)]
        y_taps = []
        for k in range(5):
            tap = jnp.broadcast_to(taps[span, 5 + k:6 + k], (8, LANES))
            inside = (lane + (k - 2) >= 0) & (lane + (k - 2) < LANES)
            y_taps.append(jnp.where(inside, tap, 0.0))

        def expanded(column):
            start = pl.multiple_of(starts[column], LANES)
            chosen = pick[column]
            within = chosen & (LANES - 1)
            low = jnp.take_along_axis(lined[span, pl.ds(start, LANES)], within, axis=1)
            high = jnp.take_along_axis(lined[span, pl.ds(start + LANES, LANES)], within, axis=1)
            return jnp.where(chosen >= LANES, high, low) * sea[column]

        def store(result, column):
            owner, place = divmod(column - halo, columns_tile)
            start = (owner * per + first_bin) * columns_tile + place
            if valid == 8:
                out[pl.ds(start, 8, stride=columns_tile), :] = result
            else:
                for row in range(valid):
                    out[pl.ds(start + row * columns_tile, 1), :] = result[row:row + 1]

        def sweep(values, column):
            value = x_taps[2] * values[2]
            for k in (0, 1, 3, 4):
                value = value + x_taps[k] * values[k]
            value = value * sea[column]
            moved = y_taps[2] * value
            for k in (0, 1, 3, 4):
                moved = moved + y_taps[k] * pltpu.roll(value, (2 - k) % LANES, 1)
            return moved * sea[column]

        reach = halo // STEPS
        first = {}
        middle = {}

        def neighbours(values, column):
            return [values[(column + k) % columns] for k in range(-2, 3)]

        for column in range(columns):
            first[column] = expanded(column)
        for column in range(reach, columns - reach):
            middle[column] = sweep(neighbours(first, column), column)
        results = {}
        for column in range(halo, columns - halo):
            results[column] = sweep(neighbours(middle, column), column)
        for column, result in results.items():
            store(result, column)

    def full_step(tile, carry):
        bins_step(pl.multiple_of(tile * 8, 8), 8)
        return carry

    lax.fori_loop(0, per // 8, full_step, 0)
    if per % 8:
        bins_step(per // 8 * 8, per % 8)


def propagate(plan, slots, part, base, got, rel, taps):
    columns = plan.window
    padded = round_up(plan.per, 8)
    ranks = plan.group * slots
    smem = pl.BlockSpec(memory_space=pltpu.SMEM)
    vmem = pl.BlockSpec(memory_space=pltpu.VMEM)
    return pl.pallas_call(
        functools.partial(propagate_kernel, plan, slots),
        out_shape=jax.ShapeDtypeStruct(((columns - 2 * plan.halo) * plan.per, LANES), jnp.float32),
        in_specs=[smem, smem, vmem, vmem, vmem],
        out_specs=vmem,
        scratch_shapes=[
            pltpu.VMEM((ranks, LANES), jnp.float32),
            pltpu.VMEM((ranks if plan.rest else 8, LANES), jnp.float32),
            pltpu.VMEM((padded, ranks + 2 * LANES), jnp.float32),
            pltpu.VMEM((columns, 8, LANES), jnp.int32),
            pltpu.VMEM((columns, 8, LANES), jnp.float32),
            pltpu.SMEM((columns,), jnp.int32),
        ],
        compiler_params=pltpu.CompilerParams(vmem_limit_bytes=VMEM_BYTES),
        name="propagate",
    )(part, base, got, rel, taps)


@dataclasses.dataclass(frozen=True)
class Plan:
    tiles: int
    halves: int
    parts: int
    half_bins: int
    columns: int

    @property
    def group(self):
        return self.tiles * self.halves

    @property
    def members(self):
        return self.tiles // self.parts

    @property
    def per(self):
        return -(-self.half_bins // self.members)

    @property
    def main(self):
        return min(self.per, LANES)

    @property
    def rest(self):
        return self.per - self.main

    @property
    def fold(self):
        return -(-self.rest // 2)

    @property
    def columns_tile(self):
        return self.columns // self.tiles

    @property
    def halo(self):
        return 2 * STEPS if self.parts > 1 else 0

    @property
    def window(self):
        return self.columns // self.parts + 2 * self.halo

    def rows(self, slots):
        return self.rest + (2 if slots > COMMON else 1) * self.fold + slots


def shards(spectra, wind, mask, dia_index, dia_weight, nl_coef):
    count_bins, points = spectra.shape
    columns, latitudes = mask.shape
    plan = Plan(
        tiles=lax.axis_size("tile"), halves=lax.axis_size("bin"), parts=2,
        half_bins=count_bins // lax.axis_size("bin"), columns=columns,
    )
    members, parts = plan.members, plan.parts
    sea_total = plan.group * points
    tile_rank = lax.axis_index("tile")

    part = (tile_rank // members).astype(jnp.int32).reshape(1)
    need, first_point, floor, rel = sea_ranks(plan, sea_total, part, mask)
    wanted = need
    bands = lax.axis_size("band")
    for step in range(1, bands):
        wanted = jnp.maximum(
            wanted, lax.ppermute(need, "band", [(band, (band + step) % bands) for band in range(bands)])
        )
    wanted = wanted[0]

    payload = source_terms(plan, first_point, spectra, wind, dia_index, dia_weight, nl_coef)

    cosine, sine, speed = bin_tables(count_bins)
    weights = np.concatenate([stencil(speed * cosine), stencil(speed * sine)])
    table = np.zeros((plan.halves, members, round_up(plan.per, 8), LANES), np.float32)
    for side in range(plan.halves):
        for member in range(members):
            valid = max(0, min(plan.per, plan.half_bins - member * plan.per))
            begin = side * plan.half_bins + member * plan.per
            table[side, member, :valid, :10] = weights[:, begin:begin + valid].T
    taps = lax.dynamic_slice(
        jnp.asarray(table), (lax.axis_index("bin"), tile_rank % members, 0, 0), (1, 1) + table.shape[2:]
    ).reshape(table.shape[2:])

    def with_slots(slots):
        def run(payload, part, floor, rel, taps):
            got = lax.all_to_all(
                payload[:, :plan.rows(slots)], ("tile", "bin"), split_axis=0, concat_axis=0, tiled=True
            )
            return propagate(plan, slots, part, floor, got, rel, taps)

        return run

    sizes = [size for size in SIZES if size < points] + [points]
    choice = sum((wanted > size).astype(jnp.int32) for size in sizes[:-1])
    moved = lax.switch(choice, [with_slots(size) for size in sizes], payload, part, floor, rel, taps)
    result = lax.all_to_all(
        moved.reshape(members, plan.per, plan.columns_tile, latitudes), "tile", split_axis=0, concat_axis=0,
        axis_index_groups=[list(range(p * members, (p + 1) * members)) for p in range(parts)], tiled=True,
    ).reshape(members * plan.per, plan.columns_tile, latitudes)
    return result[:plan.half_bins]


def solution(mesh):
    in_specs = (
        P(None, ("band", "tile", "bin")),
        P(None, ("band", "tile", "bin")),
        P(None, "band"),
        P(),
        P(),
        P(),
    )
    out_specs = P("bin", "tile", "band")
    return jax.shard_map(shards, mesh=mesh, in_specs=in_specs, out_specs=out_specs, check_vma=False)
```

```python
import dataclasses
import functools
import math

import jax
import jax.numpy as jnp
import numpy as np
from jax import lax
from jax.experimental import pallas as pl
from jax.experimental.pallas import tpu as pltpu
from jax.sharding import PartitionSpec as P

NTH = 36
STEPS = 2
LANES = 128
ROWS = 256
RING = 40
COMMON = 192
VMEM_BYTES = 58 * 1024 * 1024
SIZES = (160, 176, 192, 208, 224, 240)
BATCH = 8
AWAY = (-2, -1, 1, 2)

LAMBDA = 0.25
COEF_THREE = (1.0 + LAMBDA) ** (-4)
COEF_FOUR = (1.0 - LAMBDA) ** (-4)
COEF_BOTH = (1.0 - LAMBDA * LAMBDA) ** (-4)
CFL_LIMIT = 0.8
WIND_RATE = 0.2


def round_up(value, step):
    return -(-value // step) * step


def bin_tables(count_bins):
    bin_range = np.arange(count_bins)
    theta = 2.0 * math.pi * (bin_range % NTH) / NTH
    group_speed = CFL_LIMIT * 1.1 ** (-(bin_range // NTH).astype(np.float64))
    return np.cos(theta), np.sin(theta), group_speed


def stencil(courant):
    bend = (1.0 - courant * courant) / 6.0
    up = courant >= 0.0
    zero = np.zeros_like(courant)
    left = courant * np.where(up, -bend, zero)
    here = courant * (0.5 + 0.5 * courant + np.where(up, 2.0 * bend, -bend))
    right = courant * (0.5 - 0.5 * courant + np.where(up, -bend, 2.0 * bend))
    far = courant * np.where(up, zero, -bend)
    return np.stack([left, here - left, 1.0 + right - here, far - right, -far])


def source_kernel(plan, first_point, spectra_far, wind_far, index_far, weight_far, nl_far, tables_far, out,
                  spectra, wind, index, weight, nl_coef, tables, arrived, code, weight_pad, nl_pad, spaced, flat_t, low_t, matrix, inter, total, twice):
    count_bins, points = spectra.shape
    padded = flat_t.shape[1]
    chunks = padded // LANES
    rings = count_bins // NTH
    depth = spaced.shape[0]
    whole = count_bins // LANES
    rest = count_bins - whole * LANES
    pairs = [(index_far, index), (weight_far, weight), (nl_far, nl_coef), (wind_far, wind),
             (tables_far, tables), (spectra_far, spectra)]
    copies = [pltpu.make_async_copy(far, near, arrived.at[k]) for k, (far, near) in enumerate(pairs)]
    for copy in copies:
        copy.start()

    code[...] = jnp.zeros(code.shape, jnp.int32)
    weight_pad[...] = jnp.zeros(weight_pad.shape, jnp.float32)
    nl_pad[...] = jnp.zeros(nl_pad.shape, jnp.float32)
    for copy in copies:
        copy.wait()
    nl_pad[:, :count_bins] = nl_coef[...].reshape(1, count_bins)
    for mirror in range(2):
        for member in range(2):
            row = (mirror * 2 + member) * 4
            bins = index[mirror, member]
            ring = ((bins.astype(jnp.float32) + 0.5) * (1.0 / NTH)).astype(jnp.int32)
            lowest = jnp.minimum(jnp.minimum(ring[0:1], ring[1:2]), jnp.minimum(ring[2:3], ring[3:4]))
            direction = bins - ring * NTH
            code[row:row + 4, :count_bins] = jnp.where(ring == lowest, direction, direction + RING)
            code[16 + mirror * 2 + member:17 + mirror * 2 + member, :count_bins] = lowest
            weight_pad[row:row + 4, :count_bins] = weight[mirror, member].astype(jnp.float32)

    gap = jnp.zeros((RING - NTH, points), jnp.float32)
    for ring in range(rings):
        spaced[ring * RING:ring * RING + NTH, :] = spectra[ring * NTH:(ring + 1) * NTH, :]
        spaced[ring * RING + NTH:(ring + 1) * RING, :] = gap
    spaced[rings * RING:, :] = jnp.zeros((depth - rings * RING, points), jnp.float32)
    for half in range(points // LANES):
        span = slice(half * LANES, (half + 1) * LANES)
        for block in range(depth // LANES):
            lanes = slice(block * LANES, (block + 1) * LANES)
            low_t[span, lanes] = spaced[lanes, span].T.astype(jnp.bfloat16)
        for block in range(chunks):
            lanes = slice(block * LANES, (block + 1) * LANES)
            if block < whole:
                values = spectra[lanes, span]
            else:
                values = jnp.concatenate(
                    [spectra[whole * LANES:, span], jnp.zeros((LANES - rest, LANES), jnp.float32)], axis=0
                )
            flat_t[span, lanes] = values.T

    used = rings * RING
    matrix[used:, :] = jnp.zeros((depth - used, matrix.shape[1]), jnp.bfloat16)

    def members_of(chunk):
        lanes = slice(chunk * LANES, (chunk + 1) * LANES)
        wide = chunk * 4 * LANES
        place = lax.broadcasted_iota(jnp.int32, (RING, LANES), 0)
        patterns = []
        for pair in range(4):
            low = jnp.zeros((RING, LANES), jnp.float32)
            high = low
            for corner in range(4):
                r = pair * 4 + corner
                where = code[r:r + 1, lanes]
                amount = jnp.broadcast_to(weight_pad[r:r + 1, lanes], (RING, LANES))
                low = jnp.where(place == where, amount, low)
                high = jnp.where(place + RING == where, amount, high)
            lowest = jnp.broadcast_to(code[16 + pair:17 + pair, lanes], (8, LANES))
            patterns.append((low, high, lowest))
        members = [jnp.zeros((points, 2 * LANES), jnp.float32) for _ in range(2)]
        done = 0
        for ring in range(0, rings, 2):
            for pair in range(4):
                low, high, lowest = patterns[pair]
                parts = []
                for offset in range(2):
                    first = lowest == ring + offset
                    second = lowest == ring + offset - 1
                    for sub in range(0, RING, 8):
                        parts.append(
                            jnp.where(first, low[sub:sub + 8], jnp.where(second, high[sub:sub + 8], 0.0))
                        )
                matrix[ring * RING:(ring + 2) * RING, wide + pair * LANES:wide + (pair + 1) * LANES] = (
                    jnp.concatenate(parts, axis=0).astype(jnp.bfloat16)
                )
            ready = (ring + 2) * RING
            while done < depth and (ready >= done + ROWS or ready == used):
                size = min(ROWS, depth - done)
                for mirror in range(2):
                    members[mirror] = members[mirror] + jnp.dot(
                        low_t[:, done:done + size],
                        matrix[done:done + size, wide + mirror * 2 * LANES:wide + (mirror + 1) * 2 * LANES],
                        preferred_element_type=jnp.float32,
                    )
                done += size
        return members

    def interact(chunk, members):
        lanes = slice(chunk * LANES, (chunk + 1) * LANES)
        wide = chunk * 4 * LANES
        valid = min(LANES, count_bins - chunk * LANES)
        rows = slice(chunk * LANES, chunk * LANES + valid)
        values = flat_t[:, lanes]
        coef = nl_pad[:, lanes]
        turned = []
        for mirror in range(2):
            third = members[mirror][:, :LANES]
            fourth = members[mirror][:, LANES:]
            interaction = coef * (
                values * values * (COEF_THREE * third + COEF_FOUR * fourth)
                - 2.0 * COEF_BOTH * values * third * fourth
            )
            turned.append([interaction[half * LANES:(half + 1) * LANES].T for half in range(points // LANES)])
        for half in range(points // LANES):
            span = slice(half * LANES, (half + 1) * LANES)
            for mirror in range(2):
                low = turned[mirror][half].astype(jnp.bfloat16)
                for member in range(2):
                    start = wide + (mirror * 2 + member) * LANES
                    inter[start:start + LANES, span] = low
            drive = jnp.maximum(
                wind[0:1, span] * tables[0, rows, :] + wind[1:2, span] * tables[1, rows, :], 0.0
            )
            here = spectra[rows, span]
            both = (turned[0][half] + turned[1][half])[:valid]
            total[rows, span] = here + WIND_RATE * drive * here - 2.0 * both

    previous = None
    for chunk in range(chunks):
        members = members_of(chunk)
        if previous is not None:
            interact(chunk - 1, previous)
        previous = members
    interact(chunks - 1, previous)
    added = 0
    packed = 0
    owners = [(side, member) for side in range(plan.halves) for member in range(plan.members)]
    for start in range(0, used, ROWS):
        size = min(ROWS, used - start)
        spaced[start:start + size, :] = jnp.dot(
            matrix[start:start + size, :], inter[...], preferred_element_type=jnp.float32
        )
        while added < rings and added * RING + NTH <= start + size:
            total[added * NTH:(added + 1) * NTH, :] += spaced[added * RING:added * RING + NTH, :]
            added += 1
        while packed < len(owners):
            side, member = owners[packed]
            if min(side * plan.half_bins + (member + 1) * plan.per, count_bins) > added * NTH:
                break
            pack_payload(plan, first_point, total, out, twice, side, member)
            packed += 1


def pack_payload(plan, first_point, total, out, twice, side, member):
    points = total.shape[1]
    main, rest, fold = plan.main, plan.rest, plan.fold
    lane = lax.broadcasted_iota(jnp.int32, (1, LANES), 1)
    first = side * plan.half_bins + member * plan.per
    valid = min(main, plan.half_bins - member * plan.per)
    slot = (side * plan.members + member) % 2
    for half in range(points // LANES):
        values = total[first:first + valid, half * LANES:(half + 1) * LANES]
        if valid < LANES:
            values = jnp.concatenate([values, jnp.zeros((LANES - valid, LANES), jnp.float32)], axis=0)
        turned = values.T
        twice[slot, half * LANES:(half + 1) * LANES, :] = turned
        twice[slot, points + half * LANES:points + (half + 1) * LANES, :] = turned
    for part in range(plan.parts):
        owner = (part * plan.members + member) * plan.halves + side
        begin = lax.rem(first_point[part], points)
        out[owner, rest + fold:rest + fold + COMMON, :] = twice[slot, pl.ds(begin, COMMON), :]
        out[owner, rest + 2 * fold + COMMON:rest + 2 * fold + points, :] = twice[
            slot, pl.ds(begin + COMMON, points - COMMON), :
        ]
        if not rest:
            continue
        shift = lax.rem(begin, LANES)
        swapped = begin >= LANES
        near = pltpu.roll(total[first + main:first + main + rest, :LANES], lax.rem(LANES - shift, LANES), 1)
        away = pltpu.roll(total[first + main:first + main + rest, LANES:], lax.rem(LANES - shift, LANES), 1)
        keep = (lane < LANES - shift) != swapped
        lead = jnp.where(keep, near, away)
        tail = jnp.where(keep, away, near)
        moved = pltpu.roll(tail, LANES // 2, 1)
        out[owner, :rest, :] = lead
        out[owner, rest:rest + fold, :] = jnp.where(lane < LANES // 2, tail[:fold], moved[rest - fold:])
        out[owner, rest + fold + COMMON:rest + 2 * fold + COMMON, :] = jnp.where(
            lane < LANES // 2, moved[:fold], tail[rest - fold:]
        )


def source_terms(plan, first_point, spectra, wind, index, weight, nl_coef):
    count_bins, points = spectra.shape
    padded = round_up(count_bins, LANES)
    depth = round_up(count_bins // NTH * RING, LANES)
    cosine, sine, _ = bin_tables(count_bins)
    tables = np.stack([cosine, sine]).astype(np.float32)[:, :, None] * np.ones((1, 1, LANES), np.float32)
    smem = pl.BlockSpec(memory_space=pltpu.SMEM)
    vmem = pl.BlockSpec(memory_space=pltpu.VMEM)
    operands = (spectra, wind, index, weight, nl_coef, jnp.asarray(tables))
    return pl.pallas_call(
        functools.partial(source_kernel, plan),
        out_shape=jax.ShapeDtypeStruct((plan.group, plan.rows(points), LANES), jnp.float32),
        in_specs=[smem] + [pl.BlockSpec(memory_space=pl.ANY)] * len(operands),
        out_specs=vmem,
        scratch_shapes=[pltpu.VMEM(operand.shape, operand.dtype) for operand in operands] + [
            pltpu.SemaphoreType.DMA((len(operands),)),
            pltpu.VMEM((24, padded), jnp.int32),
            pltpu.VMEM((16, padded), jnp.float32),
            pltpu.VMEM((1, padded), jnp.float32),
            pltpu.VMEM((depth, points), jnp.float32),
            pltpu.VMEM((points, padded), jnp.float32),
            pltpu.VMEM((points, depth), jnp.bfloat16),
            pltpu.VMEM((depth, 4 * padded), jnp.bfloat16),
            pltpu.VMEM((4 * padded, points), jnp.bfloat16),
            pltpu.VMEM((padded, points), jnp.float32),
            pltpu.VMEM((2, 2 * points, LANES), jnp.float32),
        ],
        compiler_params=pltpu.CompilerParams(vmem_limit_bytes=VMEM_BYTES),
        cost_estimate=pl.CostEstimate(
            flops=4 * depth * 4 * padded * points, bytes_accessed=8 * count_bins * points, transcendentals=0
        ),
        name="source_terms",
    )(first_point, *operands)


def ranks_kernel(plan, sea_total, part, mask, triangle, need, first_point, floor, rel):
    columns, latitudes = mask.shape
    sea = mask[...].astype(jnp.float32).astype(jnp.bfloat16)

    def product(left, right):
        return jnp.dot(left, right, preferred_element_type=jnp.float32)

    upto = product(sea, triangle[...])
    counts = lax.dot_general(
        jnp.ones((8, latitudes), jnp.bfloat16), sea, (((1,), (1,)), ((), ())), preferred_element_type=jnp.float32
    )
    row = lax.broadcasted_iota(jnp.int32, (columns, columns), 0)
    col = lax.broadcasted_iota(jnp.int32, (columns, columns), 1)
    before_row = product(counts.astype(jnp.bfloat16), jnp.where(row < col, 1.0, 0.0).astype(jnp.bfloat16))
    before_col = jnp.sum(product(jnp.where(col < row, 1.0, 0.0).astype(jnp.bfloat16), sea), axis=1, keepdims=True)
    lane = lax.broadcasted_iota(jnp.int32, (1, columns), 1)
    most = 0
    chosen = 0
    for p in range(plan.parts):
        begin = (p * (columns // plan.parts) - plan.halo) % columns
        inside = (lane + (columns - begin)) & (columns - 1)
        start = jnp.sum(jnp.where(lane == begin, before_row[:1], 0.0)).astype(jnp.int32)
        held = jnp.sum(jnp.where(inside < plan.window, counts[:1], 0.0)).astype(jnp.int32)
        wanted = (held + lax.rem(start, plan.group) + plan.group - 1) // plan.group
        first = jnp.where(wanted * plan.group <= sea_total, start // plan.group, 0)
        first_point[p] = first
        most = jnp.maximum(most, wanted)
        chosen = jnp.where(part[0] == p, first, chosen)
    need[0] = most

    def split(before):
        place = before.astype(jnp.int32) - chosen * plan.group
        place = jnp.where(place < 0, place + sea_total, place)
        within = place & (LANES - 1)
        return place - within, within

    floor[...] = split(before_row[:1])[0]
    rel[...] = jnp.where(mask[...] == 1, upto.astype(jnp.int32) - 1 + split(before_col)[1], -1)


def sea_ranks(plan, sea_total, part, mask):
    columns, latitudes = mask.shape
    smem = pl.BlockSpec(memory_space=pltpu.SMEM)
    vmem = pl.BlockSpec(memory_space=pltpu.VMEM)
    return pl.pallas_call(
        functools.partial(ranks_kernel, plan, sea_total),
        out_shape=[
            jax.ShapeDtypeStruct((1,), jnp.int32),
            jax.ShapeDtypeStruct((plan.parts,), jnp.int32),
            jax.ShapeDtypeStruct((1, columns), jnp.int32),
            jax.ShapeDtypeStruct((columns, latitudes), jnp.int32),
        ],
        in_specs=[smem, vmem, vmem],
        out_specs=[smem, smem, vmem, vmem],
        name="sea_ranks",
    )(part, mask, jnp.asarray(np.triu(np.ones((latitudes, latitudes))), jnp.bfloat16))


def propagate_kernel(plan, slots, part, base, got, rel, taps, out, ranked, extra, lined, pick, sea, starts, shifts):
    group = got.shape[0]
    columns = plan.window
    all_columns = rel.shape[0]
    begin = part[0] * (all_columns // plan.parts) + (all_columns - plan.halo)
    per, columns_tile, halo = plan.per, plan.columns_tile, plan.halo
    main, rest, fold = plan.main, plan.rest, plan.fold
    half_lanes = lax.broadcasted_iota(jnp.int32, (1, LANES), 1) < LANES // 2
    rest_rows = round_up(rest, 8)

    common = min(slots, COMMON)
    fill = jnp.zeros((LANES // 2 - rest, LANES), jnp.float32)

    def turned_rest(owner):
        near = got[owner, rest:rest + fold, :]
        first = near
        second = pltpu.roll(near, LANES // 2, 1)
        if slots > COMMON:
            away = got[owner, rest + fold + COMMON:rest + 2 * fold + COMMON, :]
            first = jnp.where(half_lanes, first, pltpu.roll(away, LANES // 2, 1))
            second = jnp.where(half_lanes, second, away)
        return jnp.concatenate([got[owner, :rest, :], fill, first[:rest - fold], second, fill], axis=0).T

    def order(step, carry):
        owners = [step * BATCH + k for k in range(BATCH)]
        turned = [turned_rest(owner) for owner in owners] if rest else []
        for owner in owners:
            ranked[pl.ds(owner, common, stride=group), :] = got[owner, rest + fold:rest + fold + common, :]
            if slots > COMMON:
                ranked[pl.ds(owner + COMMON * group, slots - COMMON, stride=group), :] = got[
                    owner, rest + 2 * fold + COMMON:rest + 2 * fold + slots, :
                ]
        for owner, values in zip(owners, turned):
            extra[pl.ds(owner, LANES, stride=group), :] = values
        return carry

    lax.fori_loop(0, group // BATCH, order, 0)

    rank_tiles = ranked.shape[0] // LANES
    padded = lined.shape[0]
    main_rows = round_up(main, 8)

    def line_up(step, carry):
        starts = [pl.multiple_of(step * (2 * LANES) + k * LANES, LANES) for k in range(2)]
        turned = [ranked[pl.ds(start, LANES), :].T[:main_rows] for start in starts]
        for start, values in zip(starts, turned):
            lined[:main_rows, pl.ds(start, LANES)] = values
            if not rest and main % 8:
                lined[main_rows - 8:main_rows, pl.ds(start, LANES)] = values[main - 8:main]
        return carry

    lax.fori_loop(0, rank_tiles // 2, line_up, 0)

    def line_up_rest(both, step, carry):
        starts = [pl.multiple_of(step * (2 * LANES) + k * LANES, LANES) for k in range(2)]
        turned = [extra[pl.ds(start, LANES), :].T for start in starts]
        for start, values in zip(starts, turned):
            for half in range(2 if both else 1):
                lanes = pl.ds(start + half * group * LANES, LANES)
                lined[main:main + rest_rows - 8, lanes] = values[half * LANES // 2:half * LANES // 2 + rest_rows - 8]
                lined[main + rest_rows - 8:main + rest_rows, lanes] = values[
                    half * LANES // 2 + rest - 8:half * LANES // 2 + rest
                ]
        return carry

    if rest:
        second = (rank_tiles - group) // 2
        lax.fori_loop(0, second, functools.partial(line_up_rest, True), 0)
        lax.fori_loop(second, group // 2, functools.partial(line_up_rest, False), 0)
    lined[:, rank_tiles * LANES:] = jnp.zeros((padded, 2 * LANES), jnp.float32)

    for column in range(columns):
        source = (begin + column) & (all_columns - 1)
        starts[column] = base[0, source]
        row = jnp.broadcast_to(rel[pl.ds(source, 1), :], (8, LANES))
        pick[column] = row
        sea[column] = jnp.where(row >= 0, 1.0, 0.0)

    row = lax.broadcasted_iota(jnp.int32, (LANES, LANES), 0)
    col = lax.broadcasted_iota(jnp.int32, (LANES, LANES), 1)
    for k, offset in enumerate(AWAY):
        step = jnp.where(row == col + offset, 1.0, 0.0).astype(jnp.bfloat16)
        for part_of in range(2):
            shifts[part_of * LANES:(part_of + 1) * LANES, k * LANES:(k + 1) * LANES] = step

    def bins_step(tile, carry):
        span = pl.ds(pl.multiple_of(tile * 8, 8), 8)
        first_bin = jnp.minimum(tile * 8, per - 8)
        x_taps = [jnp.broadcast_to(taps[span, k:k + 1], (8, LANES)) for k in range(5)]
        y_taps = [jnp.broadcast_to(taps[span, 5 + k:6 + k], (8, LANES)) for k in range(5)]

        def expanded(column):
            start = pl.multiple_of(starts[column], LANES)
            chosen = pick[column]
            within = chosen & (LANES - 1)
            low = jnp.take_along_axis(lined[span, pl.ds(start, LANES)], within, axis=1)
            high = jnp.take_along_axis(lined[span, pl.ds(start + LANES, LANES)], within, axis=1)
            return jnp.where(chosen >= LANES, high, low) * sea[column]

        def store(result, column):
            owner, place = divmod(column - halo, columns_tile)
            start = (owner * per + first_bin) * columns_tile + place
            out[pl.ds(start, 8, stride=columns_tile), :] = result

        def sweep(values, wanted):
            along = {}
            for column in wanted:
                near = neighbours(values, column)
                value = x_taps[2] * near[2]
                for k in (0, 1, 3, 4):
                    value = value + x_taps[k] * near[k]
                along[column] = value * sea[column]
            stacked = jnp.concatenate([along[column] for column in wanted], axis=0)
            high = stacked.astype(jnp.bfloat16)
            low = (stacked - high.astype(jnp.float32)).astype(jnp.bfloat16)
            moved = jnp.dot(
                jnp.concatenate([high, low], axis=1), shifts[...], preferred_element_type=jnp.float32
            )
            swept = {}
            for place, column in enumerate(wanted):
                value = y_taps[2] * along[column]
                for k, offset in enumerate(AWAY):
                    value = value + y_taps[2 + offset] * moved[place * 8:(place + 1) * 8, k * LANES:(k + 1) * LANES]
                swept[column] = value * sea[column]
            return swept

        reach = halo // STEPS
        first = {}

        def neighbours(values, column):
            return [values[(column + k) % columns] for k in range(-2, 3)]

        for column in range(columns):
            first[column] = expanded(column)
        middle = sweep(first, range(reach, columns - reach))
        for column, result in sweep(middle, range(halo, columns - halo)).items():
            store(result, column)
        return carry

    lax.fori_loop(0, -(-per // 8), bins_step, 0)


def propagate(plan, slots, part, base, got, rel, taps):
    columns = plan.window
    padded = round_up(plan.per, 8)
    ranks = plan.group * slots
    smem = pl.BlockSpec(memory_space=pltpu.SMEM)
    vmem = pl.BlockSpec(memory_space=pltpu.VMEM)
    return pl.pallas_call(
        functools.partial(propagate_kernel, plan, slots),
        out_shape=jax.ShapeDtypeStruct(((columns - 2 * plan.halo) * plan.per, LANES), jnp.float32),
        in_specs=[smem, smem, vmem, vmem, vmem],
        out_specs=vmem,
        scratch_shapes=[
            pltpu.VMEM((ranks, LANES), jnp.float32),
            pltpu.VMEM((LANES * plan.group if plan.rest else 8, LANES), jnp.float32),
            pltpu.VMEM((padded, ranks + 2 * LANES), jnp.float32),
            pltpu.VMEM((columns, 8, LANES), jnp.int32),
            pltpu.VMEM((columns, 8, LANES), jnp.float32),
            pltpu.SMEM((columns,), jnp.int32),
            pltpu.VMEM((2 * LANES, len(AWAY) * LANES), jnp.bfloat16),
        ],
        compiler_params=pltpu.CompilerParams(vmem_limit_bytes=VMEM_BYTES),
        name="propagate",
    )(part, base, got, rel, taps)


@dataclasses.dataclass(frozen=True)
class Plan:
    tiles: int
    halves: int
    parts: int
    half_bins: int
    columns: int

    @property
    def group(self):
        return self.tiles * self.halves

    @property
    def members(self):
        return self.tiles // self.parts

    @property
    def per(self):
        return -(-self.half_bins // self.members)

    @property
    def main(self):
        return min(self.per, LANES)

    @property
    def rest(self):
        return self.per - self.main

    @property
    def fold(self):
        return -(-self.rest // 2)

    @property
    def columns_tile(self):
        return self.columns // self.tiles

    @property
    def halo(self):
        return 2 * STEPS if self.parts > 1 else 0

    @property
    def window(self):
        return self.columns // self.parts + 2 * self.halo

    def rows(self, slots):
        return self.rest + (2 if slots > COMMON else 1) * self.fold + slots


def shards(spectra, wind, mask, dia_index, dia_weight, nl_coef):
    count_bins, points = spectra.shape
    columns, latitudes = mask.shape
    plan = Plan(
        tiles=lax.axis_size("tile"), halves=lax.axis_size("bin"), parts=2,
        half_bins=count_bins // lax.axis_size("bin"), columns=columns,
    )
    members, parts = plan.members, plan.parts
    sea_total = plan.group * points
    tile_rank = lax.axis_index("tile")

    part = (tile_rank // members).astype(jnp.int32).reshape(1)
    need, first_point, floor, rel = sea_ranks(plan, sea_total, part, mask)
    wanted = need
    bands = lax.axis_size("band")
    for step in range(1, bands):
        wanted = jnp.maximum(
            wanted, lax.ppermute(need, "band", [(band, (band + step) % bands) for band in range(bands)])
        )
    wanted = wanted[0]

    payload = source_terms(plan, first_point, spectra, wind, dia_index, dia_weight, nl_coef)

    cosine, sine, speed = bin_tables(count_bins)
    weights = np.concatenate([stencil(speed * cosine), stencil(speed * sine)])
    table = np.zeros((plan.halves, members, round_up(plan.per, 8), LANES), np.float32)
    for side in range(plan.halves):
        for member in range(members):
            valid = max(0, min(plan.per, plan.half_bins - member * plan.per))
            begin = side * plan.half_bins + member * plan.per
            table[side, member, :valid, :10] = weights[:, begin:begin + valid].T
            if plan.per % 8:
                table[side, member, -8:] = table[side, member, plan.per - 8:plan.per].copy()
    taps = lax.dynamic_slice(
        jnp.asarray(table), (lax.axis_index("bin"), tile_rank % members, 0, 0), (1, 1) + table.shape[2:]
    ).reshape(table.shape[2:])

    def with_slots(slots):
        def run(payload, part, floor, rel, taps):
            got = lax.all_to_all(
                payload[:, :plan.rows(slots)], ("tile", "bin"), split_axis=0, concat_axis=0, tiled=True
            )
            moved = propagate(plan, slots, part, floor, got, rel, taps)
            result = lax.all_to_all(
                moved.reshape(members, plan.per, plan.columns_tile, latitudes), "tile", split_axis=0, concat_axis=0,
                axis_index_groups=[list(range(p * members, (p + 1) * members)) for p in range(parts)], tiled=True,
            ).reshape(members * plan.per, plan.columns_tile, latitudes)
            return result[:plan.half_bins]

        return run

    sizes = [size for size in SIZES if size < points] + [points]
    choice = sum((wanted > size).astype(jnp.int32) for size in sizes[:-1])
    return lax.switch(choice, [with_slots(size) for size in sizes], payload, part, floor, rel, taps)


def solution(mesh):
    in_specs = (
        P(None, ("band", "tile", "bin")),
        P(None, ("band", "tile", "bin")),
        P(None, "band"),
        P(),
        P(),
        P(),
    )
    out_specs = P("bin", "tile", "band")
    return jax.shard_map(shards, mesh=mesh, in_specs=in_specs, out_specs=out_specs, check_vma=False)
```

```python
import dataclasses
import functools
import math

import jax
import jax.numpy as jnp
import numpy as np
from jax import lax
from jax.experimental import pallas as pl
from jax.experimental.pallas import tpu as pltpu
from jax.sharding import PartitionSpec as P

NTH = 36
STEPS = 2
LANES = 128
ROWS = 256
RING = 40
COMMON = 192
VMEM_BYTES = 58 * 1024 * 1024
SIZES = (160, 176, 192, 208, 224, 240)
BATCH = 8

LAMBDA = 0.25
COEF_THREE = (1.0 + LAMBDA) ** (-4)
COEF_FOUR = (1.0 - LAMBDA) ** (-4)
COEF_BOTH = (1.0 - LAMBDA * LAMBDA) ** (-4)
CFL_LIMIT = 0.8
WIND_RATE = 0.2


def round_up(value, step):
    return -(-value // step) * step


def bin_tables(count_bins):
    bin_range = np.arange(count_bins)
    theta = 2.0 * math.pi * (bin_range % NTH) / NTH
    group_speed = CFL_LIMIT * 1.1 ** (-(bin_range // NTH).astype(np.float64))
    return np.cos(theta), np.sin(theta), group_speed


def stencil(courant):
    bend = (1.0 - courant * courant) / 6.0
    up = courant >= 0.0
    zero = np.zeros_like(courant)
    left = courant * np.where(up, -bend, zero)
    here = courant * (0.5 + 0.5 * courant + np.where(up, 2.0 * bend, -bend))
    right = courant * (0.5 - 0.5 * courant + np.where(up, -bend, 2.0 * bend))
    far = courant * np.where(up, zero, -bend)
    return np.stack([left, here - left, 1.0 + right - here, far - right, -far])


def source_kernel(plan, first_point, spectra_far, wind_far, index_far, weight_far, nl_far, tables_far, out,
                  spectra, wind, index, weight, nl_coef, tables, arrived, code, weight_pad, nl_pad, spaced, flat_t, low_t, matrix, inter, total, twice):
    count_bins, points = spectra.shape
    padded = flat_t.shape[1]
    chunks = padded // LANES
    rings = count_bins // NTH
    depth = spaced.shape[0]
    whole = count_bins // LANES
    rest = count_bins - whole * LANES
    pairs = [(index_far, index), (weight_far, weight), (nl_far, nl_coef), (wind_far, wind),
             (tables_far, tables), (spectra_far, spectra)]
    copies = [pltpu.make_async_copy(far, near, arrived.at[k]) for k, (far, near) in enumerate(pairs)]
    for copy in copies:
        copy.start()

    code[...] = jnp.zeros(code.shape, jnp.int32)
    weight_pad[...] = jnp.zeros(weight_pad.shape, jnp.float32)
    nl_pad[...] = jnp.zeros(nl_pad.shape, jnp.float32)
    for copy in copies:
        copy.wait()
    nl_pad[:, :count_bins] = nl_coef[...].reshape(1, count_bins)
    for mirror in range(2):
        for member in range(2):
            row = (mirror * 2 + member) * 4
            bins = index[mirror, member]
            ring = ((bins.astype(jnp.float32) + 0.5) * (1.0 / NTH)).astype(jnp.int32)
            lowest = jnp.minimum(jnp.minimum(ring[0:1], ring[1:2]), jnp.minimum(ring[2:3], ring[3:4]))
            direction = bins - ring * NTH
            code[row:row + 4, :count_bins] = jnp.where(ring == lowest, direction, direction + RING)
            code[16 + mirror * 2 + member:17 + mirror * 2 + member, :count_bins] = lowest
            weight_pad[row:row + 4, :count_bins] = weight[mirror, member].astype(jnp.float32)

    gap = jnp.zeros((RING - NTH, points), jnp.float32)
    for ring in range(rings):
        spaced[ring * RING:ring * RING + NTH, :] = spectra[ring * NTH:(ring + 1) * NTH, :]
        spaced[ring * RING + NTH:(ring + 1) * RING, :] = gap
    spaced[rings * RING:, :] = jnp.zeros((depth - rings * RING, points), jnp.float32)
    for half in range(points // LANES):
        span = slice(half * LANES, (half + 1) * LANES)
        for block in range(depth // LANES):
            lanes = slice(block * LANES, (block + 1) * LANES)
            low_t[span, lanes] = spaced[lanes, span].T.astype(jnp.bfloat16)
        for block in range(chunks):
            lanes = slice(block * LANES, (block + 1) * LANES)
            if block < whole:
                values = spectra[lanes, span]
            else:
                values = jnp.concatenate(
                    [spectra[whole * LANES:, span], jnp.zeros((LANES - rest, LANES), jnp.float32)], axis=0
                )
            flat_t[span, lanes] = values.T

    used = rings * RING
    matrix[used:, :] = jnp.zeros((depth - used, matrix.shape[1]), jnp.bfloat16)

    def members_of(chunk):
        lanes = slice(chunk * LANES, (chunk + 1) * LANES)
        wide = chunk * 4 * LANES
        place = lax.broadcasted_iota(jnp.int32, (RING, LANES), 0)
        patterns = []
        for pair in range(4):
            low = jnp.zeros((RING, LANES), jnp.float32)
            high = low
            for corner in range(4):
                r = pair * 4 + corner
                where = code[r:r + 1, lanes]
                amount = jnp.broadcast_to(weight_pad[r:r + 1, lanes], (RING, LANES))
                low = jnp.where(place == where, amount, low)
                high = jnp.where(place + RING == where, amount, high)
            lowest = jnp.broadcast_to(code[16 + pair:17 + pair, lanes], (8, LANES))
            patterns.append((low, high, lowest))
        members = [jnp.zeros((points, 2 * LANES), jnp.float32) for _ in range(2)]
        done = 0
        for ring in range(0, rings, 2):
            for pair in range(4):
                low, high, lowest = patterns[pair]
                parts = []
                for offset in range(2):
                    first = lowest == ring + offset
                    second = lowest == ring + offset - 1
                    for sub in range(0, RING, 8):
                        parts.append(
                            jnp.where(first, low[sub:sub + 8], jnp.where(second, high[sub:sub + 8], 0.0))
                        )
                matrix[ring * RING:(ring + 2) * RING, wide + pair * LANES:wide + (pair + 1) * LANES] = (
                    jnp.concatenate(parts, axis=0).astype(jnp.bfloat16)
                )
            ready = (ring + 2) * RING
            while done < depth and (ready >= done + ROWS or ready == used):
                size = min(ROWS, depth - done)
                for mirror in range(2):
                    members[mirror] = members[mirror] + jnp.dot(
                        low_t[:, done:done + size],
                        matrix[done:done + size, wide + mirror * 2 * LANES:wide + (mirror + 1) * 2 * LANES],
                        preferred_element_type=jnp.float32,
                    )
                done += size
        return members

    def interact(chunk, members):
        lanes = slice(chunk * LANES, (chunk + 1) * LANES)
        wide = chunk * 4 * LANES
        valid = min(LANES, count_bins - chunk * LANES)
        rows = slice(chunk * LANES, chunk * LANES + valid)
        values = flat_t[:, lanes]
        coef = nl_pad[:, lanes]
        turned = []
        for mirror in range(2):
            third = members[mirror][:, :LANES]
            fourth = members[mirror][:, LANES:]
            interaction = coef * (
                values * values * (COEF_THREE * third + COEF_FOUR * fourth)
                - 2.0 * COEF_BOTH * values * third * fourth
            )
            turned.append([interaction[half * LANES:(half + 1) * LANES].T for half in range(points // LANES)])
        for half in range(points // LANES):
            span = slice(half * LANES, (half + 1) * LANES)
            for mirror in range(2):
                low = turned[mirror][half].astype(jnp.bfloat16)
                for member in range(2):
                    start = wide + (mirror * 2 + member) * LANES
                    inter[start:start + LANES, span] = low
            drive = jnp.maximum(
                wind[0:1, span] * tables[0, rows, :] + wind[1:2, span] * tables[1, rows, :], 0.0
            )
            here = spectra[rows, span]
            both = (turned[0][half] + turned[1][half])[:valid]
            total[rows, span] = here + WIND_RATE * drive * here - 2.0 * both

    previous = None
    for chunk in range(chunks):
        members = members_of(chunk)
        if previous is not None:
            interact(chunk - 1, previous)
        previous = members
    interact(chunks - 1, previous)
    added = 0
    packed = 0
    owners = [(side, member) for side in range(plan.halves) for member in range(plan.members)]
    for start in range(0, used, ROWS):
        size = min(ROWS, used - start)
        spaced[start:start + size, :] = jnp.dot(
            matrix[start:start + size, :], inter[...], preferred_element_type=jnp.float32
        )
        while added < rings and added * RING + NTH <= start + size:
            total[added * NTH:(added + 1) * NTH, :] += spaced[added * RING:added * RING + NTH, :]
            added += 1
        while packed < len(owners):
            side, member = owners[packed]
            if min(side * plan.half_bins + (member + 1) * plan.per, count_bins) > added * NTH:
                break
            pack_payload(plan, first_point, total, out, twice, side, member)
            packed += 1


def pack_payload(plan, first_point, total, out, twice, side, member):
    points = total.shape[1]
    main, rest, fold = plan.main, plan.rest, plan.fold
    lane = lax.broadcasted_iota(jnp.int32, (1, LANES), 1)
    first = side * plan.half_bins + member * plan.per
    valid = min(main, plan.half_bins - member * plan.per)
    slot = (side * plan.members + member) % 2
    for half in range(points // LANES):
        values = total[first:first + valid, half * LANES:(half + 1) * LANES]
        if valid < LANES:
            values = jnp.concatenate([values, jnp.zeros((LANES - valid, LANES), jnp.float32)], axis=0)
        turned = values.T
        twice[slot, half * LANES:(half + 1) * LANES, :] = turned
        twice[slot, points + half * LANES:points + (half + 1) * LANES, :] = turned
    for part in range(plan.parts):
        owner = (part * plan.members + member) * plan.halves + side
        begin = lax.rem(first_point[part], points)
        out[owner, rest + fold:rest + fold + COMMON, :] = twice[slot, pl.ds(begin, COMMON), :]
        out[owner, rest + 2 * fold + COMMON:rest + 2 * fold + points, :] = twice[
            slot, pl.ds(begin + COMMON, points - COMMON), :
        ]
        if not rest:
            continue
        shift = lax.rem(begin, LANES)
        swapped = begin >= LANES
        near = pltpu.roll(total[first + main:first + main + rest, :LANES], lax.rem(LANES - shift, LANES), 1)
        away = pltpu.roll(total[first + main:first + main + rest, LANES:], lax.rem(LANES - shift, LANES), 1)
        keep = (lane < LANES - shift) != swapped
        lead = jnp.where(keep, near, away)
        tail = jnp.where(keep, away, near)
        moved = pltpu.roll(tail, LANES // 2, 1)
        out[owner, :rest, :] = lead
        out[owner, rest:rest + fold, :] = jnp.where(lane < LANES // 2, tail[:fold], moved[rest - fold:])
        out[owner, rest + fold + COMMON:rest + 2 * fold + COMMON, :] = jnp.where(
            lane < LANES // 2, moved[:fold], tail[rest - fold:]
        )


def source_terms(plan, first_point, spectra, wind, index, weight, nl_coef):
    count_bins, points = spectra.shape
    padded = round_up(count_bins, LANES)
    depth = round_up(count_bins // NTH * RING, LANES)
    cosine, sine, _ = bin_tables(count_bins)
    tables = np.stack([cosine, sine]).astype(np.float32)[:, :, None] * np.ones((1, 1, LANES), np.float32)
    smem = pl.BlockSpec(memory_space=pltpu.SMEM)
    vmem = pl.BlockSpec(memory_space=pltpu.VMEM)
    operands = (spectra, wind, index, weight, nl_coef, jnp.asarray(tables))
    return pl.pallas_call(
        functools.partial(source_kernel, plan),
        out_shape=jax.ShapeDtypeStruct((plan.group, plan.rows(points), LANES), jnp.float32),
        in_specs=[smem] + [pl.BlockSpec(memory_space=pl.ANY)] * len(operands),
        out_specs=vmem,
        scratch_shapes=[pltpu.VMEM(operand.shape, operand.dtype) for operand in operands] + [
            pltpu.SemaphoreType.DMA((len(operands),)),
            pltpu.VMEM((24, padded), jnp.int32),
            pltpu.VMEM((16, padded), jnp.float32),
            pltpu.VMEM((1, padded), jnp.float32),
            pltpu.VMEM((depth, points), jnp.float32),
            pltpu.VMEM((points, padded), jnp.float32),
            pltpu.VMEM((points, depth), jnp.bfloat16),
            pltpu.VMEM((depth, 4 * padded), jnp.bfloat16),
            pltpu.VMEM((4 * padded, points), jnp.bfloat16),
            pltpu.VMEM((padded, points), jnp.float32),
            pltpu.VMEM((2, 2 * points, LANES), jnp.float32),
        ],
        compiler_params=pltpu.CompilerParams(vmem_limit_bytes=VMEM_BYTES),
        cost_estimate=pl.CostEstimate(
            flops=4 * depth * 4 * padded * points, bytes_accessed=8 * count_bins * points, transcendentals=0
        ),
        name="source_terms",
    )(first_point, *operands)


def ranks_kernel(plan, sea_total, part, mask, triangle, need, first_point, floor, rel):
    columns, latitudes = mask.shape
    sea = mask[...].astype(jnp.float32).astype(jnp.bfloat16)

    def product(left, right):
        return jnp.dot(left, right, preferred_element_type=jnp.float32)

    upto = product(sea, triangle[...])
    counts = lax.dot_general(
        jnp.ones((8, latitudes), jnp.bfloat16), sea, (((1,), (1,)), ((), ())), preferred_element_type=jnp.float32
    )
    row = lax.broadcasted_iota(jnp.int32, (columns, columns), 0)
    col = lax.broadcasted_iota(jnp.int32, (columns, columns), 1)
    before_row = product(counts.astype(jnp.bfloat16), jnp.where(row < col, 1.0, 0.0).astype(jnp.bfloat16))
    before_col = jnp.sum(product(jnp.where(col < row, 1.0, 0.0).astype(jnp.bfloat16), sea), axis=1, keepdims=True)
    lane = lax.broadcasted_iota(jnp.int32, (1, columns), 1)
    most = 0
    chosen = 0
    for p in range(plan.parts):
        begin = (p * (columns // plan.parts) - plan.halo) % columns
        inside = (lane + (columns - begin)) & (columns - 1)
        start = jnp.sum(jnp.where(lane == begin, before_row[:1], 0.0)).astype(jnp.int32)
        held = jnp.sum(jnp.where(inside < plan.window, counts[:1], 0.0)).astype(jnp.int32)
        wanted = (held + lax.rem(start, plan.group) + plan.group - 1) // plan.group
        first = jnp.where(wanted * plan.group <= sea_total, start // plan.group, 0)
        first_point[p] = first
        most = jnp.maximum(most, wanted)
        chosen = jnp.where(part[0] == p, first, chosen)
    need[0] = most

    def placed(before):
        place = before.astype(jnp.int32) - chosen * plan.group
        place = jnp.where(place < 0, place + sea_total, place)
        return place

    floor[...] = placed(before_row[:1])
    rel[...] = jnp.where(mask[...] == 1, upto.astype(jnp.int32) - 1 + placed(before_col), -1)


def sea_ranks(plan, sea_total, part, mask):
    columns, latitudes = mask.shape
    smem = pl.BlockSpec(memory_space=pltpu.SMEM)
    vmem = pl.BlockSpec(memory_space=pltpu.VMEM)
    return pl.pallas_call(
        functools.partial(ranks_kernel, plan, sea_total),
        out_shape=[
            jax.ShapeDtypeStruct((1,), jnp.int32),
            jax.ShapeDtypeStruct((plan.parts,), jnp.int32),
            jax.ShapeDtypeStruct((1, columns), jnp.int32),
            jax.ShapeDtypeStruct((columns, latitudes), jnp.int32),
        ],
        in_specs=[smem, vmem, vmem],
        out_specs=[smem, smem, vmem, vmem],
        name="sea_ranks",
    )(part, mask, jnp.asarray(np.triu(np.ones((latitudes, latitudes))), jnp.bfloat16))


def propagate_kernel(plan, slots, part, base, got, rel, taps, out, ranked, extra, lined, pick, sea, starts):
    group = got.shape[0]
    columns = plan.window
    all_columns = rel.shape[0]
    begin = part[0] * (all_columns // plan.parts) + (all_columns - plan.halo)
    per, columns_tile, halo = plan.per, plan.columns_tile, plan.halo
    main, rest, fold = plan.main, plan.rest, plan.fold
    half_lanes = lax.broadcasted_iota(jnp.int32, (1, LANES), 1) < LANES // 2
    rest_rows = round_up(rest, 8)

    common = min(slots, COMMON)
    fill = jnp.zeros((LANES // 2 - rest, LANES), jnp.float32)

    def turned_rest(owner):
        near = got[owner, rest:rest + fold, :]
        first = near
        second = pltpu.roll(near, LANES // 2, 1)
        if slots > COMMON:
            away = got[owner, rest + fold + COMMON:rest + 2 * fold + COMMON, :]
            first = jnp.where(half_lanes, first, pltpu.roll(away, LANES // 2, 1))
            second = jnp.where(half_lanes, second, away)
        return jnp.concatenate([got[owner, :rest, :], fill, first[:rest - fold], second, fill], axis=0).T

    def order(step, carry):
        owners = [step * BATCH + k for k in range(BATCH)]
        turned = [turned_rest(owner) for owner in owners] if rest else []
        for owner in owners:
            ranked[pl.ds(owner, common, stride=group), :] = got[owner, rest + fold:rest + fold + common, :]
            if slots > COMMON:
                ranked[pl.ds(owner + COMMON * group, slots - COMMON, stride=group), :] = got[
                    owner, rest + 2 * fold + COMMON:rest + 2 * fold + slots, :
                ]
        for owner, values in zip(owners, turned):
            extra[pl.ds(owner, LANES, stride=group), :] = values
        return carry

    lax.fori_loop(0, group // BATCH, order, 0)

    rank_tiles = ranked.shape[0] // LANES
    padded = lined.shape[0]
    main_rows = round_up(main, 8)

    def line_up(step, carry):
        starts = [pl.multiple_of(step * (2 * LANES) + k * LANES, LANES) for k in range(2)]
        turned = [ranked[pl.ds(start, LANES), :].T[:main_rows] for start in starts]
        for start, values in zip(starts, turned):
            lined[:main_rows, pl.ds(start, LANES)] = values
            if not rest and main % 8:
                lined[main_rows - 8:main_rows, pl.ds(start, LANES)] = values[main - 8:main]
        return carry

    lax.fori_loop(0, rank_tiles // 2, line_up, 0)

    def line_up_rest(both, step, carry):
        starts = [pl.multiple_of(step * (2 * LANES) + k * LANES, LANES) for k in range(2)]
        turned = [extra[pl.ds(start, LANES), :].T for start in starts]
        for start, values in zip(starts, turned):
            for half in range(2 if both else 1):
                lanes = pl.ds(start + half * group * LANES, LANES)
                lined[main:main + rest_rows - 8, lanes] = values[half * LANES // 2:half * LANES // 2 + rest_rows - 8]
                lined[main + rest_rows - 8:main + rest_rows, lanes] = values[
                    half * LANES // 2 + rest - 8:half * LANES // 2 + rest
                ]
        return carry

    if rest:
        second = (rank_tiles - group) // 2
        lax.fori_loop(0, second, functools.partial(line_up_rest, True), 0)
        lax.fori_loop(second, group // 2, functools.partial(line_up_rest, False), 0)
    lined[:, rank_tiles * LANES:] = jnp.zeros((padded, 2 * LANES), jnp.float32)

    for column in range(columns):
        source = (begin + column) & (all_columns - 1)
        starts[column] = base[0, source]
        row = jnp.broadcast_to(rel[pl.ds(source, 1), :], (8, LANES))
        pick[column] = row & (LANES - 1)
        sea[column] = jnp.where(row >= 0, 1.0, 0.0)

    lane = lax.broadcasted_iota(jnp.int32, (8, LANES), 1)

    def bins_step(tile, carry):
        span = pl.ds(pl.multiple_of(tile * 8, 8), 8)
        first_bin = jnp.minimum(tile * 8, per - 8)
        tap = [jnp.broadcast_to(taps[span, k:k + 1], (8, LANES)) for k in range(10)]
        x_up = tap[0] != 0.0
        x_far = jnp.where(x_up, tap[0], tap[4])
        y_up = tap[5] != 0.0
        far_lane = jnp.where(y_up, lane - 2, lane + 2)
        y_far = jnp.where((far_lane >= 0) & (far_lane < LANES), jnp.where(y_up, tap[5], tap[9]), 0.0)
        far_lane = far_lane & (LANES - 1)
        y_left = jnp.where(lane >= 1, tap[6], 0.0)
        y_right = jnp.where(lane < LANES - 1, tap[8], 0.0)

        def expanded(column):
            place = starts[column]
            offset = place & (LANES - 1)
            start = pl.multiple_of(place - offset, LANES)
            low = lined[span, pl.ds(start, LANES)]
            high = lined[span, pl.ds(start + LANES, LANES)]
            both = jnp.where(lane >= offset, low, high)
            return jnp.take_along_axis(both, pick[column], axis=1) * sea[column]

        def store(result, column):
            owner, place = divmod(column - halo, columns_tile)
            start = (owner * per + first_bin) * columns_tile + place
            out[pl.ds(start, 8, stride=columns_tile), :] = result

        def sweep(values, column):
            left_two, left, here, right, right_two = neighbours(values, column)
            value = tap[2] * here + tap[1] * left + tap[3] * right + x_far * jnp.where(x_up, left_two, right_two)
            value = value * sea[column]
            moved = (
                tap[7] * value + y_left * pltpu.roll(value, 1, 1) + y_right * pltpu.roll(value, LANES - 1, 1)
                + y_far * jnp.take_along_axis(value, far_lane, axis=1)
            )
            return moved * sea[column]

        reach = halo // STEPS
        first = {}

        def neighbours(values, column):
            return [values[(column + k) % columns] for k in range(-2, 3)]

        for column in range(columns):
            first[column] = expanded(column)
        middle = {column: sweep(first, column) for column in range(reach, columns - reach)}
        results = {column: sweep(middle, column) for column in range(halo, columns - halo)}
        for column, result in results.items():
            store(result, column)
        return carry

    lax.fori_loop(0, -(-per // 8), bins_step, 0)


def propagate(plan, slots, part, base, got, rel, taps):
    columns = plan.window
    padded = round_up(plan.per, 8)
    ranks = plan.group * slots
    smem = pl.BlockSpec(memory_space=pltpu.SMEM)
    vmem = pl.BlockSpec(memory_space=pltpu.VMEM)
    return pl.pallas_call(
        functools.partial(propagate_kernel, plan, slots),
        out_shape=jax.ShapeDtypeStruct(((columns - 2 * plan.halo) * plan.per, LANES), jnp.float32),
        in_specs=[smem, smem, vmem, vmem, vmem],
        out_specs=vmem,
        scratch_shapes=[
            pltpu.VMEM((ranks, LANES), jnp.float32),
            pltpu.VMEM((LANES * plan.group if plan.rest else 8, LANES), jnp.float32),
            pltpu.VMEM((padded, ranks + 2 * LANES), jnp.float32),
            pltpu.VMEM((columns, 8, LANES), jnp.int32),
            pltpu.VMEM((columns, 8, LANES), jnp.float32),
            pltpu.SMEM((columns,), jnp.int32),
        ],
        compiler_params=pltpu.CompilerParams(vmem_limit_bytes=VMEM_BYTES),
        name="propagate",
    )(part, base, got, rel, taps)


@dataclasses.dataclass(frozen=True)
class Plan:
    tiles: int
    halves: int
    parts: int
    half_bins: int
    columns: int

    @property
    def group(self):
        return self.tiles * self.halves

    @property
    def members(self):
        return self.tiles // self.parts

    @property
    def per(self):
        return -(-self.half_bins // self.members)

    @property
    def main(self):
        return min(self.per, LANES)

    @property
    def rest(self):
        return self.per - self.main

    @property
    def fold(self):
        return -(-self.rest // 2)

    @property
    def columns_tile(self):
        return self.columns // self.tiles

    @property
    def halo(self):
        return 2 * STEPS if self.parts > 1 else 0

    @property
    def window(self):
        return self.columns // self.parts + 2 * self.halo

    def rows(self, slots):
        return self.rest + (2 if slots > COMMON else 1) * self.fold + slots


def shards(spectra, wind, mask, dia_index, dia_weight, nl_coef):
    count_bins, points = spectra.shape
    columns, latitudes = mask.shape
    plan = Plan(
        tiles=lax.axis_size("tile"), halves=lax.axis_size("bin"), parts=2,
        half_bins=count_bins // lax.axis_size("bin"), columns=columns,
    )
    members, parts = plan.members, plan.parts
    sea_total = plan.group * points
    tile_rank = lax.axis_index("tile")

    part = (tile_rank // members).astype(jnp.int32).reshape(1)
    need, first_point, floor, rel = sea_ranks(plan, sea_total, part, mask)
    wanted = need
    bands = lax.axis_size("band")
    for step in range(1, bands):
        wanted = jnp.maximum(
            wanted, lax.ppermute(need, "band", [(band, (band + step) % bands) for band in range(bands)])
        )
    wanted = wanted[0]

    payload = source_terms(plan, first_point, spectra, wind, dia_index, dia_weight, nl_coef)

    cosine, sine, speed = bin_tables(count_bins)
    weights = np.concatenate([stencil(speed * cosine), stencil(speed * sine)])
    table = np.zeros((plan.halves, members, round_up(plan.per, 8), LANES), np.float32)
    for side in range(plan.halves):
        for member in range(members):
            valid = max(0, min(plan.per, plan.half_bins - member * plan.per))
            begin = side * plan.half_bins + member * plan.per
            table[side, member, :valid, :10] = weights[:, begin:begin + valid].T
            if plan.per % 8:
                table[side, member, -8:] = table[side, member, plan.per - 8:plan.per].copy()
    taps = lax.dynamic_slice(
        jnp.asarray(table), (lax.axis_index("bin"), tile_rank % members, 0, 0), (1, 1) + table.shape[2:]
    ).reshape(table.shape[2:])

    def with_slots(slots):
        def run(payload, part, floor, rel, taps):
            got = lax.all_to_all(
                payload[:, :plan.rows(slots)], ("tile", "bin"), split_axis=0, concat_axis=0, tiled=True
            )
            return propagate(plan, slots, part, floor, got, rel, taps)

        return run

    sizes = [size for size in SIZES if size < points] + [points]
    choice = sum((wanted > size).astype(jnp.int32) for size in sizes[:-1])
    moved = lax.switch(choice, [with_slots(size) for size in sizes], payload, part, floor, rel, taps)
    result = lax.all_to_all(
        moved.reshape(members, plan.per, plan.columns_tile, latitudes), "tile", split_axis=0, concat_axis=0,
        axis_index_groups=[list(range(p * members, (p + 1) * members)) for p in range(parts)], tiled=True,
    ).reshape(members * plan.per, plan.columns_tile, latitudes)
    return result[:plan.half_bins]


def solution(mesh):
    in_specs = (
        P(None, ("band", "tile", "bin")),
        P(None, ("band", "tile", "bin")),
        P(None, "band"),
        P(),
        P(),
        P(),
    )
    out_specs = P("bin", "tile", "band")
    return jax.shard_map(shards, mesh=mesh, in_specs=in_specs, out_specs=out_specs, check_vma=False)
```

```python
import dataclasses
import functools
import math

import jax
import jax.numpy as jnp
import numpy as np
from jax import lax
from jax.experimental import pallas as pl
from jax.experimental.pallas import tpu as pltpu
from jax.sharding import PartitionSpec as P

NTH = 36
STEPS = 2
LANES = 128
ROWS = 256
RING = 40
FIRST = 160
COMMON = 192
VMEM_BYTES = 58 * 1024 * 1024
SIZES = (160, 176, 192, 208, 224, 240)
BATCH = 8

LAMBDA = 0.25
COEF_THREE = (1.0 + LAMBDA) ** (-4)
COEF_FOUR = (1.0 - LAMBDA) ** (-4)
COEF_BOTH = (1.0 - LAMBDA * LAMBDA) ** (-4)
CFL_LIMIT = 0.8
WIND_RATE = 0.2


def round_up(value, step):
    return -(-value // step) * step


def bin_tables(count_bins):
    bin_range = np.arange(count_bins)
    theta = 2.0 * math.pi * (bin_range % NTH) / NTH
    group_speed = CFL_LIMIT * 1.1 ** (-(bin_range // NTH).astype(np.float64))
    return np.cos(theta), np.sin(theta), group_speed


def stencil(courant):
    bend = (1.0 - courant * courant) / 6.0
    up = courant >= 0.0
    zero = np.zeros_like(courant)
    left = courant * np.where(up, -bend, zero)
    here = courant * (0.5 + 0.5 * courant + np.where(up, 2.0 * bend, -bend))
    right = courant * (0.5 - 0.5 * courant + np.where(up, -bend, 2.0 * bend))
    far = courant * np.where(up, zero, -bend)
    return np.stack([left, here - left, 1.0 + right - here, far - right, -far])


def source_kernel(plan, first_point, spectra_far, wind_far, index_far, weight_far, nl_far, tables_far, out,
                  spectra, wind, index, weight, nl_coef, tables, arrived, code, weight_pad, nl_pad, spaced, flat_t, low_t, matrix, inter, total, twice):
    count_bins, points = spectra.shape
    padded = flat_t.shape[1]
    chunks = padded // LANES
    rings = count_bins // NTH
    depth = spaced.shape[0]
    whole = count_bins // LANES
    rest = count_bins - whole * LANES
    pairs = [(index_far, index), (weight_far, weight), (nl_far, nl_coef), (wind_far, wind),
             (tables_far, tables), (spectra_far, spectra)]
    copies = [pltpu.make_async_copy(far, near, arrived.at[k]) for k, (far, near) in enumerate(pairs)]
    for copy in copies:
        copy.start()

    code[...] = jnp.zeros(code.shape, jnp.int32)
    weight_pad[...] = jnp.zeros(weight_pad.shape, jnp.float32)
    nl_pad[...] = jnp.zeros(nl_pad.shape, jnp.float32)
    for copy in copies:
        copy.wait()
    nl_pad[:, :count_bins] = nl_coef[...].reshape(1, count_bins)
    for mirror in range(2):
        for member in range(2):
            row = (mirror * 2 + member) * 4
            bins = index[mirror, member]
            ring = ((bins.astype(jnp.float32) + 0.5) * (1.0 / NTH)).astype(jnp.int32)
            lowest = jnp.minimum(jnp.minimum(ring[0:1], ring[1:2]), jnp.minimum(ring[2:3], ring[3:4]))
            direction = bins - ring * NTH
            code[row:row + 4, :count_bins] = jnp.where(ring == lowest, direction, direction + RING)
            code[16 + mirror * 2 + member:17 + mirror * 2 + member, :count_bins] = lowest
            weight_pad[row:row + 4, :count_bins] = weight[mirror, member].astype(jnp.float32)

    gap = jnp.zeros((RING - NTH, points), jnp.float32)
    for ring in range(rings):
        spaced[ring * RING:ring * RING + NTH, :] = spectra[ring * NTH:(ring + 1) * NTH, :]
        spaced[ring * RING + NTH:(ring + 1) * RING, :] = gap
    spaced[rings * RING:, :] = jnp.zeros((depth - rings * RING, points), jnp.float32)
    for half in range(points // LANES):
        span = slice(half * LANES, (half + 1) * LANES)
        for block in range(depth // LANES):
            lanes = slice(block * LANES, (block + 1) * LANES)
            low_t[span, lanes] = spaced[lanes, span].T.astype(jnp.bfloat16)
        for block in range(chunks):
            lanes = slice(block * LANES, (block + 1) * LANES)
            if block < whole:
                values = spectra[lanes, span]
            else:
                values = jnp.concatenate(
                    [spectra[whole * LANES:, span], jnp.zeros((LANES - rest, LANES), jnp.float32)], axis=0
                )
            flat_t[span, lanes] = values.T

    used = rings * RING
    matrix[used:, :] = jnp.zeros((depth - used, matrix.shape[1]), jnp.bfloat16)

    def members_of(chunk):
        lanes = slice(chunk * LANES, (chunk + 1) * LANES)
        wide = chunk * 4 * LANES
        place = lax.broadcasted_iota(jnp.int32, (RING, LANES), 0)
        patterns = []
        for pair in range(4):
            low = jnp.zeros((RING, LANES), jnp.float32)
            high = low
            for corner in range(4):
                r = pair * 4 + corner
                where = code[r:r + 1, lanes]
                amount = jnp.broadcast_to(weight_pad[r:r + 1, lanes], (RING, LANES))
                low = jnp.where(place == where, amount, low)
                high = jnp.where(place + RING == where, amount, high)
            lowest = jnp.broadcast_to(code[16 + pair:17 + pair, lanes], (8, LANES))
            patterns.append((low, high, lowest))
        members = [jnp.zeros((points, 2 * LANES), jnp.float32) for _ in range(2)]
        done = 0
        for ring in range(0, rings, 2):
            for pair in range(4):
                low, high, lowest = patterns[pair]
                parts = []
                for offset in range(2):
                    first = lowest == ring + offset
                    second = lowest == ring + offset - 1
                    for sub in range(0, RING, 8):
                        parts.append(
                            jnp.where(first, low[sub:sub + 8], jnp.where(second, high[sub:sub + 8], 0.0))
                        )
                matrix[ring * RING:(ring + 2) * RING, wide + pair * LANES:wide + (pair + 1) * LANES] = (
                    jnp.concatenate(parts, axis=0).astype(jnp.bfloat16)
                )
            ready = (ring + 2) * RING
            while done < depth and (ready >= done + ROWS or ready == used):
                size = min(ROWS, depth - done)
                for mirror in range(2):
                    members[mirror] = members[mirror] + jnp.dot(
                        low_t[:, done:done + size],
                        matrix[done:done + size, wide + mirror * 2 * LANES:wide + (mirror + 1) * 2 * LANES],
                        preferred_element_type=jnp.float32,
                    )
                done += size
        return members

    def interact(chunk, members):
        lanes = slice(chunk * LANES, (chunk + 1) * LANES)
        wide = chunk * 4 * LANES
        valid = min(LANES, count_bins - chunk * LANES)
        rows = slice(chunk * LANES, chunk * LANES + valid)
        values = flat_t[:, lanes]
        coef = nl_pad[:, lanes]
        turned = []
        for mirror in range(2):
            third = members[mirror][:, :LANES]
            fourth = members[mirror][:, LANES:]
            interaction = coef * (
                values * values * (COEF_THREE * third + COEF_FOUR * fourth)
                - 2.0 * COEF_BOTH * values * third * fourth
            )
            turned.append([interaction[half * LANES:(half + 1) * LANES].T for half in range(points // LANES)])
        for half in range(points // LANES):
            span = slice(half * LANES, (half + 1) * LANES)
            for mirror in range(2):
                low = turned[mirror][half].astype(jnp.bfloat16)
                for member in range(2):
                    start = wide + (mirror * 2 + member) * LANES
                    inter[start:start + LANES, span] = low
            drive = jnp.maximum(
                wind[0:1, span] * tables[0, rows, :] + wind[1:2, span] * tables[1, rows, :], 0.0
            )
            here = spectra[rows, span]
            both = (turned[0][half] + turned[1][half])[:valid]
            total[rows, span] = here + WIND_RATE * drive * here - 2.0 * both

    previous = None
    for chunk in range(chunks):
        members = members_of(chunk)
        if previous is not None:
            interact(chunk - 1, previous)
        previous = members
    interact(chunks - 1, previous)
    added = 0
    packed = 0
    owners = [(side, member) for side in range(plan.halves) for member in range(plan.members)]
    for start in range(0, used, ROWS):
        size = min(ROWS, used - start)
        spaced[start:start + size, :] = jnp.dot(
            matrix[start:start + size, :], inter[...], preferred_element_type=jnp.float32
        )
        while added < rings and added * RING + NTH <= start + size:
            total[added * NTH:(added + 1) * NTH, :] += spaced[added * RING:added * RING + NTH, :]
            added += 1
        while packed < len(owners):
            side, member = owners[packed]
            if min(side * plan.half_bins + (member + 1) * plan.per, count_bins) > added * NTH:
                break
            pack_payload(plan, first_point, total, out, twice, side, member)
            packed += 1


def pack_payload(plan, first_point, total, out, twice, side, member):
    points = total.shape[1]
    main, rest, fold = plan.main, plan.rest, plan.fold
    lane = lax.broadcasted_iota(jnp.int32, (1, LANES), 1)
    first = side * plan.half_bins + member * plan.per
    valid = min(main, plan.half_bins - member * plan.per)
    slot = (side * plan.members + member) % 2
    for half in range(points // LANES):
        values = total[first:first + valid, half * LANES:(half + 1) * LANES]
        if valid < LANES:
            values = jnp.concatenate([values, jnp.zeros((LANES - valid, LANES), jnp.float32)], axis=0)
        turned = values.T
        twice[slot, half * LANES:(half + 1) * LANES, :] = turned
        twice[slot, points + half * LANES:points + (half + 1) * LANES, :] = turned
    for part in range(plan.parts):
        owner = (part * plan.members + member) * plan.halves + side
        begin = lax.rem(first_point[part], points)
        for low, high in ((0, FIRST), (FIRST, COMMON), (COMMON, points)):
            row = plan.row_of(low)
            out[owner, row:row + high - low, :] = twice[slot, pl.ds(begin + low, high - low), :]
        if not rest:
            continue
        shift = lax.rem(begin, LANES)
        swapped = begin >= LANES
        near = pltpu.roll(total[first + main:first + main + rest, :LANES], lax.rem(LANES - shift, LANES), 1)
        away = pltpu.roll(total[first + main:first + main + rest, LANES:], lax.rem(LANES - shift, LANES), 1)
        keep = (lane < LANES - shift) != swapped
        lead = jnp.where(keep, near, away)
        tail = jnp.where(keep, away, near)
        moved = pltpu.roll(tail, LANES // 2, 1)
        out[owner, FIRST:FIRST + rest, :] = lead
        out[owner, FIRST + rest:FIRST + rest + fold, :] = jnp.where(lane < LANES // 2, tail[:fold], moved[rest - fold:])
        out[owner, rest + fold + COMMON:rest + 2 * fold + COMMON, :] = jnp.where(
            lane < LANES // 2, moved[:fold], tail[rest - fold:]
        )


def source_terms(plan, first_point, spectra, wind, index, weight, nl_coef):
    count_bins, points = spectra.shape
    padded = round_up(count_bins, LANES)
    depth = round_up(count_bins // NTH * RING, LANES)
    cosine, sine, _ = bin_tables(count_bins)
    tables = np.stack([cosine, sine]).astype(np.float32)[:, :, None] * np.ones((1, 1, LANES), np.float32)
    smem = pl.BlockSpec(memory_space=pltpu.SMEM)
    vmem = pl.BlockSpec(memory_space=pltpu.VMEM)
    operands = (spectra, wind, index, weight, nl_coef, jnp.asarray(tables))
    return pl.pallas_call(
        functools.partial(source_kernel, plan),
        out_shape=jax.ShapeDtypeStruct((plan.group, plan.rows(points), LANES), jnp.float32),
        in_specs=[smem] + [pl.BlockSpec(memory_space=pl.ANY)] * len(operands),
        out_specs=vmem,
        scratch_shapes=[pltpu.VMEM(operand.shape, operand.dtype) for operand in operands] + [
            pltpu.SemaphoreType.DMA((len(operands),)),
            pltpu.VMEM((24, padded), jnp.int32),
            pltpu.VMEM((16, padded), jnp.float32),
            pltpu.VMEM((1, padded), jnp.float32),
            pltpu.VMEM((depth, points), jnp.float32),
            pltpu.VMEM((points, padded), jnp.float32),
            pltpu.VMEM((points, depth), jnp.bfloat16),
            pltpu.VMEM((depth, 4 * padded), jnp.bfloat16),
            pltpu.VMEM((4 * padded, points), jnp.bfloat16),
            pltpu.VMEM((padded, points), jnp.float32),
            pltpu.VMEM((2, 2 * points, LANES), jnp.float32),
        ],
        compiler_params=pltpu.CompilerParams(vmem_limit_bytes=VMEM_BYTES),
        cost_estimate=pl.CostEstimate(
            flops=4 * depth * 4 * padded * points, bytes_accessed=8 * count_bins * points, transcendentals=0
        ),
        name="source_terms",
    )(first_point, *operands)


def ranks_kernel(plan, sea_total, rank, mask, triangle, need, first_point, floor, rel):
    columns, latitudes = mask.shape
    sea = mask[...].astype(jnp.float32).astype(jnp.bfloat16)

    def product(left, right):
        return jnp.dot(left, right, preferred_element_type=jnp.float32)

    upto = product(sea, triangle[...])
    counts = lax.dot_general(
        jnp.ones((8, latitudes), jnp.bfloat16), sea, (((1,), (1,)), ((), ())), preferred_element_type=jnp.float32
    )
    row = lax.broadcasted_iota(jnp.int32, (columns, columns), 0)
    col = lax.broadcasted_iota(jnp.int32, (columns, columns), 1)
    before_row = product(counts.astype(jnp.bfloat16), jnp.where(row < col, 1.0, 0.0).astype(jnp.bfloat16))
    before_col = jnp.sum(product(jnp.where(col < row, 1.0, 0.0).astype(jnp.bfloat16), sea), axis=1, keepdims=True)
    lane = lax.broadcasted_iota(jnp.int32, (1, columns), 1)
    most = 0
    chosen = 0
    for p in range(plan.parts):
        begin = (p * (columns // plan.parts) - plan.halo) % columns
        inside = (lane + (columns - begin)) & (columns - 1)
        start = jnp.sum(jnp.where(lane == begin, before_row[:1], 0.0)).astype(jnp.int32)
        held = jnp.sum(jnp.where(inside < plan.window, counts[:1], 0.0)).astype(jnp.int32)
        wanted = (held + lax.rem(start, plan.group) + plan.group - 1) // plan.group
        first = jnp.where(wanted * plan.group <= sea_total, start // plan.group, 0)
        first_point[p] = first
        most = jnp.maximum(most, wanted)
        chosen = jnp.where(rank[0] // (plan.halves * plan.members) == p, first, chosen)
    need[0] = most

    def placed(before):
        place = before.astype(jnp.int32) - chosen * plan.group
        place = jnp.where(place < 0, place + sea_total, place)
        return place

    floor[...] = placed(before_row[:1])
    rel[...] = jnp.where(mask[...] == 1, upto.astype(jnp.int32) - 1 + placed(before_col), -1)


def sea_ranks(plan, sea_total, rank, mask):
    columns, latitudes = mask.shape
    smem = pl.BlockSpec(memory_space=pltpu.SMEM)
    vmem = pl.BlockSpec(memory_space=pltpu.VMEM)
    return pl.pallas_call(
        functools.partial(ranks_kernel, plan, sea_total),
        out_shape=[
            jax.ShapeDtypeStruct((1,), jnp.int32),
            jax.ShapeDtypeStruct((plan.parts,), jnp.int32),
            jax.ShapeDtypeStruct((1, columns), jnp.int32),
            jax.ShapeDtypeStruct((columns, latitudes), jnp.int32),
        ],
        in_specs=[smem, vmem, vmem],
        out_specs=[smem, smem, vmem, vmem],
        name="sea_ranks",
    )(rank, mask, jnp.asarray(np.triu(np.ones((latitudes, latitudes))), jnp.bfloat16))


def propagate_kernel(plan, slots, rank, base, got, rel, table, out, taps, arrived, ranked, extra, lined, pick, sea, starts):
    group = got.shape[0]
    columns = plan.window
    all_columns = rel.shape[0]
    shares = plan.halves * plan.members
    begin = rank[0] // shares * (all_columns // plan.parts) + (all_columns - plan.halo)
    copy = pltpu.make_async_copy(table.at[lax.rem(rank[0], shares)], taps, arrived)
    copy.start()
    per, columns_tile, halo = plan.per, plan.columns_tile, plan.halo
    main, rest, fold = plan.main, plan.rest, plan.fold
    half_lanes = lax.broadcasted_iota(jnp.int32, (1, LANES), 1) < LANES // 2
    rest_rows = round_up(rest, 8)

    fill = jnp.zeros((LANES // 2 - rest, LANES), jnp.float32)

    def turned_rest(owner):
        near = got[owner, FIRST + rest:FIRST + rest + fold, :]
        first = near
        second = pltpu.roll(near, LANES // 2, 1)
        if slots > COMMON:
            away = got[owner, rest + fold + COMMON:rest + 2 * fold + COMMON, :]
            first = jnp.where(half_lanes, first, pltpu.roll(away, LANES // 2, 1))
            second = jnp.where(half_lanes, second, away)
        return jnp.concatenate([got[owner, FIRST:FIRST + rest, :], fill, first[:rest - fold], second, fill], axis=0).T

    def order(step, carry):
        owners = [step * BATCH + k for k in range(BATCH)]
        turned = [turned_rest(owner) for owner in owners] if rest else []
        for owner in owners:
            for low, high in ((0, FIRST), (FIRST, min(slots, COMMON)), (COMMON, slots)):
                if high > low:
                    row = plan.row_of(low)
                    ranked[pl.ds(owner + low * group, high - low, stride=group), :] = got[
                        owner, row:row + high - low, :
                    ]
        for owner, values in zip(owners, turned):
            extra[pl.ds(owner, LANES, stride=group), :] = values
        return carry

    lax.fori_loop(0, group // BATCH, order, 0)

    rank_tiles = ranked.shape[0] // LANES
    padded = lined.shape[0]
    main_rows = round_up(main, 8)

    def line_up(step, carry):
        starts = [pl.multiple_of(step * (2 * LANES) + k * LANES, LANES) for k in range(2)]
        turned = [ranked[pl.ds(start, LANES), :].T[:main_rows] for start in starts]
        for start, values in zip(starts, turned):
            lined[:main_rows, pl.ds(start, LANES)] = values
            if not rest and main % 8:
                lined[main_rows - 8:main_rows, pl.ds(start, LANES)] = values[main - 8:main]
        return carry

    lax.fori_loop(0, rank_tiles // 2, line_up, 0)

    def line_up_rest(both, step, carry):
        starts = [pl.multiple_of(step * (2 * LANES) + k * LANES, LANES) for k in range(2)]
        turned = [extra[pl.ds(start, LANES), :].T for start in starts]
        for start, values in zip(starts, turned):
            for half in range(2 if both else 1):
                lanes = pl.ds(start + half * group * LANES, LANES)
                lined[main:main + rest_rows - 8, lanes] = values[half * LANES // 2:half * LANES // 2 + rest_rows - 8]
                lined[main + rest_rows - 8:main + rest_rows, lanes] = values[
                    half * LANES // 2 + rest - 8:half * LANES // 2 + rest
                ]
        return carry

    if rest:
        second = (rank_tiles - group) // 2
        lax.fori_loop(0, second, functools.partial(line_up_rest, True), 0)
        lax.fori_loop(second, group // 2, functools.partial(line_up_rest, False), 0)
    lined[:, rank_tiles * LANES:] = jnp.zeros((padded, 2 * LANES), jnp.float32)

    for column in range(columns):
        source = (begin + column) & (all_columns - 1)
        starts[column] = base[0, source]
        row = jnp.broadcast_to(rel[pl.ds(source, 1), :], (8, LANES))
        pick[column] = row & (LANES - 1)
        sea[column] = jnp.where(row >= 0, 1.0, 0.0)

    lane = lax.broadcasted_iota(jnp.int32, (8, LANES), 1)
    copy.wait()

    def bins_step(tile, carry):
        span = pl.ds(pl.multiple_of(tile * 8, 8), 8)
        first_bin = jnp.minimum(tile * 8, per - 8)
        tap = [jnp.broadcast_to(taps[span, k:k + 1], (8, LANES)) for k in range(10)]
        x_up = tap[0] != 0.0
        x_far = jnp.where(x_up, tap[0], tap[4])
        y_up = tap[5] != 0.0
        far_lane = jnp.where(y_up, lane - 2, lane + 2)
        y_far = jnp.where((far_lane >= 0) & (far_lane < LANES), jnp.where(y_up, tap[5], tap[9]), 0.0)
        far_lane = far_lane & (LANES - 1)
        y_left = jnp.where(lane >= 1, tap[6], 0.0)
        y_right = jnp.where(lane < LANES - 1, tap[8], 0.0)

        def expanded(column):
            place = starts[column]
            offset = place & (LANES - 1)
            start = pl.multiple_of(place - offset, LANES)
            low = lined[span, pl.ds(start, LANES)]
            high = lined[span, pl.ds(start + LANES, LANES)]
            both = jnp.where(lane >= offset, low, high)
            return jnp.take_along_axis(both, pick[column], axis=1) * sea[column]

        def store(result, column):
            owner, place = divmod(column - halo, columns_tile)
            start = (owner * per + first_bin) * columns_tile + place
            out[pl.ds(start, 8, stride=columns_tile), :] = result

        def sweep(values, column):
            left_two, left, here, right, right_two = neighbours(values, column)
            value = tap[2] * here + tap[1] * left + tap[3] * right + x_far * jnp.where(x_up, left_two, right_two)
            value = value * sea[column]
            moved = (
                tap[7] * value + y_left * pltpu.roll(value, 1, 1) + y_right * pltpu.roll(value, LANES - 1, 1)
                + y_far * jnp.take_along_axis(value, far_lane, axis=1)
            )
            return moved * sea[column]

        reach = halo // STEPS
        first = {}

        def neighbours(values, column):
            return [values[(column + k) % columns] for k in range(-2, 3)]

        for column in range(columns):
            first[column] = expanded(column)
        middle = {column: sweep(first, column) for column in range(reach, columns - reach)}
        results = {column: sweep(middle, column) for column in range(halo, columns - halo)}
        for column, result in results.items():
            store(result, column)
        return carry

    lax.fori_loop(0, -(-per // 8), bins_step, 0)


def propagate(plan, slots, rank, base, got, rel, table):
    columns = plan.window
    padded = round_up(plan.per, 8)
    ranks = plan.group * slots
    smem = pl.BlockSpec(memory_space=pltpu.SMEM)
    vmem = pl.BlockSpec(memory_space=pltpu.VMEM)
    return pl.pallas_call(
        functools.partial(propagate_kernel, plan, slots),
        out_shape=jax.ShapeDtypeStruct(((columns - 2 * plan.halo) * plan.per, LANES), jnp.float32),
        in_specs=[smem, smem, vmem, vmem, pl.BlockSpec(memory_space=pl.ANY)],
        out_specs=vmem,
        scratch_shapes=[
            pltpu.VMEM((padded, LANES), jnp.float32),
            pltpu.SemaphoreType.DMA,
            pltpu.VMEM((ranks, LANES), jnp.float32),
            pltpu.VMEM((LANES * plan.group if plan.rest else 8, LANES), jnp.float32),
            pltpu.VMEM((padded, ranks + 2 * LANES), jnp.float32),
            pltpu.VMEM((columns, 8, LANES), jnp.int32),
            pltpu.VMEM((columns, 8, LANES), jnp.float32),
            pltpu.SMEM((columns,), jnp.int32),
        ],
        compiler_params=pltpu.CompilerParams(vmem_limit_bytes=VMEM_BYTES),
        name="propagate",
    )(rank, base, got, rel, table)


@dataclasses.dataclass(frozen=True)
class Plan:
    tiles: int
    halves: int
    parts: int
    half_bins: int
    columns: int

    @property
    def group(self):
        return self.tiles * self.halves

    @property
    def members(self):
        return self.tiles // self.parts

    @property
    def per(self):
        return -(-self.half_bins // self.members)

    @property
    def main(self):
        return min(self.per, LANES)

    @property
    def rest(self):
        return self.per - self.main

    @property
    def fold(self):
        return -(-self.rest // 2)

    @property
    def columns_tile(self):
        return self.columns // self.tiles

    @property
    def halo(self):
        return 2 * STEPS if self.parts > 1 else 0

    @property
    def window(self):
        return self.columns // self.parts + 2 * self.halo

    def row_of(self, point):
        return point + (self.rest + self.fold if point >= FIRST else 0) + (self.fold if point >= COMMON else 0)

    def rows(self, slots):
        return self.rest + (2 if slots > COMMON else 1) * self.fold + slots


def shards(spectra, wind, mask, dia_index, dia_weight, nl_coef):
    count_bins, points = spectra.shape
    columns, latitudes = mask.shape
    plan = Plan(
        tiles=lax.axis_size("tile"), halves=lax.axis_size("bin"), parts=2,
        half_bins=count_bins // lax.axis_size("bin"), columns=columns,
    )
    members, parts = plan.members, plan.parts
    sea_total = plan.group * points
    tile_rank = lax.axis_index("tile")

    rank = (
        tile_rank // members * (plan.halves * members) + lax.axis_index("bin") * members + tile_rank % members
    ).astype(jnp.int32).reshape(1)
    need, first_point, floor, rel = sea_ranks(plan, sea_total, rank, mask)
    wanted = need
    bands = lax.axis_size("band")
    for step in range(1, bands):
        wanted = jnp.maximum(
            wanted, lax.ppermute(need, "band", [(band, (band + step) % bands) for band in range(bands)])
        )
    wanted = wanted[0]

    payload = source_terms(plan, first_point, spectra, wind, dia_index, dia_weight, nl_coef)

    cosine, sine, speed = bin_tables(count_bins)
    weights = np.concatenate([stencil(speed * cosine), stencil(speed * sine)])
    table = np.zeros((plan.halves, members, round_up(plan.per, 8), LANES), np.float32)
    for side in range(plan.halves):
        for member in range(members):
            valid = max(0, min(plan.per, plan.half_bins - member * plan.per))
            begin = side * plan.half_bins + member * plan.per
            table[side, member, :valid, :10] = weights[:, begin:begin + valid].T
            if plan.per % 8:
                table[side, member, -8:] = table[side, member, plan.per - 8:plan.per].copy()
    table = jnp.asarray(table.reshape((plan.halves * members,) + table.shape[2:]))

    def with_slots(slots):
        def run(payload, rank, floor, rel, table):
            got = lax.all_to_all(
                payload[:, :plan.rows(slots)], ("tile", "bin"), split_axis=0, concat_axis=0, tiled=True
            )
            return propagate(plan, slots, rank, floor, got, rel, table)

        return run

    sizes = [size for size in SIZES if size < points] + [points]
    choice = sum((wanted > size).astype(jnp.int32) for size in sizes[:-1])
    moved = lax.switch(choice, [with_slots(size) for size in sizes], payload, rank, floor, rel, table)
    result = lax.all_to_all(
        moved.reshape(members, plan.per, plan.columns_tile, latitudes), "tile", split_axis=0, concat_axis=0,
        axis_index_groups=[list(range(p * members, (p + 1) * members)) for p in range(parts)], tiled=True,
    ).reshape(members * plan.per, plan.columns_tile, latitudes)
    return result[:plan.half_bins]


def solution(mesh):
    in_specs = (
        P(None, ("band", "tile", "bin")),
        P(None, ("band", "tile", "bin")),
        P(None, "band"),
        P(),
        P(),
        P(),
    )
    out_specs = P("bin", "tile", "band")
    return jax.shard_map(shards, mesh=mesh, in_specs=in_specs, out_specs=out_specs, check_vma=False)
```

```python
import dataclasses
import functools
import math

import jax
import jax.numpy as jnp
import numpy as np
from jax import lax
from jax.experimental import pallas as pl
from jax.experimental.pallas import tpu as pltpu
from jax.sharding import PartitionSpec as P

NTH = 36
STEPS = 2
LANES = 128
ROWS = 256
RING = 40
FIRST = 160
COMMON = 192
VMEM_BYTES = 58 * 1024 * 1024
SIZES = (160, 176, 192, 208, 224, 240)
BATCH = 8

LAMBDA = 0.25
COEF_THREE = (1.0 + LAMBDA) ** (-4)
COEF_FOUR = (1.0 - LAMBDA) ** (-4)
COEF_BOTH = (1.0 - LAMBDA * LAMBDA) ** (-4)
CFL_LIMIT = 0.8
WIND_RATE = 0.2


def round_up(value, step):
    return -(-value // step) * step


def bin_tables(count_bins):
    bin_range = np.arange(count_bins)
    theta = 2.0 * math.pi * (bin_range % NTH) / NTH
    group_speed = CFL_LIMIT * 1.1 ** (-(bin_range // NTH).astype(np.float64))
    return np.cos(theta), np.sin(theta), group_speed


def stencil(courant):
    bend = (1.0 - courant * courant) / 6.0
    up = courant >= 0.0
    zero = np.zeros_like(courant)
    left = courant * np.where(up, -bend, zero)
    here = courant * (0.5 + 0.5 * courant + np.where(up, 2.0 * bend, -bend))
    right = courant * (0.5 - 0.5 * courant + np.where(up, -bend, 2.0 * bend))
    far = courant * np.where(up, zero, -bend)
    return np.stack([left, here - left, 1.0 + right - here, far - right, -far])


def source_kernel(plan, first_point, spectra_far, wind_far, index_far, weight_far, nl_far, tables_far, out,
                  spectra, wind, index, weight, nl_coef, tables, arrived, code, weight_pad, nl_pad, spaced, flat_t, low_t, matrix, inter, total, twice):
    count_bins, points = spectra.shape
    padded = flat_t.shape[1]
    chunks = padded // LANES
    rings = count_bins // NTH
    depth = spaced.shape[0]
    whole = count_bins // LANES
    rest = count_bins - whole * LANES
    pairs = [(index_far, index), (weight_far, weight), (nl_far, nl_coef), (wind_far, wind),
             (tables_far, tables), (spectra_far, spectra)]
    copies = [pltpu.make_async_copy(far, near, arrived.at[k]) for k, (far, near) in enumerate(pairs)]
    for copy in copies:
        copy.start()

    code[...] = jnp.zeros(code.shape, jnp.int32)
    weight_pad[...] = jnp.zeros(weight_pad.shape, jnp.float32)
    nl_pad[...] = jnp.zeros(nl_pad.shape, jnp.float32)
    for copy in copies:
        copy.wait()
    nl_pad[:, :count_bins] = nl_coef[...].reshape(1, count_bins)
    for mirror in range(2):
        for member in range(2):
            row = (mirror * 2 + member) * 4
            bins = index[mirror, member]
            ring = ((bins.astype(jnp.float32) + 0.5) * (1.0 / NTH)).astype(jnp.int32)
            lowest = jnp.minimum(jnp.minimum(ring[0:1], ring[1:2]), jnp.minimum(ring[2:3], ring[3:4]))
            direction = bins - ring * NTH
            code[row:row + 4, :count_bins] = jnp.where(ring == lowest, direction, direction + RING)
            code[16 + mirror * 2 + member:17 + mirror * 2 + member, :count_bins] = lowest
            weight_pad[row:row + 4, :count_bins] = weight[mirror, member].astype(jnp.float32)

    gap = jnp.zeros((RING - NTH, points), jnp.float32)
    for ring in range(rings):
        spaced[ring * RING:ring * RING + NTH, :] = spectra[ring * NTH:(ring + 1) * NTH, :]
        spaced[ring * RING + NTH:(ring + 1) * RING, :] = gap
    spaced[rings * RING:, :] = jnp.zeros((depth - rings * RING, points), jnp.float32)
    for half in range(points // LANES):
        span = slice(half * LANES, (half + 1) * LANES)
        for block in range(depth // LANES):
            lanes = slice(block * LANES, (block + 1) * LANES)
            low_t[span, lanes] = spaced[lanes, span].T.astype(jnp.bfloat16)
        for block in range(chunks):
            lanes = slice(block * LANES, (block + 1) * LANES)
            if block < whole:
                values = spectra[lanes, span]
            else:
                values = jnp.concatenate(
                    [spectra[whole * LANES:, span], jnp.zeros((LANES - rest, LANES), jnp.float32)], axis=0
                )
            flat_t[span, lanes] = values.T

    used = rings * RING
    matrix[used:, :] = jnp.zeros((depth - used, matrix.shape[1]), jnp.bfloat16)

    def members_of(chunk):
        lanes = slice(chunk * LANES, (chunk + 1) * LANES)
        wide = chunk * 4 * LANES
        place = lax.broadcasted_iota(jnp.int32, (RING, LANES), 0)
        patterns = []
        for pair in range(4):
            low = jnp.zeros((RING, LANES), jnp.float32)
            high = low
            for corner in range(4):
                r = pair * 4 + corner
                where = code[r:r + 1, lanes]
                amount = jnp.broadcast_to(weight_pad[r:r + 1, lanes], (RING, LANES))
                low = jnp.where(place == where, amount, low)
                high = jnp.where(place + RING == where, amount, high)
            lowest = jnp.broadcast_to(code[16 + pair:17 + pair, lanes], (16, LANES)).astype(jnp.float32)
            empty = jnp.zeros((RING, LANES), jnp.float32)
            patterns.append((
                lowest.astype(jnp.bfloat16),
                [
                    jnp.concatenate(rings_of, axis=0).astype(jnp.bfloat16)
                    for rings_of in ((low, high), (empty, low), (high, empty))
                ],
            ))
        members = [jnp.zeros((points, 2 * LANES), jnp.float32) for _ in range(2)]
        done = 0
        for ring in range(0, rings, 2):
            for pair in range(4):
                lowest, (here, after, ahead) = patterns[pair]
                none = jnp.zeros((16, LANES), jnp.bfloat16)
                for start in range(0, 2 * RING, 16):
                    rows = slice(start, start + 16)
                    block = none
                    if start < RING:
                        block = jnp.where(lowest == float(ring - 1), ahead[rows], block)
                    if start + 16 > RING:
                        block = jnp.where(lowest == float(ring + 1), after[rows], block)
                    block = jnp.where(lowest == float(ring), here[rows], block)
                    matrix[ring * RING + start:ring * RING + start + 16,
                           wide + pair * LANES:wide + (pair + 1) * LANES] = block
            ready = (ring + 2) * RING
            while done < depth and (ready >= done + ROWS or ready == used):
                size = min(ROWS, depth - done)
                for mirror in range(2):
                    members[mirror] = members[mirror] + jnp.dot(
                        low_t[:, done:done + size],
                        matrix[done:done + size, wide + mirror * 2 * LANES:wide + (mirror + 1) * 2 * LANES],
                        preferred_element_type=jnp.float32,
                    )
                done += size
        return members

    def interact(chunk, members):
        lanes = slice(chunk * LANES, (chunk + 1) * LANES)
        wide = chunk * 4 * LANES
        valid = min(LANES, count_bins - chunk * LANES)
        rows = slice(chunk * LANES, chunk * LANES + valid)
        values = flat_t[:, lanes]
        coef = nl_pad[:, lanes]
        turned = []
        for mirror in range(2):
            third = members[mirror][:, :LANES]
            fourth = members[mirror][:, LANES:]
            interaction = coef * (
                values * values * (COEF_THREE * third + COEF_FOUR * fourth)
                - 2.0 * COEF_BOTH * values * third * fourth
            )
            turned.append([interaction[half * LANES:(half + 1) * LANES].T for half in range(points // LANES)])
        for half in range(points // LANES):
            span = slice(half * LANES, (half + 1) * LANES)
            for mirror in range(2):
                low = turned[mirror][half].astype(jnp.bfloat16)
                for member in range(2):
                    start = wide + (mirror * 2 + member) * LANES
                    inter[start:start + LANES, span] = low
            drive = jnp.maximum(
                wind[0:1, span] * tables[0, rows, :] + wind[1:2, span] * tables[1, rows, :], 0.0
            )
            here = spectra[rows, span]
            both = (turned[0][half] + turned[1][half])[:valid]
            total[rows, span] = here + WIND_RATE * drive * here - 2.0 * both

    previous = None
    for chunk in range(chunks):
        members = members_of(chunk)
        if previous is not None:
            interact(chunk - 1, previous)
        previous = members
    interact(chunks - 1, previous)
    added = 0
    packed = 0
    owners = [(side, member) for side in range(plan.halves) for member in range(plan.members)]
    for start in range(0, used, ROWS):
        size = min(ROWS, used - start)
        spaced[start:start + size, :] = jnp.dot(
            matrix[start:start + size, :], inter[...], preferred_element_type=jnp.float32
        )
        while added < rings and added * RING + NTH <= start + size:
            total[added * NTH:(added + 1) * NTH, :] += spaced[added * RING:added * RING + NTH, :]
            added += 1
        while packed < len(owners):
            side, member = owners[packed]
            if min(side * plan.half_bins + (member + 1) * plan.per, count_bins) > added * NTH:
                break
            pack_payload(plan, first_point, total, out, twice, side, member)
            packed += 1


def pack_payload(plan, first_point, total, out, twice, side, member):
    points = total.shape[1]
    main, rest, fold = plan.main, plan.rest, plan.fold
    lane = lax.broadcasted_iota(jnp.int32, (1, LANES), 1)
    first = side * plan.half_bins + member * plan.per
    valid = min(main, plan.half_bins - member * plan.per)
    slot = (side * plan.members + member) % 2
    for half in range(points // LANES):
        values = total[first:first + valid, half * LANES:(half + 1) * LANES]
        if valid < LANES:
            values = jnp.concatenate([values, jnp.zeros((LANES - valid, LANES), jnp.float32)], axis=0)
        turned = values.T
        twice[slot, half * LANES:(half + 1) * LANES, :] = turned
        twice[slot, points + half * LANES:points + (half + 1) * LANES, :] = turned
    for part in range(plan.parts):
        owner = (part * plan.members + member) * plan.halves + side
        begin = lax.rem(first_point[part], points)
        for low, high in ((0, FIRST), (FIRST, COMMON), (COMMON, points)):
            row = plan.row_of(low)
            out[owner, row:row + high - low, :] = twice[slot, pl.ds(begin + low, high - low), :]
        if not rest:
            continue
        shift = lax.rem(begin, LANES)
        swapped = begin >= LANES
        near = pltpu.roll(total[first + main:first + main + rest, :LANES], lax.rem(LANES - shift, LANES), 1)
        away = pltpu.roll(total[first + main:first + main + rest, LANES:], lax.rem(LANES - shift, LANES), 1)
        keep = (lane < LANES - shift) != swapped
        lead = jnp.where(keep, near, away)
        tail = jnp.where(keep, away, near)
        moved = pltpu.roll(tail, LANES // 2, 1)
        out[owner, FIRST:FIRST + rest, :] = lead
        out[owner, FIRST + rest:FIRST + rest + fold, :] = jnp.where(lane < LANES // 2, tail[:fold], moved[rest - fold:])
        out[owner, rest + fold + COMMON:rest + 2 * fold + COMMON, :] = jnp.where(
            lane < LANES // 2, moved[:fold], tail[rest - fold:]
        )


def source_terms(plan, first_point, spectra, wind, index, weight, nl_coef):
    count_bins, points = spectra.shape
    padded = round_up(count_bins, LANES)
    depth = round_up(count_bins // NTH * RING, LANES)
    cosine, sine, _ = bin_tables(count_bins)
    tables = np.stack([cosine, sine]).astype(np.float32)[:, :, None] * np.ones((1, 1, LANES), np.float32)
    smem = pl.BlockSpec(memory_space=pltpu.SMEM)
    vmem = pl.BlockSpec(memory_space=pltpu.VMEM)
    operands = (spectra, wind, index, weight, nl_coef, jnp.asarray(tables))
    return pl.pallas_call(
        functools.partial(source_kernel, plan),
        out_shape=jax.ShapeDtypeStruct((plan.group, plan.rows(points), LANES), jnp.float32),
        in_specs=[smem] + [pl.BlockSpec(memory_space=pl.ANY)] * len(operands),
        out_specs=vmem,
        scratch_shapes=[pltpu.VMEM(operand.shape, operand.dtype) for operand in operands] + [
            pltpu.SemaphoreType.DMA((len(operands),)),
            pltpu.VMEM((24, padded), jnp.int32),
            pltpu.VMEM((16, padded), jnp.float32),
            pltpu.VMEM((1, padded), jnp.float32),
            pltpu.VMEM((depth, points), jnp.float32),
            pltpu.VMEM((points, padded), jnp.float32),
            pltpu.VMEM((points, depth), jnp.bfloat16),
            pltpu.VMEM((depth, 4 * padded), jnp.bfloat16),
            pltpu.VMEM((4 * padded, points), jnp.bfloat16),
            pltpu.VMEM((padded, points), jnp.float32),
            pltpu.VMEM((2, 2 * points, LANES), jnp.float32),
        ],
        compiler_params=pltpu.CompilerParams(vmem_limit_bytes=VMEM_BYTES),
        cost_estimate=pl.CostEstimate(
            flops=4 * depth * 4 * padded * points, bytes_accessed=8 * count_bins * points, transcendentals=0
        ),
        name="source_terms",
    )(first_point, *operands)


def ranks_kernel(plan, sea_total, rank, mask, triangle, need, first_point, floor, rel):
    columns, latitudes = mask.shape
    sea = mask[...].astype(jnp.float32).astype(jnp.bfloat16)

    def product(left, right):
        return jnp.dot(left, right, preferred_element_type=jnp.float32)

    upto = product(sea, triangle[...])
    counts = lax.dot_general(
        jnp.ones((8, latitudes), jnp.bfloat16), sea, (((1,), (1,)), ((), ())), preferred_element_type=jnp.float32
    )
    row = lax.broadcasted_iota(jnp.int32, (columns, columns), 0)
    col = lax.broadcasted_iota(jnp.int32, (columns, columns), 1)
    before_row = product(counts.astype(jnp.bfloat16), jnp.where(row < col, 1.0, 0.0).astype(jnp.bfloat16))
    before_col = jnp.sum(product(jnp.where(col < row, 1.0, 0.0).astype(jnp.bfloat16), sea), axis=1, keepdims=True)
    lane = lax.broadcasted_iota(jnp.int32, (1, columns), 1)
    most = 0
    chosen = 0
    for p in range(plan.parts):
        begin = (p * (columns // plan.parts) - plan.halo) % columns
        inside = (lane + (columns - begin)) & (columns - 1)
        start = jnp.sum(jnp.where(lane == begin, before_row[:1], 0.0)).astype(jnp.int32)
        held = jnp.sum(jnp.where(inside < plan.window, counts[:1], 0.0)).astype(jnp.int32)
        wanted = (held + lax.rem(start, plan.group) + plan.group - 1) // plan.group
        first = jnp.where(wanted * plan.group <= sea_total, start // plan.group, 0)
        first_point[p] = first
        most = jnp.maximum(most, wanted)
        chosen = jnp.where(rank[0] // (plan.halves * plan.members) == p, first, chosen)
    need[0] = most

    def placed(before):
        place = before.astype(jnp.int32) - chosen * plan.group
        place = jnp.where(place < 0, place + sea_total, place)
        return place

    floor[...] = placed(before_row[:1])
    rel[...] = jnp.where(mask[...] == 1, upto.astype(jnp.int32) - 1 + placed(before_col), -1)


def sea_ranks(plan, sea_total, rank, mask):
    columns, latitudes = mask.shape
    smem = pl.BlockSpec(memory_space=pltpu.SMEM)
    vmem = pl.BlockSpec(memory_space=pltpu.VMEM)
    return pl.pallas_call(
        functools.partial(ranks_kernel, plan, sea_total),
        out_shape=[
            jax.ShapeDtypeStruct((1,), jnp.int32),
            jax.ShapeDtypeStruct((plan.parts,), jnp.int32),
            jax.ShapeDtypeStruct((1, columns), jnp.int32),
            jax.ShapeDtypeStruct((columns, latitudes), jnp.int32),
        ],
        in_specs=[smem, vmem, vmem],
        out_specs=[smem, smem, vmem, vmem],
        name="sea_ranks",
    )(rank, mask, jnp.asarray(np.triu(np.ones((latitudes, latitudes))), jnp.bfloat16))


def propagate_kernel(plan, slots, rank, base, got, rel, table, out, taps, arrived, ranked, extra, lined, pick, sea, starts):
    group = got.shape[0]
    columns = plan.window
    all_columns = rel.shape[0]
    shares = plan.halves * plan.members
    begin = rank[0] // shares * (all_columns // plan.parts) + (all_columns - plan.halo)
    copy = pltpu.make_async_copy(table.at[lax.rem(rank[0], shares)], taps, arrived)
    copy.start()
    per, columns_tile, halo = plan.per, plan.columns_tile, plan.halo
    main, rest, fold = plan.main, plan.rest, plan.fold
    half_lanes = lax.broadcasted_iota(jnp.int32, (1, LANES), 1) < LANES // 2
    rest_rows = round_up(rest, 8)

    fill = jnp.zeros((LANES // 2 - rest, LANES), jnp.float32)

    def turned_rest(owner):
        near = got[owner, FIRST + rest:FIRST + rest + fold, :]
        first = near
        second = pltpu.roll(near, LANES // 2, 1)
        if slots > COMMON:
            away = got[owner, rest + fold + COMMON:rest + 2 * fold + COMMON, :]
            first = jnp.where(half_lanes, first, pltpu.roll(away, LANES // 2, 1))
            second = jnp.where(half_lanes, second, away)
        return jnp.concatenate([got[owner, FIRST:FIRST + rest, :], fill, first[:rest - fold], second, fill], axis=0).T

    def order(step, carry):
        owners = [step * BATCH + k for k in range(BATCH)]
        turned = [turned_rest(owner) for owner in owners] if rest else []
        for owner in owners:
            for low, high in ((0, FIRST), (FIRST, min(slots, COMMON)), (COMMON, slots)):
                if high > low:
                    row = plan.row_of(low)
                    ranked[pl.ds(owner + low * group, high - low, stride=group), :] = got[
                        owner, row:row + high - low, :
                    ]
        for owner, values in zip(owners, turned):
            extra[pl.ds(owner, LANES, stride=group), :] = values
        return carry

    lax.fori_loop(0, group // BATCH, order, 0)

    rank_tiles = ranked.shape[0] // LANES
    padded = lined.shape[0]
    main_rows = round_up(main, 8)

    def line_up(step, carry):
        starts = [pl.multiple_of(step * (2 * LANES) + k * LANES, LANES) for k in range(2)]
        turned = [ranked[pl.ds(start, LANES), :].T[:main_rows] for start in starts]
        for start, values in zip(starts, turned):
            lined[:main_rows, pl.ds(start, LANES)] = values
            if not rest and main % 8:
                lined[main_rows - 8:main_rows, pl.ds(start, LANES)] = values[main - 8:main]
        return carry

    lax.fori_loop(0, rank_tiles // 2, line_up, 0)

    def line_up_rest(both, step, carry):
        starts = [pl.multiple_of(step * (2 * LANES) + k * LANES, LANES) for k in range(2)]
        turned = [extra[pl.ds(start, LANES), :].T for start in starts]
        for start, values in zip(starts, turned):
            for half in range(2 if both else 1):
                lanes = pl.ds(start + half * group * LANES, LANES)
                lined[main:main + rest_rows - 8, lanes] = values[half * LANES // 2:half * LANES // 2 + rest_rows - 8]
                lined[main + rest_rows - 8:main + rest_rows, lanes] = values[
                    half * LANES // 2 + rest - 8:half * LANES // 2 + rest
                ]
        return carry

    if rest:
        second = (rank_tiles - group) // 2
        lax.fori_loop(0, second, functools.partial(line_up_rest, True), 0)
        lax.fori_loop(second, group // 2, functools.partial(line_up_rest, False), 0)
    lined[:, rank_tiles * LANES:] = jnp.zeros((padded, 2 * LANES), jnp.float32)

    for column in range(columns):
        source = (begin + column) & (all_columns - 1)
        starts[column] = base[0, source]
        row = jnp.broadcast_to(rel[pl.ds(source, 1), :], (8, LANES))
        pick[column] = row & (LANES - 1)
        sea[column] = jnp.where(row >= 0, 1.0, 0.0)

    lane = lax.broadcasted_iota(jnp.int32, (8, LANES), 1)
    copy.wait()

    tiles = -(-per // 8)

    def expanded(tile, column):
        span = pl.ds(pl.multiple_of(tile * 8, 8), 8)
        place = starts[column]
        offset = place & (LANES - 1)
        start = pl.multiple_of(place - offset, LANES)
        low = lined[span, pl.ds(start, LANES)]
        high = lined[span, pl.ds(start + LANES, LANES)]
        both = jnp.where(lane >= offset, low, high)
        return jnp.take_along_axis(both, pick[column], axis=1) * sea[column]

    def bins_step(tile, first):
        following = jnp.minimum(tile + 1, tiles - 1)
        coming = tuple(expanded(following, column) for column in range(columns))
        span = pl.ds(pl.multiple_of(tile * 8, 8), 8)
        first_bin = jnp.minimum(tile * 8, per - 8)
        tap = [jnp.broadcast_to(taps[span, k:k + 1], (8, LANES)) for k in range(10)]
        x_up = tap[0] != 0.0
        x_far = jnp.where(x_up, tap[0], tap[4])
        y_up = tap[5] != 0.0
        far_lane = jnp.where(y_up, lane - 2, lane + 2)
        y_far = jnp.where((far_lane >= 0) & (far_lane < LANES), jnp.where(y_up, tap[5], tap[9]), 0.0)
        far_lane = far_lane & (LANES - 1)
        y_left = jnp.where(lane >= 1, tap[6], 0.0)
        y_right = jnp.where(lane < LANES - 1, tap[8], 0.0)

        def store(result, column):
            owner, place = divmod(column - halo, columns_tile)
            start = (owner * per + first_bin) * columns_tile + place
            out[pl.ds(start, 8, stride=columns_tile), :] = result

        def sweep(values, column):
            left_two, left, here, right, right_two = neighbours(values, column)
            value = tap[2] * here + tap[1] * left + tap[3] * right + x_far * jnp.where(x_up, left_two, right_two)
            value = value * sea[column]
            moved = (
                tap[7] * value + y_left * pltpu.roll(value, 1, 1) + y_right * pltpu.roll(value, LANES - 1, 1)
                + y_far * jnp.take_along_axis(value, far_lane, axis=1)
            )
            return moved * sea[column]

        reach = halo // STEPS

        def neighbours(values, column):
            return [values[(column + k) % columns] for k in range(-2, 3)]

        middle = {column: sweep(first, column) for column in range(reach, columns - reach)}
        results = {column: sweep(middle, column) for column in range(halo, columns - halo)}
        for column, result in results.items():
            store(result, column)
        return coming

    lax.fori_loop(0, tiles, bins_step, tuple(expanded(0, column) for column in range(columns)))


def propagate(plan, slots, rank, base, got, rel, table):
    columns = plan.window
    padded = round_up(plan.per, 8)
    ranks = plan.group * slots
    smem = pl.BlockSpec(memory_space=pltpu.SMEM)
    vmem = pl.BlockSpec(memory_space=pltpu.VMEM)
    return pl.pallas_call(
        functools.partial(propagate_kernel, plan, slots),
        out_shape=jax.ShapeDtypeStruct(((columns - 2 * plan.halo) * plan.per, LANES), jnp.float32),
        in_specs=[smem, smem, vmem, vmem, pl.BlockSpec(memory_space=pl.ANY)],
        out_specs=vmem,
        scratch_shapes=[
            pltpu.VMEM((padded, LANES), jnp.float32),
            pltpu.SemaphoreType.DMA,
            pltpu.VMEM((ranks, LANES), jnp.float32),
            pltpu.VMEM((LANES * plan.group if plan.rest else 8, LANES), jnp.float32),
            pltpu.VMEM((padded, ranks + 2 * LANES), jnp.float32),
            pltpu.VMEM((columns, 8, LANES), jnp.int32),
            pltpu.VMEM((columns, 8, LANES), jnp.float32),
            pltpu.SMEM((columns,), jnp.int32),
        ],
        compiler_params=pltpu.CompilerParams(vmem_limit_bytes=VMEM_BYTES),
        name="propagate",
    )(rank, base, got, rel, table)


@dataclasses.dataclass(frozen=True)
class Plan:
    tiles: int
    halves: int
    parts: int
    half_bins: int
    columns: int

    @property
    def group(self):
        return self.tiles * self.halves

    @property
    def members(self):
        return self.tiles // self.parts

    @property
    def per(self):
        return -(-self.half_bins // self.members)

    @property
    def main(self):
        return min(self.per, LANES)

    @property
    def rest(self):
        return self.per - self.main

    @property
    def fold(self):
        return -(-self.rest // 2)

    @property
    def columns_tile(self):
        return self.columns // self.tiles

    @property
    def halo(self):
        return 2 * STEPS if self.parts > 1 else 0

    @property
    def window(self):
        return self.columns // self.parts + 2 * self.halo

    def row_of(self, point):
        return point + (self.rest + self.fold if point >= FIRST else 0) + (self.fold if point >= COMMON else 0)

    def rows(self, slots):
        return self.rest + (2 if slots > COMMON else 1) * self.fold + slots


def shards(spectra, wind, mask, dia_index, dia_weight, nl_coef):
    count_bins, points = spectra.shape
    columns, latitudes = mask.shape
    plan = Plan(
        tiles=lax.axis_size("tile"), halves=lax.axis_size("bin"), parts=2,
        half_bins=count_bins // lax.axis_size("bin"), columns=columns,
    )
    members, parts = plan.members, plan.parts
    sea_total = plan.group * points
    tile_rank = lax.axis_index("tile")

    rank = (
        tile_rank // members * (plan.halves * members) + lax.axis_index("bin") * members + tile_rank % members
    ).astype(jnp.int32).reshape(1)
    need, first_point, floor, rel = sea_ranks(plan, sea_total, rank, mask)
    wanted = need
    bands = lax.axis_size("band")
    for step in range(1, bands):
        wanted = jnp.maximum(
            wanted, lax.ppermute(need, "band", [(band, (band + step) % bands) for band in range(bands)])
        )
    wanted = wanted[0]

    payload = source_terms(plan, first_point, spectra, wind, dia_index, dia_weight, nl_coef)

    cosine, sine, speed = bin_tables(count_bins)
    weights = np.concatenate([stencil(speed * cosine), stencil(speed * sine)])
    table = np.zeros((plan.halves, members, round_up(plan.per, 8), LANES), np.float32)
    for side in range(plan.halves):
        for member in range(members):
            valid = max(0, min(plan.per, plan.half_bins - member * plan.per))
            begin = side * plan.half_bins + member * plan.per
            table[side, member, :valid, :10] = weights[:, begin:begin + valid].T
            if plan.per % 8:
                table[side, member, -8:] = table[side, member, plan.per - 8:plan.per].copy()
    table = jnp.asarray(table.reshape((plan.halves * members,) + table.shape[2:]))

    def with_slots(slots):
        def run(payload, rank, floor, rel, table):
            got = lax.all_to_all(
                payload[:, :plan.rows(slots)], ("tile", "bin"), split_axis=0, concat_axis=0, tiled=True
            )
            return propagate(plan, slots, rank, floor, got, rel, table)

        return run

    sizes = [size for size in SIZES if size < points] + [points]
    choice = sum((wanted > size).astype(jnp.int32) for size in sizes[:-1])
    moved = lax.switch(choice, [with_slots(size) for size in sizes], payload, rank, floor, rel, table)
    result = lax.all_to_all(
        moved.reshape(members, plan.per, plan.columns_tile, latitudes), "tile", split_axis=0, concat_axis=0,
        axis_index_groups=[list(range(p * members, (p + 1) * members)) for p in range(parts)], tiled=True,
    ).reshape(members * plan.per, plan.columns_tile, latitudes)
    return result[:plan.half_bins]


def solution(mesh):
    in_specs = (
        P(None, ("band", "tile", "bin")),
        P(None, ("band", "tile", "bin")),
        P(None, "band"),
        P(),
        P(),
        P(),
    )
    out_specs = P("bin", "tile", "band")
    return jax.shard_map(shards, mesh=mesh, in_specs=in_specs, out_specs=out_specs, check_vma=False)
```

```python
import dataclasses
import functools
import math

import jax
import jax.numpy as jnp
import numpy as np
from jax import lax
from jax.experimental import pallas as pl
from jax.experimental.pallas import tpu as pltpu
from jax.sharding import PartitionSpec as P

NTH = 36
STEPS = 2
LANES = 128
ROWS = 256
RING = 40
FIRST = 160
COMMON = 192
VMEM_BYTES = 58 * 1024 * 1024
SIZES = (176, 192, 208, 224)
BATCH = 8

LAMBDA = 0.25
COEF_THREE = (1.0 + LAMBDA) ** (-4)
COEF_FOUR = (1.0 - LAMBDA) ** (-4)
COEF_BOTH = (1.0 - LAMBDA * LAMBDA) ** (-4)
CFL_LIMIT = 0.8
WIND_RATE = 0.2


def round_up(value, step):
    return -(-value // step) * step


def bin_tables(count_bins):
    bin_range = np.arange(count_bins)
    theta = 2.0 * math.pi * (bin_range % NTH) / NTH
    group_speed = CFL_LIMIT * 1.1 ** (-(bin_range // NTH).astype(np.float64))
    return np.cos(theta), np.sin(theta), group_speed


def stencil(courant):
    bend = (1.0 - courant * courant) / 6.0
    up = courant >= 0.0
    zero = np.zeros_like(courant)
    left = courant * np.where(up, -bend, zero)
    here = courant * (0.5 + 0.5 * courant + np.where(up, 2.0 * bend, -bend))
    right = courant * (0.5 - 0.5 * courant + np.where(up, -bend, 2.0 * bend))
    far = courant * np.where(up, zero, -bend)
    return np.stack([left, here - left, 1.0 + right - here, far - right, -far])


def source_kernel(plan, first_point, spectra_far, wind_far, index_far, weight_far, nl_far, tables_far, out,
                  spectra, wind, index, weight, nl_coef, tables, arrived, code, weight_pad, nl_pad, spaced, flat_t, low_t, matrix, inter, total, twice):
    count_bins, points = spectra.shape
    padded = flat_t.shape[1]
    chunks = padded // LANES
    rings = count_bins // NTH
    depth = spaced.shape[0]
    whole = count_bins // LANES
    rest = count_bins - whole * LANES
    pairs = [(index_far, index), (weight_far, weight), (nl_far, nl_coef), (wind_far, wind),
             (tables_far, tables), (spectra_far, spectra)]
    copies = [pltpu.make_async_copy(far, near, arrived.at[k]) for k, (far, near) in enumerate(pairs)]
    for copy in copies:
        copy.start()

    code[...] = jnp.zeros(code.shape, jnp.int32)
    weight_pad[...] = jnp.zeros(weight_pad.shape, jnp.float32)
    nl_pad[...] = jnp.zeros(nl_pad.shape, jnp.float32)
    for copy in copies:
        copy.wait()
    nl_pad[:, :count_bins] = nl_coef[...].reshape(1, count_bins)
    for mirror in range(2):
        for member in range(2):
            row = (mirror * 2 + member) * 4
            bins = index[mirror, member]
            ring = ((bins.astype(jnp.float32) + 0.5) * (1.0 / NTH)).astype(jnp.int32)
            lowest = jnp.minimum(jnp.minimum(ring[0:1], ring[1:2]), jnp.minimum(ring[2:3], ring[3:4]))
            direction = bins - ring * NTH
            code[row:row + 4, :count_bins] = jnp.where(ring == lowest, direction, direction + RING)
            code[16 + mirror * 2 + member:17 + mirror * 2 + member, :count_bins] = lowest
            weight_pad[row:row + 4, :count_bins] = weight[mirror, member].astype(jnp.float32)

    gap = jnp.zeros((RING - NTH, points), jnp.float32)
    for ring in range(rings):
        spaced[ring * RING:ring * RING + NTH, :] = spectra[ring * NTH:(ring + 1) * NTH, :]
        spaced[ring * RING + NTH:(ring + 1) * RING, :] = gap
    spaced[rings * RING:, :] = jnp.zeros((depth - rings * RING, points), jnp.float32)
    for half in range(points // LANES):
        span = slice(half * LANES, (half + 1) * LANES)
        for block in range(depth // LANES):
            lanes = slice(block * LANES, (block + 1) * LANES)
            low_t[span, lanes] = spaced[lanes, span].T.astype(jnp.bfloat16)
        for block in range(chunks):
            lanes = slice(block * LANES, (block + 1) * LANES)
            if block < whole:
                values = spectra[lanes, span]
            else:
                values = jnp.concatenate(
                    [spectra[whole * LANES:, span], jnp.zeros((LANES - rest, LANES), jnp.float32)], axis=0
                )
            flat_t[span, lanes] = values.T

    used = rings * RING
    matrix[used:, :] = jnp.zeros((depth - used, matrix.shape[1]), jnp.bfloat16)

    def members_of(chunk):
        lanes = slice(chunk * LANES, (chunk + 1) * LANES)
        wide = chunk * 4 * LANES
        place = lax.broadcasted_iota(jnp.int32, (RING, LANES), 0)
        patterns = []
        for pair in range(4):
            low = jnp.zeros((RING, LANES), jnp.float32)
            high = low
            for corner in range(4):
                r = pair * 4 + corner
                where = code[r:r + 1, lanes]
                amount = jnp.broadcast_to(weight_pad[r:r + 1, lanes], (RING, LANES))
                low = jnp.where(place == where, amount, low)
                high = jnp.where(place + RING == where, amount, high)
            lowest = jnp.broadcast_to(code[16 + pair:17 + pair, lanes], (16, LANES)).astype(jnp.float32)
            empty = jnp.zeros((RING, LANES), jnp.float32)
            patterns.append((
                lowest.astype(jnp.bfloat16),
                [
                    jnp.concatenate(rings_of, axis=0).astype(jnp.bfloat16)
                    for rings_of in ((low, high), (empty, low), (high, empty))
                ],
            ))
        members = [jnp.zeros((points, 2 * LANES), jnp.float32) for _ in range(2)]
        done = 0
        for ring in range(0, rings, 2):
            for pair in range(4):
                lowest, (here, after, ahead) = patterns[pair]
                none = jnp.zeros((16, LANES), jnp.bfloat16)
                for start in range(0, 2 * RING, 16):
                    rows = slice(start, start + 16)
                    block = none
                    if start < RING:
                        block = jnp.where(lowest == float(ring - 1), ahead[rows], block)
                    if start + 16 > RING:
                        block = jnp.where(lowest == float(ring + 1), after[rows], block)
                    block = jnp.where(lowest == float(ring), here[rows], block)
                    matrix[ring * RING + start:ring * RING + start + 16,
                           wide + pair * LANES:wide + (pair + 1) * LANES] = block
            ready = (ring + 2) * RING
            while done < depth and (ready >= done + ROWS or ready == used):
                size = min(ROWS, depth - done)
                for mirror in range(2):
                    members[mirror] = members[mirror] + jnp.dot(
                        low_t[:, done:done + size],
                        matrix[done:done + size, wide + mirror * 2 * LANES:wide + (mirror + 1) * 2 * LANES],
                        preferred_element_type=jnp.float32,
                    )
                done += size
        return members

    def interact(chunk, members):
        lanes = slice(chunk * LANES, (chunk + 1) * LANES)
        wide = chunk * 4 * LANES
        valid = min(LANES, count_bins - chunk * LANES)
        rows = slice(chunk * LANES, chunk * LANES + valid)
        values = flat_t[:, lanes]
        coef = nl_pad[:, lanes]
        turned = []
        for mirror in range(2):
            third = members[mirror][:, :LANES]
            fourth = members[mirror][:, LANES:]
            interaction = coef * (
                values * values * (COEF_THREE * third + COEF_FOUR * fourth)
                - 2.0 * COEF_BOTH * values * third * fourth
            )
            turned.append([interaction[half * LANES:(half + 1) * LANES].T for half in range(points // LANES)])
        for half in range(points // LANES):
            span = slice(half * LANES, (half + 1) * LANES)
            for mirror in range(2):
                low = turned[mirror][half].astype(jnp.bfloat16)
                for member in range(2):
                    start = wide + (mirror * 2 + member) * LANES
                    inter[start:start + LANES, span] = low
            drive = jnp.maximum(
                wind[0:1, span] * tables[0, rows, :] + wind[1:2, span] * tables[1, rows, :], 0.0
            )
            here = spectra[rows, span]
            both = (turned[0][half] + turned[1][half])[:valid]
            total[rows, span] = here + WIND_RATE * drive * here - 2.0 * both

    previous = None
    for chunk in range(chunks):
        members = members_of(chunk)
        if previous is not None:
            interact(chunk - 1, previous)
        previous = members
    interact(chunks - 1, previous)
    added = 0
    packed = 0
    owners = [(side, member) for side in range(plan.halves) for member in range(plan.members)]
    for start in range(0, used, ROWS):
        size = min(ROWS, used - start)
        spaced[start:start + size, :] = jnp.dot(
            matrix[start:start + size, :], inter[...], preferred_element_type=jnp.float32
        )
        while added < rings and added * RING + NTH <= start + size:
            total[added * NTH:(added + 1) * NTH, :] += spaced[added * RING:added * RING + NTH, :]
            added += 1
        while packed < len(owners):
            side, member = owners[packed]
            if min(side * plan.half_bins + (member + 1) * plan.per, count_bins) > added * NTH:
                break
            pack_payload(plan, first_point, total, out, twice, side, member)
            packed += 1


def pack_payload(plan, first_point, total, out, twice, side, member):
    points = total.shape[1]
    main, rest, fold = plan.main, plan.rest, plan.fold
    lane = lax.broadcasted_iota(jnp.int32, (1, LANES), 1)
    first = side * plan.half_bins + member * plan.per
    valid = min(main, plan.half_bins - member * plan.per)
    slot = (side * plan.members + member) % 2
    for half in range(points // LANES):
        values = total[first:first + valid, half * LANES:(half + 1) * LANES]
        if valid < LANES:
            values = jnp.concatenate([values, jnp.zeros((LANES - valid, LANES), jnp.float32)], axis=0)
        turned = values.T
        twice[slot, half * LANES:(half + 1) * LANES, :] = turned
        twice[slot, points + half * LANES:points + (half + 1) * LANES, :] = turned
    for part in range(plan.parts):
        owner = (part * plan.members + member) * plan.halves + side
        begin = lax.rem(first_point[part], points)
        for low, high in ((0, FIRST), (FIRST, COMMON), (COMMON, points)):
            row = plan.row_of(low)
            out[owner, row:row + high - low, :] = twice[slot, pl.ds(begin + low, high - low), :]
        if not rest:
            continue
        shift = lax.rem(begin, LANES)
        swapped = begin >= LANES
        near = pltpu.roll(total[first + main:first + main + rest, :LANES], lax.rem(LANES - shift, LANES), 1)
        away = pltpu.roll(total[first + main:first + main + rest, LANES:], lax.rem(LANES - shift, LANES), 1)
        keep = (lane < LANES - shift) != swapped
        lead = jnp.where(keep, near, away)
        tail = jnp.where(keep, away, near)
        moved = pltpu.roll(tail, LANES // 2, 1)
        out[owner, FIRST:FIRST + rest, :] = lead
        out[owner, FIRST + rest:FIRST + rest + fold, :] = jnp.where(lane < LANES // 2, tail[:fold], moved[rest - fold:])
        out[owner, rest + fold + COMMON:rest + 2 * fold + COMMON, :] = jnp.where(
            lane < LANES // 2, moved[:fold], tail[rest - fold:]
        )


def source_terms(plan, first_point, spectra, wind, index, weight, nl_coef):
    count_bins, points = spectra.shape
    padded = round_up(count_bins, LANES)
    depth = round_up(count_bins // NTH * RING, LANES)
    cosine, sine, _ = bin_tables(count_bins)
    tables = np.stack([cosine, sine]).astype(np.float32)[:, :, None] * np.ones((1, 1, LANES), np.float32)
    smem = pl.BlockSpec(memory_space=pltpu.SMEM)
    vmem = pl.BlockSpec(memory_space=pltpu.VMEM)
    operands = (spectra, wind, index, weight, nl_coef, jnp.asarray(tables))
    return pl.pallas_call(
        functools.partial(source_kernel, plan),
        out_shape=jax.ShapeDtypeStruct((plan.group, plan.rows(points), LANES), jnp.float32),
        in_specs=[smem] + [pl.BlockSpec(memory_space=pl.ANY)] * len(operands),
        out_specs=vmem,
        scratch_shapes=[pltpu.VMEM(operand.shape, operand.dtype) for operand in operands] + [
            pltpu.SemaphoreType.DMA((len(operands),)),
            pltpu.VMEM((24, padded), jnp.int32),
            pltpu.VMEM((16, padded), jnp.float32),
            pltpu.VMEM((1, padded), jnp.float32),
            pltpu.VMEM((depth, points), jnp.float32),
            pltpu.VMEM((points, padded), jnp.float32),
            pltpu.VMEM((points, depth), jnp.bfloat16),
            pltpu.VMEM((depth, 4 * padded), jnp.bfloat16),
            pltpu.VMEM((4 * padded, points), jnp.bfloat16),
            pltpu.VMEM((padded, points), jnp.float32),
            pltpu.VMEM((2, 2 * points, LANES), jnp.float32),
        ],
        compiler_params=pltpu.CompilerParams(vmem_limit_bytes=VMEM_BYTES),
        cost_estimate=pl.CostEstimate(
            flops=4 * depth * 4 * padded * points, bytes_accessed=8 * count_bins * points, transcendentals=0
        ),
        name="source_terms",
    )(first_point, *operands)


def ranks_kernel(plan, sea_total, rank, mask, triangle, need, first_point, floor, rel):
    columns, latitudes = mask.shape
    sea = mask[...].astype(jnp.float32).astype(jnp.bfloat16)

    def product(left, right):
        return jnp.dot(left, right, preferred_element_type=jnp.float32)

    upto = product(sea, triangle[...])
    counts = lax.dot_general(
        jnp.ones((8, latitudes), jnp.bfloat16), sea, (((1,), (1,)), ((), ())), preferred_element_type=jnp.float32
    )
    row = lax.broadcasted_iota(jnp.int32, (columns, columns), 0)
    col = lax.broadcasted_iota(jnp.int32, (columns, columns), 1)
    before_row = product(counts.astype(jnp.bfloat16), jnp.where(row < col, 1.0, 0.0).astype(jnp.bfloat16))
    before_col = jnp.sum(product(jnp.where(col < row, 1.0, 0.0).astype(jnp.bfloat16), sea), axis=1, keepdims=True)
    lane = lax.broadcasted_iota(jnp.int32, (1, columns), 1)
    most = 0
    chosen = 0
    for p in range(plan.parts):
        begin = (p * (columns // plan.parts) - plan.halo) % columns
        inside = (lane + (columns - begin)) & (columns - 1)
        start = jnp.sum(jnp.where(lane == begin, before_row[:1], 0.0)).astype(jnp.int32)
        held = jnp.sum(jnp.where(inside < plan.window, counts[:1], 0.0)).astype(jnp.int32)
        wanted = (held + lax.rem(start, plan.group) + plan.group - 1) // plan.group
        first = jnp.where(wanted * plan.group <= sea_total, start // plan.group, 0)
        first_point[p] = first
        most = jnp.maximum(most, wanted)
        chosen = jnp.where(rank[0] // (plan.halves * plan.members) == p, first, chosen)
    need[0] = most

    def placed(before):
        place = before.astype(jnp.int32) - chosen * plan.group
        place = jnp.where(place < 0, place + sea_total, place)
        return place

    floor[...] = placed(before_row[:1])
    rel[...] = jnp.where(mask[...] == 1, upto.astype(jnp.int32) - 1 + placed(before_col), -1)


def sea_ranks(plan, sea_total, rank, mask):
    columns, latitudes = mask.shape
    smem = pl.BlockSpec(memory_space=pltpu.SMEM)
    vmem = pl.BlockSpec(memory_space=pltpu.VMEM)
    return pl.pallas_call(
        functools.partial(ranks_kernel, plan, sea_total),
        out_shape=[
            jax.ShapeDtypeStruct((1,), jnp.int32),
            jax.ShapeDtypeStruct((plan.parts,), jnp.int32),
            jax.ShapeDtypeStruct((1, columns), jnp.int32),
            jax.ShapeDtypeStruct((columns, latitudes), jnp.int32),
        ],
        in_specs=[smem, vmem, vmem],
        out_specs=[smem, smem, vmem, vmem],
        name="sea_ranks",
    )(rank, mask, jnp.asarray(np.triu(np.ones((latitudes, latitudes))), jnp.bfloat16))


def propagate_kernel(plan, slots, rank, base, got, rel, table, out, taps, arrived, ranked, extra, lined, pick, sea, starts):
    group = got.shape[0]
    columns = plan.window
    all_columns = rel.shape[0]
    shares = plan.halves * plan.members
    begin = rank[0] // shares * (all_columns // plan.parts) + (all_columns - plan.halo)
    copy = pltpu.make_async_copy(table.at[lax.rem(rank[0], shares)], taps, arrived)
    copy.start()
    per, columns_tile, halo = plan.per, plan.columns_tile, plan.halo
    main, rest, fold = plan.main, plan.rest, plan.fold
    half_lanes = lax.broadcasted_iota(jnp.int32, (1, LANES), 1) < LANES // 2
    rest_rows = round_up(rest, 8)

    fill = jnp.zeros((LANES // 2 - rest, LANES), jnp.float32)

    def turned_rest(owner):
        near = got[owner, FIRST + rest:FIRST + rest + fold, :]
        first = near
        second = pltpu.roll(near, LANES // 2, 1)
        if slots > COMMON:
            away = got[owner, rest + fold + COMMON:rest + 2 * fold + COMMON, :]
            first = jnp.where(half_lanes, first, pltpu.roll(away, LANES // 2, 1))
            second = jnp.where(half_lanes, second, away)
        return jnp.concatenate([got[owner, FIRST:FIRST + rest, :], fill, first[:rest - fold], second, fill], axis=0).T

    def order(step, carry):
        owners = [step * BATCH + k for k in range(BATCH)]
        turned = [turned_rest(owner) for owner in owners] if rest else []
        for owner in owners:
            for low, high in ((0, FIRST), (FIRST, min(slots, COMMON)), (COMMON, slots)):
                if high > low:
                    row = plan.row_of(low)
                    ranked[pl.ds(owner + low * group, high - low, stride=group), :] = got[
                        owner, row:row + high - low, :
                    ]
        for owner, values in zip(owners, turned):
            extra[pl.ds(owner, LANES, stride=group), :] = values
        return carry

    lax.fori_loop(0, group // BATCH, order, 0)

    rank_tiles = ranked.shape[0] // LANES
    padded = lined.shape[0]
    main_rows = round_up(main, 8)

    def line_up(step, carry):
        starts = [pl.multiple_of(step * (2 * LANES) + k * LANES, LANES) for k in range(2)]
        turned = [ranked[pl.ds(start, LANES), :].T[:main_rows] for start in starts]
        for start, values in zip(starts, turned):
            lined[:main_rows, pl.ds(start, LANES)] = values
            if not rest and main % 8:
                lined[main_rows - 8:main_rows, pl.ds(start, LANES)] = values[main - 8:main]
        return carry

    lax.fori_loop(0, rank_tiles // 2, line_up, 0)

    def line_up_rest(both, step, carry):
        starts = [pl.multiple_of(step * (2 * LANES) + k * LANES, LANES) for k in range(2)]
        turned = [extra[pl.ds(start, LANES), :].T for start in starts]
        for start, values in zip(starts, turned):
            for half in range(2 if both else 1):
                lanes = pl.ds(start + half * group * LANES, LANES)
                lined[main:main + rest_rows - 8, lanes] = values[half * LANES // 2:half * LANES // 2 + rest_rows - 8]
                lined[main + rest_rows - 8:main + rest_rows, lanes] = values[
                    half * LANES // 2 + rest - 8:half * LANES // 2 + rest
                ]
        return carry

    if rest:
        second = (rank_tiles - group) // 2
        lax.fori_loop(0, second, functools.partial(line_up_rest, True), 0)
        lax.fori_loop(second, group // 2, functools.partial(line_up_rest, False), 0)
    lined[:, rank_tiles * LANES:] = jnp.zeros((padded, 2 * LANES), jnp.float32)

    for column in range(columns):
        source = (begin + column) & (all_columns - 1)
        starts[column] = base[0, source]
        row = jnp.broadcast_to(rel[pl.ds(source, 1), :], (8, LANES))
        pick[column] = row & (LANES - 1)
        sea[column] = jnp.where(row >= 0, 1.0, 0.0)

    lane = lax.broadcasted_iota(jnp.int32, (8, LANES), 1)
    copy.wait()

    def bins_step(tile, carry):
        span = pl.ds(pl.multiple_of(tile * 8, 8), 8)
        first_bin = jnp.minimum(tile * 8, per - 8)
        tap = [jnp.broadcast_to(taps[span, k:k + 1], (8, LANES)) for k in range(10)]
        x_up = tap[0] != 0.0
        x_far = jnp.where(x_up, tap[0], tap[4])
        y_up = tap[5] != 0.0
        far_lane = jnp.where(y_up, lane - 2, lane + 2)
        y_far = jnp.where((far_lane >= 0) & (far_lane < LANES), jnp.where(y_up, tap[5], tap[9]), 0.0)
        far_lane = far_lane & (LANES - 1)
        y_left = jnp.where(lane >= 1, tap[6], 0.0)
        y_right = jnp.where(lane < LANES - 1, tap[8], 0.0)

        def expanded(column):
            place = starts[column]
            offset = place & (LANES - 1)
            start = pl.multiple_of(place - offset, LANES)
            low = lined[span, pl.ds(start, LANES)]
            high = lined[span, pl.ds(start + LANES, LANES)]
            both = jnp.where(lane >= offset, low, high)
            return jnp.take_along_axis(both, pick[column], axis=1) * sea[column]

        def store(result, column):
            owner, place = divmod(column - halo, columns_tile)
            start = (owner * per + first_bin) * columns_tile + place
            out[pl.ds(start, 8, stride=columns_tile), :] = result

        def sweep(values, column):
            left_two, left, here, right, right_two = neighbours(values, column)
            value = tap[2] * here + tap[1] * left + tap[3] * right + x_far * jnp.where(x_up, left_two, right_two)
            value = value * sea[column]
            moved = (
                tap[7] * value + y_left * pltpu.roll(value, 1, 1) + y_right * pltpu.roll(value, LANES - 1, 1)
                + y_far * jnp.take_along_axis(value, far_lane, axis=1)
            )
            return moved * sea[column]

        reach = halo // STEPS
        first = {}

        def neighbours(values, column):
            return [values[(column + k) % columns] for k in range(-2, 3)]

        for column in range(columns):
            first[column] = expanded(column)
        middle = {column: sweep(first, column) for column in range(reach, columns - reach)}
        results = {column: sweep(middle, column) for column in range(halo, columns - halo)}
        for column, result in results.items():
            store(result, column)
        return carry

    lax.fori_loop(0, -(-per // 8), bins_step, 0)


def propagate(plan, slots, rank, base, got, rel, table):
    columns = plan.window
    padded = round_up(plan.per, 8)
    ranks = plan.group * slots
    smem = pl.BlockSpec(memory_space=pltpu.SMEM)
    vmem = pl.BlockSpec(memory_space=pltpu.VMEM)
    return pl.pallas_call(
        functools.partial(propagate_kernel, plan, slots),
        out_shape=jax.ShapeDtypeStruct(((columns - 2 * plan.halo) * plan.per, LANES), jnp.float32),
        in_specs=[smem, smem, vmem, vmem, pl.BlockSpec(memory_space=pl.ANY)],
        out_specs=vmem,
        scratch_shapes=[
            pltpu.VMEM((padded, LANES), jnp.float32),
            pltpu.SemaphoreType.DMA,
            pltpu.VMEM((ranks, LANES), jnp.float32),
            pltpu.VMEM((LANES * plan.group if plan.rest else 8, LANES), jnp.float32),
            pltpu.VMEM((padded, ranks + 2 * LANES), jnp.float32),
            pltpu.VMEM((columns, 8, LANES), jnp.int32),
            pltpu.VMEM((columns, 8, LANES), jnp.float32),
            pltpu.SMEM((columns,), jnp.int32),
        ],
        compiler_params=pltpu.CompilerParams(vmem_limit_bytes=VMEM_BYTES),
        name="propagate",
    )(rank, base, got, rel, table)


@dataclasses.dataclass(frozen=True)
class Plan:
    tiles: int
    halves: int
    parts: int
    half_bins: int
    columns: int

    @property
    def group(self):
        return self.tiles * self.halves

    @property
    def members(self):
        return self.tiles // self.parts

    @property
    def per(self):
        return -(-self.half_bins // self.members)

    @property
    def main(self):
        return min(self.per, LANES)

    @property
    def rest(self):
        return self.per - self.main

    @property
    def fold(self):
        return -(-self.rest // 2)

    @property
    def columns_tile(self):
        return self.columns // self.tiles

    @property
    def halo(self):
        return 2 * STEPS if self.parts > 1 else 0

    @property
    def window(self):
        return self.columns // self.parts + 2 * self.halo

    def row_of(self, point):
        return point + (self.rest + self.fold if point >= FIRST else 0) + (self.fold if point >= COMMON else 0)

    def rows(self, slots):
        return self.rest + (2 if slots > COMMON else 1) * self.fold + slots


def shards(spectra, wind, mask, dia_index, dia_weight, nl_coef):
    count_bins, points = spectra.shape
    columns, latitudes = mask.shape
    plan = Plan(
        tiles=lax.axis_size("tile"), halves=lax.axis_size("bin"), parts=2,
        half_bins=count_bins // lax.axis_size("bin"), columns=columns,
    )
    members, parts = plan.members, plan.parts
    sea_total = plan.group * points
    tile_rank = lax.axis_index("tile")

    rank = (
        tile_rank // members * (plan.halves * members) + lax.axis_index("bin") * members + tile_rank % members
    ).astype(jnp.int32).reshape(1)
    need, first_point, floor, rel = sea_ranks(plan, sea_total, rank, mask)
    wanted = need
    bands = lax.axis_size("band")
    for step in range(1, bands):
        wanted = jnp.maximum(
            wanted, lax.ppermute(need, "band", [(band, (band + step) % bands) for band in range(bands)])
        )
    wanted = wanted[0]

    payload = source_terms(plan, first_point, spectra, wind, dia_index, dia_weight, nl_coef)

    cosine, sine, speed = bin_tables(count_bins)
    weights = np.concatenate([stencil(speed * cosine), stencil(speed * sine)])
    table = np.zeros((plan.halves, members, round_up(plan.per, 8), LANES), np.float32)
    for side in range(plan.halves):
        for member in range(members):
            valid = max(0, min(plan.per, plan.half_bins - member * plan.per))
            begin = side * plan.half_bins + member * plan.per
            table[side, member, :valid, :10] = weights[:, begin:begin + valid].T
            if plan.per % 8:
                table[side, member, -8:] = table[side, member, plan.per - 8:plan.per].copy()
    table = jnp.asarray(table.reshape((plan.halves * members,) + table.shape[2:]))

    def with_slots(slots):
        def run(payload, rank, floor, rel, table):
            got = lax.all_to_all(
                payload[:, :plan.rows(slots)], ("tile", "bin"), split_axis=0, concat_axis=0, tiled=True
            )
            return propagate(plan, slots, rank, floor, got, rel, table)

        return run

    sizes = [size for size in SIZES if size < points] + [points]
    choice = sum((wanted > size).astype(jnp.int32) for size in sizes[:-1])
    moved = lax.switch(choice, [with_slots(size) for size in sizes], payload, rank, floor, rel, table)
    result = lax.all_to_all(
        moved.reshape(members, plan.per, plan.columns_tile, latitudes), "tile", split_axis=0, concat_axis=0,
        axis_index_groups=[list(range(p * members, (p + 1) * members)) for p in range(parts)], tiled=True,
    ).reshape(members * plan.per, plan.columns_tile, latitudes)
    return result[:plan.half_bins]


def solution(mesh):
    in_specs = (
        P(None, ("band", "tile", "bin")),
        P(None, ("band", "tile", "bin")),
        P(None, "band"),
        P(),
        P(),
        P(),
    )
    out_specs = P("bin", "tile", "band")
    return jax.shard_map(shards, mesh=mesh, in_specs=in_specs, out_specs=out_specs, check_vma=False)
```

```python
import dataclasses
import functools
import math

import jax
import jax.numpy as jnp
import numpy as np
from jax import lax
from jax.experimental import pallas as pl
from jax.experimental.pallas import tpu as pltpu
from jax.sharding import PartitionSpec as P

NTH = 36
STEPS = 2
LANES = 128
ROWS = 256
RING = 40
FIRST = 160
COMMON = 192
VMEM_BYTES = 58 * 1024 * 1024
SIZES = (176, 192, 208, 224)
BATCH = 16

LAMBDA = 0.25
COEF_THREE = (1.0 + LAMBDA) ** (-4)
COEF_FOUR = (1.0 - LAMBDA) ** (-4)
COEF_BOTH = (1.0 - LAMBDA * LAMBDA) ** (-4)
CFL_LIMIT = 0.8
WIND_RATE = 0.2


def round_up(value, step):
    return -(-value // step) * step


def bin_tables(count_bins):
    bin_range = np.arange(count_bins)
    theta = 2.0 * math.pi * (bin_range % NTH) / NTH
    group_speed = CFL_LIMIT * 1.1 ** (-(bin_range // NTH).astype(np.float64))
    return np.cos(theta), np.sin(theta), group_speed


def stencil(courant):
    bend = (1.0 - courant * courant) / 6.0
    up = courant >= 0.0
    zero = np.zeros_like(courant)
    left = courant * np.where(up, -bend, zero)
    here = courant * (0.5 + 0.5 * courant + np.where(up, 2.0 * bend, -bend))
    right = courant * (0.5 - 0.5 * courant + np.where(up, -bend, 2.0 * bend))
    far = courant * np.where(up, zero, -bend)
    return np.stack([left, here - left, 1.0 + right - here, far - right, -far])


def source_kernel(plan, first_point, spectra_far, wind_far, index_far, weight_far, nl_far, tables_far, out,
                  spectra, wind, index, weight, nl_coef, tables, arrived, code, weight_pad, nl_pad, spaced, flat_t, low_t, matrix, inter, total, twice):
    count_bins, points = spectra.shape
    padded = flat_t.shape[1]
    chunks = padded // LANES
    rings = count_bins // NTH
    depth = spaced.shape[0]
    whole = count_bins // LANES
    rest = count_bins - whole * LANES
    pairs = [(index_far, index), (weight_far, weight), (nl_far, nl_coef), (wind_far, wind),
             (tables_far, tables), (spectra_far, spectra)]
    copies = [pltpu.make_async_copy(far, near, arrived.at[k]) for k, (far, near) in enumerate(pairs)]
    for copy in copies:
        copy.start()

    code[...] = jnp.zeros(code.shape, jnp.int32)
    weight_pad[...] = jnp.zeros(weight_pad.shape, jnp.float32)
    nl_pad[...] = jnp.zeros(nl_pad.shape, jnp.float32)
    for copy in copies:
        copy.wait()
    nl_pad[:, :count_bins] = nl_coef[...].reshape(1, count_bins)
    for mirror in range(2):
        for member in range(2):
            row = (mirror * 2 + member) * 4
            bins = index[mirror, member]
            ring = ((bins.astype(jnp.float32) + 0.5) * (1.0 / NTH)).astype(jnp.int32)
            lowest = jnp.minimum(jnp.minimum(ring[0:1], ring[1:2]), jnp.minimum(ring[2:3], ring[3:4]))
            direction = bins - ring * NTH
            code[row:row + 4, :count_bins] = jnp.where(ring == lowest, direction, direction + RING)
            code[16 + mirror * 2 + member:17 + mirror * 2 + member, :count_bins] = lowest
            weight_pad[row:row + 4, :count_bins] = weight[mirror, member].astype(jnp.float32)

    gap = jnp.zeros((RING - NTH, points), jnp.float32)
    for ring in range(rings):
        spaced[ring * RING:ring * RING + NTH, :] = spectra[ring * NTH:(ring + 1) * NTH, :]
        spaced[ring * RING + NTH:(ring + 1) * RING, :] = gap
    spaced[rings * RING:, :] = jnp.zeros((depth - rings * RING, points), jnp.float32)
    for half in range(points // LANES):
        span = slice(half * LANES, (half + 1) * LANES)
        for block in range(depth // LANES):
            lanes = slice(block * LANES, (block + 1) * LANES)
            low_t[span, lanes] = spaced[lanes, span].T.astype(jnp.bfloat16)
        for block in range(chunks):
            lanes = slice(block * LANES, (block + 1) * LANES)
            if block < whole:
                values = spectra[lanes, span]
            else:
                values = jnp.concatenate(
                    [spectra[whole * LANES:, span], jnp.zeros((LANES - rest, LANES), jnp.float32)], axis=0
                )
            flat_t[span, lanes] = values.T

    used = rings * RING
    matrix[used:, :] = jnp.zeros((depth - used, matrix.shape[1]), jnp.bfloat16)

    def members_of(chunk):
        lanes = slice(chunk * LANES, (chunk + 1) * LANES)
        wide = chunk * 4 * LANES
        place = lax.broadcasted_iota(jnp.int32, (RING, LANES), 0)
        patterns = []
        for pair in range(4):
            low = jnp.zeros((RING, LANES), jnp.float32)
            high = low
            for corner in range(4):
                r = pair * 4 + corner
                where = code[r:r + 1, lanes]
                amount = jnp.broadcast_to(weight_pad[r:r + 1, lanes], (RING, LANES))
                low = jnp.where(place == where, amount, low)
                high = jnp.where(place + RING == where, amount, high)
            lowest = jnp.broadcast_to(code[16 + pair:17 + pair, lanes], (16, LANES)).astype(jnp.float32)
            empty = jnp.zeros((RING, LANES), jnp.float32)
            patterns.append((
                lowest.astype(jnp.bfloat16),
                [
                    jnp.concatenate(rings_of, axis=0).astype(jnp.bfloat16)
                    for rings_of in ((low, high), (empty, low), (high, empty))
                ],
            ))
        members = [jnp.zeros((points, 2 * LANES), jnp.float32) for _ in range(2)]
        done = 0
        for ring in range(0, rings, 2):
            for pair in range(4):
                lowest, (here, after, ahead) = patterns[pair]
                none = jnp.zeros((16, LANES), jnp.bfloat16)
                for start in range(0, 2 * RING, 16):
                    rows = slice(start, start + 16)
                    block = none
                    if start < RING:
                        block = jnp.where(lowest == float(ring - 1), ahead[rows], block)
                    if start + 16 > RING:
                        block = jnp.where(lowest == float(ring + 1), after[rows], block)
                    block = jnp.where(lowest == float(ring), here[rows], block)
                    matrix[ring * RING + start:ring * RING + start + 16,
                           wide + pair * LANES:wide + (pair + 1) * LANES] = block
            ready = (ring + 2) * RING
            while done < depth and (ready >= done + ROWS or ready == used):
                size = min(ROWS, depth - done)
                for mirror in range(2):
                    members[mirror] = members[mirror] + jnp.dot(
                        low_t[:, done:done + size],
                        matrix[done:done + size, wide + mirror * 2 * LANES:wide + (mirror + 1) * 2 * LANES],
                        preferred_element_type=jnp.float32,
                    )
                done += size
        return members

    def interact(chunk, members):
        lanes = slice(chunk * LANES, (chunk + 1) * LANES)
        wide = chunk * 4 * LANES
        valid = min(LANES, count_bins - chunk * LANES)
        rows = slice(chunk * LANES, chunk * LANES + valid)
        values = flat_t[:, lanes]
        coef = nl_pad[:, lanes]
        turned = []
        for mirror in range(2):
            third = members[mirror][:, :LANES]
            fourth = members[mirror][:, LANES:]
            interaction = coef * (
                values * values * (COEF_THREE * third + COEF_FOUR * fourth)
                - 2.0 * COEF_BOTH * values * third * fourth
            )
            turned.append([interaction[half * LANES:(half + 1) * LANES].T for half in range(points // LANES)])
        for half in range(points // LANES):
            span = slice(half * LANES, (half + 1) * LANES)
            for mirror in range(2):
                low = turned[mirror][half].astype(jnp.bfloat16)
                for member in range(2):
                    start = wide + (mirror * 2 + member) * LANES
                    inter[start:start + LANES, span] = low
            drive = jnp.maximum(
                wind[0:1, span] * tables[0, rows, :] + wind[1:2, span] * tables[1, rows, :], 0.0
            )
            here = spectra[rows, span]
            both = (turned[0][half] + turned[1][half])[:valid]
            total[rows, span] = here + WIND_RATE * drive * here - 2.0 * both

    previous = None
    for chunk in range(chunks):
        members = members_of(chunk)
        if previous is not None:
            interact(chunk - 1, previous)
        previous = members
    interact(chunks - 1, previous)
    added = 0
    packed = 0
    owners = [(side, member) for side in range(plan.halves) for member in range(plan.members)]
    for start in range(0, used, ROWS):
        size = min(ROWS, used - start)
        spaced[start:start + size, :] = jnp.dot(
            matrix[start:start + size, :], inter[...], preferred_element_type=jnp.float32
        )
        while added < rings and added * RING + NTH <= start + size:
            total[added * NTH:(added + 1) * NTH, :] += spaced[added * RING:added * RING + NTH, :]
            added += 1
        while packed < len(owners):
            side, member = owners[packed]
            if min(side * plan.half_bins + (member + 1) * plan.per, count_bins) > added * NTH:
                break
            pack_payload(plan, first_point, total, out, twice, side, member)
            packed += 1


def pack_payload(plan, first_point, total, out, twice, side, member):
    points = total.shape[1]
    main, rest, fold = plan.main, plan.rest, plan.fold
    lane = lax.broadcasted_iota(jnp.int32, (1, LANES), 1)
    first = side * plan.half_bins + member * plan.per
    valid = min(main, plan.half_bins - member * plan.per)
    slot = (side * plan.members + member) % 2
    for half in range(points // LANES):
        values = total[first:first + valid, half * LANES:(half + 1) * LANES]
        if valid < LANES:
            values = jnp.concatenate([values, jnp.zeros((LANES - valid, LANES), jnp.float32)], axis=0)
        turned = values.T
        twice[slot, half * LANES:(half + 1) * LANES, :] = turned
        twice[slot, points + half * LANES:points + (half + 1) * LANES, :] = turned
    for part in range(plan.parts):
        owner = (part * plan.members + member) * plan.halves + side
        begin = lax.rem(first_point[part], points)
        for low, high in ((0, FIRST), (FIRST, COMMON), (COMMON, points)):
            row = plan.row_of(low)
            out[owner, row:row + high - low, :] = twice[slot, pl.ds(begin + low, high - low), :]
        if not rest:
            continue
        shift = lax.rem(begin, LANES)
        swapped = begin >= LANES
        near = pltpu.roll(total[first + main:first + main + rest, :LANES], lax.rem(LANES - shift, LANES), 1)
        away = pltpu.roll(total[first + main:first + main + rest, LANES:], lax.rem(LANES - shift, LANES), 1)
        keep = (lane < LANES - shift) != swapped
        lead = jnp.where(keep, near, away)
        tail = jnp.where(keep, away, near)
        moved = pltpu.roll(tail, LANES // 2, 1)
        out[owner, FIRST:FIRST + rest, :] = lead
        out[owner, FIRST + rest:FIRST + rest + fold, :] = jnp.where(lane < LANES // 2, tail[:fold], moved[rest - fold:])
        out[owner, rest + fold + COMMON:rest + 2 * fold + COMMON, :] = jnp.where(
            lane < LANES // 2, moved[:fold], tail[rest - fold:]
        )


def source_terms(plan, first_point, spectra, wind, index, weight, nl_coef):
    count_bins, points = spectra.shape
    padded = round_up(count_bins, LANES)
    depth = round_up(count_bins // NTH * RING, LANES)
    cosine, sine, _ = bin_tables(count_bins)
    tables = np.stack([cosine, sine]).astype(np.float32)[:, :, None] * np.ones((1, 1, LANES), np.float32)
    smem = pl.BlockSpec(memory_space=pltpu.SMEM)
    vmem = pl.BlockSpec(memory_space=pltpu.VMEM)
    operands = (spectra, wind, index, weight, nl_coef, jnp.asarray(tables))
    return pl.pallas_call(
        functools.partial(source_kernel, plan),
        out_shape=jax.ShapeDtypeStruct((plan.group, plan.rows(points), LANES), jnp.float32),
        in_specs=[smem] + [pl.BlockSpec(memory_space=pl.ANY)] * len(operands),
        out_specs=vmem,
        scratch_shapes=[pltpu.VMEM(operand.shape, operand.dtype) for operand in operands] + [
            pltpu.SemaphoreType.DMA((len(operands),)),
            pltpu.VMEM((24, padded), jnp.int32),
            pltpu.VMEM((16, padded), jnp.float32),
            pltpu.VMEM((1, padded), jnp.float32),
            pltpu.VMEM((depth, points), jnp.float32),
            pltpu.VMEM((points, padded), jnp.float32),
            pltpu.VMEM((points, depth), jnp.bfloat16),
            pltpu.VMEM((depth, 4 * padded), jnp.bfloat16),
            pltpu.VMEM((4 * padded, points), jnp.bfloat16),
            pltpu.VMEM((padded, points), jnp.float32),
            pltpu.VMEM((2, 2 * points, LANES), jnp.float32),
        ],
        compiler_params=pltpu.CompilerParams(vmem_limit_bytes=VMEM_BYTES),
        cost_estimate=pl.CostEstimate(
            flops=4 * depth * 4 * padded * points, bytes_accessed=8 * count_bins * points, transcendentals=0
        ),
        name="source_terms",
    )(first_point, *operands)


def ranks_kernel(plan, sea_total, rank, mask, triangle, need, first_point, floor, rel):
    columns, latitudes = mask.shape
    sea = mask[...].astype(jnp.float32).astype(jnp.bfloat16)

    def product(left, right):
        return jnp.dot(left, right, preferred_element_type=jnp.float32)

    upto = product(sea, triangle[...])
    counts = lax.dot_general(
        jnp.ones((8, latitudes), jnp.bfloat16), sea, (((1,), (1,)), ((), ())), preferred_element_type=jnp.float32
    )
    row = lax.broadcasted_iota(jnp.int32, (columns, columns), 0)
    col = lax.broadcasted_iota(jnp.int32, (columns, columns), 1)
    before_row = product(counts.astype(jnp.bfloat16), jnp.where(row < col, 1.0, 0.0).astype(jnp.bfloat16))
    before_col = jnp.sum(product(jnp.where(col < row, 1.0, 0.0).astype(jnp.bfloat16), sea), axis=1, keepdims=True)
    lane = lax.broadcasted_iota(jnp.int32, (1, columns), 1)
    most = 0
    chosen = 0
    for p in range(plan.parts):
        begin = (p * (columns // plan.parts) - plan.halo) % columns
        inside = (lane + (columns - begin)) & (columns - 1)
        start = jnp.sum(jnp.where(lane == begin, before_row[:1], 0.0)).astype(jnp.int32)
        held = jnp.sum(jnp.where(inside < plan.window, counts[:1], 0.0)).astype(jnp.int32)
        wanted = (held + lax.rem(start, plan.group) + plan.group - 1) // plan.group
        first = jnp.where(wanted * plan.group <= sea_total, start // plan.group, 0)
        first_point[p] = first
        most = jnp.maximum(most, wanted)
        chosen = jnp.where(rank[0] // (plan.halves * plan.members) == p, first, chosen)
    need[0] = most

    def placed(before):
        place = before.astype(jnp.int32) - chosen * plan.group
        place = jnp.where(place < 0, place + sea_total, place)
        return place

    floor[...] = placed(before_row[:1])
    rel[...] = jnp.where(mask[...] == 1, upto.astype(jnp.int32) - 1 + placed(before_col), -1)


def sea_ranks(plan, sea_total, rank, mask):
    columns, latitudes = mask.shape
    smem = pl.BlockSpec(memory_space=pltpu.SMEM)
    vmem = pl.BlockSpec(memory_space=pltpu.VMEM)
    return pl.pallas_call(
        functools.partial(ranks_kernel, plan, sea_total),
        out_shape=[
            jax.ShapeDtypeStruct((1,), jnp.int32),
            jax.ShapeDtypeStruct((plan.parts,), jnp.int32),
            jax.ShapeDtypeStruct((1, columns), jnp.int32),
            jax.ShapeDtypeStruct((columns, latitudes), jnp.int32),
        ],
        in_specs=[smem, vmem, vmem],
        out_specs=[smem, smem, vmem, vmem],
        name="sea_ranks",
    )(rank, mask, jnp.asarray(np.triu(np.ones((latitudes, latitudes))), jnp.bfloat16))


def propagate_kernel(plan, slots, rank, base, got, rel, table, out, taps, arrived, ranked, extra, lined, pick, sea, starts):
    group = got.shape[0]
    columns = plan.window
    all_columns = rel.shape[0]
    shares = plan.halves * plan.members
    begin = rank[0] // shares * (all_columns // plan.parts) + (all_columns - plan.halo)
    copy = pltpu.make_async_copy(table.at[lax.rem(rank[0], shares)], taps, arrived)
    copy.start()
    per, columns_tile, halo = plan.per, plan.columns_tile, plan.halo
    main, rest, fold = plan.main, plan.rest, plan.fold
    half_lanes = lax.broadcasted_iota(jnp.int32, (1, LANES), 1) < LANES // 2
    rest_rows = round_up(rest, 8)

    fill = jnp.zeros((LANES // 2 - rest, LANES), jnp.float32)

    def turned_rest(owner):
        near = got[owner, FIRST + rest:FIRST + rest + fold, :]
        first = near
        second = pltpu.roll(near, LANES // 2, 1)
        if slots > COMMON:
            away = got[owner, rest + fold + COMMON:rest + 2 * fold + COMMON, :]
            first = jnp.where(half_lanes, first, pltpu.roll(away, LANES // 2, 1))
            second = jnp.where(half_lanes, second, away)
        return jnp.concatenate([got[owner, FIRST:FIRST + rest, :], fill, first[:rest - fold], second, fill], axis=0).T

    def order(step, carry):
        owners = [step * BATCH + k for k in range(BATCH)]
        turned = [turned_rest(owner) for owner in owners] if rest else []
        for owner in owners:
            for low, high in ((0, FIRST), (FIRST, min(slots, COMMON)), (COMMON, slots)):
                if high > low:
                    row = plan.row_of(low)
                    ranked[pl.ds(owner + low * group, high - low, stride=group), :] = got[
                        owner, row:row + high - low, :
                    ]
        for owner, values in zip(owners, turned):
            extra[pl.ds(owner, LANES, stride=group), :] = values
        return carry

    lax.fori_loop(0, group // BATCH, order, 0)

    rank_tiles = ranked.shape[0] // LANES
    padded = lined.shape[0]
    main_rows = round_up(main, 8)

    def line_up(tiles):
        starts = [pl.multiple_of(tile * LANES, LANES) for tile in tiles]
        turned = [ranked[pl.ds(start, LANES), :].T[:main_rows] for start in starts]
        for start, values in zip(starts, turned):
            lined[:main_rows, pl.ds(start, LANES)] = values
            if not rest and main % 8:
                lined[main_rows - 8:main_rows, pl.ds(start, LANES)] = values[main - 8:main]

    def line_up_rest(both, tiles):
        starts = [pl.multiple_of(tile * LANES, LANES) for tile in tiles]
        turned = [extra[pl.ds(start, LANES), :].T for start in starts]
        for start, values in zip(starts, turned):
            for half in range(2 if both else 1):
                lanes = pl.ds(start + half * group * LANES, LANES)
                lined[main:main + rest_rows - 8, lanes] = values[half * LANES // 2:half * LANES // 2 + rest_rows - 8]
                lined[main + rest_rows - 8:main + rest_rows, lanes] = values[
                    half * LANES // 2 + rest - 8:half * LANES // 2 + rest
                ]

    def by_four(begin, end, body):
        def step(index, carry):
            body([begin + index * 4 + k for k in range(4)])
            return carry

        lax.fori_loop(0, (end - begin) // 4, step, 0)
        if (end - begin) % 4:
            body([jnp.int32(tile) for tile in range(end - (end - begin) % 4, end)])

    by_four(0, rank_tiles, line_up)
    if rest:
        by_four(0, rank_tiles - group, functools.partial(line_up_rest, True))
        by_four(rank_tiles - group, group, functools.partial(line_up_rest, False))
    lined[:, rank_tiles * LANES:] = jnp.zeros((padded, 2 * LANES), jnp.float32)

    for column in range(columns):
        source = (begin + column) & (all_columns - 1)
        starts[column] = base[0, source]
        row = jnp.broadcast_to(rel[pl.ds(source, 1), :], (8, LANES))
        pick[column] = row & (LANES - 1)
        sea[column] = jnp.where(row >= 0, 1.0, 0.0)

    lane = lax.broadcasted_iota(jnp.int32, (8, LANES), 1)
    copy.wait()

    def bins_step(tile, carry):
        span = pl.ds(pl.multiple_of(tile * 8, 8), 8)
        first_bin = jnp.minimum(tile * 8, per - 8)
        tap = [jnp.broadcast_to(taps[span, k:k + 1], (8, LANES)) for k in range(10)]
        x_up = tap[0] != 0.0
        x_far = jnp.where(x_up, tap[0], tap[4])
        y_up = tap[5] != 0.0
        far_lane = jnp.where(y_up, lane - 2, lane + 2)
        y_far = jnp.where((far_lane >= 0) & (far_lane < LANES), jnp.where(y_up, tap[5], tap[9]), 0.0)
        far_lane = far_lane & (LANES - 1)
        y_left = jnp.where(lane >= 1, tap[6], 0.0)
        y_right = jnp.where(lane < LANES - 1, tap[8], 0.0)

        def expanded(column):
            place = starts[column]
            offset = place & (LANES - 1)
            start = pl.multiple_of(place - offset, LANES)
            low = lined[span, pl.ds(start, LANES)]
            high = lined[span, pl.ds(start + LANES, LANES)]
            both = jnp.where(lane >= offset, low, high)
            return jnp.take_along_axis(both, pick[column], axis=1) * sea[column]

        def store(result, column):
            owner, place = divmod(column - halo, columns_tile)
            start = (owner * per + first_bin) * columns_tile + place
            out[pl.ds(start, 8, stride=columns_tile), :] = result

        def sweep(values, column):
            left_two, left, here, right, right_two = neighbours(values, column)
            value = tap[2] * here + tap[1] * left + tap[3] * right + x_far * jnp.where(x_up, left_two, right_two)
            value = value * sea[column]
            moved = (
                tap[7] * value + y_left * pltpu.roll(value, 1, 1) + y_right * pltpu.roll(value, LANES - 1, 1)
                + y_far * jnp.take_along_axis(value, far_lane, axis=1)
            )
            return moved * sea[column]

        reach = halo // STEPS
        first = {}

        def neighbours(values, column):
            return [values[(column + k) % columns] for k in range(-2, 3)]

        for column in range(columns):
            first[column] = expanded(column)
        middle = {column: sweep(first, column) for column in range(reach, columns - reach)}
        results = {column: sweep(middle, column) for column in range(halo, columns - halo)}
        for column, result in results.items():
            store(result, column)
        return carry

    lax.fori_loop(0, -(-per // 8), bins_step, 0)


def propagate(plan, slots, rank, base, got, rel, table):
    columns = plan.window
    padded = round_up(plan.per, 8)
    ranks = plan.group * slots
    smem = pl.BlockSpec(memory_space=pltpu.SMEM)
    vmem = pl.BlockSpec(memory_space=pltpu.VMEM)
    return pl.pallas_call(
        functools.partial(propagate_kernel, plan, slots),
        out_shape=jax.ShapeDtypeStruct(((columns - 2 * plan.halo) * plan.per, LANES), jnp.float32),
        in_specs=[smem, smem, vmem, vmem, pl.BlockSpec(memory_space=pl.ANY)],
        out_specs=vmem,
        scratch_shapes=[
            pltpu.VMEM((padded, LANES), jnp.float32),
            pltpu.SemaphoreType.DMA,
            pltpu.VMEM((ranks, LANES), jnp.float32),
            pltpu.VMEM((LANES * plan.group if plan.rest else 8, LANES), jnp.float32),
            pltpu.VMEM((padded, ranks + 2 * LANES), jnp.float32),
            pltpu.VMEM((columns, 8, LANES), jnp.int32),
            pltpu.VMEM((columns, 8, LANES), jnp.float32),
            pltpu.SMEM((columns,), jnp.int32),
        ],
        compiler_params=pltpu.CompilerParams(vmem_limit_bytes=VMEM_BYTES),
        name="propagate",
    )(rank, base, got, rel, table)


@dataclasses.dataclass(frozen=True)
class Plan:
    tiles: int
    halves: int
    parts: int
    half_bins: int
    columns: int

    @property
    def group(self):
        return self.tiles * self.halves

    @property
    def members(self):
        return self.tiles // self.parts

    @property
    def per(self):
        return -(-self.half_bins // self.members)

    @property
    def main(self):
        return min(self.per, LANES)

    @property
    def rest(self):
        return self.per - self.main

    @property
    def fold(self):
        return -(-self.rest // 2)

    @property
    def columns_tile(self):
        return self.columns // self.tiles

    @property
    def halo(self):
        return 2 * STEPS if self.parts > 1 else 0

    @property
    def window(self):
        return self.columns // self.parts + 2 * self.halo

    def row_of(self, point):
        return point + (self.rest + self.fold if point >= FIRST else 0) + (self.fold if point >= COMMON else 0)

    def rows(self, slots):
        return self.rest + (2 if slots > COMMON else 1) * self.fold + slots


def shards(spectra, wind, mask, dia_index, dia_weight, nl_coef):
    count_bins, points = spectra.shape
    columns, latitudes = mask.shape
    plan = Plan(
        tiles=lax.axis_size("tile"), halves=lax.axis_size("bin"), parts=2,
        half_bins=count_bins // lax.axis_size("bin"), columns=columns,
    )
    members, parts = plan.members, plan.parts
    sea_total = plan.group * points
    tile_rank = lax.axis_index("tile")

    rank = (
        tile_rank // members * (plan.halves * members) + lax.axis_index("bin") * members + tile_rank % members
    ).astype(jnp.int32).reshape(1)
    need, first_point, floor, rel = sea_ranks(plan, sea_total, rank, mask)
    wanted = need
    bands = lax.axis_size("band")
    for step in range(1, bands):
        wanted = jnp.maximum(
            wanted, lax.ppermute(need, "band", [(band, (band + step) % bands) for band in range(bands)])
        )
    wanted = wanted[0]

    payload = source_terms(plan, first_point, spectra, wind, dia_index, dia_weight, nl_coef)

    cosine, sine, speed = bin_tables(count_bins)
    weights = np.concatenate([stencil(speed * cosine), stencil(speed * sine)])
    table = np.zeros((plan.halves, members, round_up(plan.per, 8), LANES), np.float32)
    for side in range(plan.halves):
        for member in range(members):
            valid = max(0, min(plan.per, plan.half_bins - member * plan.per))
            begin = side * plan.half_bins + member * plan.per
            table[side, member, :valid, :10] = weights[:, begin:begin + valid].T
            if plan.per % 8:
                table[side, member, -8:] = table[side, member, plan.per - 8:plan.per].copy()
    table = jnp.asarray(table.reshape((plan.halves * members,) + table.shape[2:]))

    def with_slots(slots):
        def run(payload, rank, floor, rel, table):
            got = lax.all_to_all(
                payload[:, :plan.rows(slots)], ("tile", "bin"), split_axis=0, concat_axis=0, tiled=True
            )
            return propagate(plan, slots, rank, floor, got, rel, table)

        return run

    sizes = [size for size in SIZES if size < points] + [points]
    choice = sum((wanted > size).astype(jnp.int32) for size in sizes[:-1])
    moved = lax.switch(choice, [with_slots(size) for size in sizes], payload, rank, floor, rel, table)
    result = lax.all_to_all(
        moved.reshape(members, plan.per, plan.columns_tile, latitudes), "tile", split_axis=0, concat_axis=0,
        axis_index_groups=[list(range(p * members, (p + 1) * members)) for p in range(parts)], tiled=True,
    ).reshape(members * plan.per, plan.columns_tile, latitudes)
    return result[:plan.half_bins]


def solution(mesh):
    in_specs = (
        P(None, ("band", "tile", "bin")),
        P(None, ("band", "tile", "bin")),
        P(None, "band"),
        P(),
        P(),
        P(),
    )
    out_specs = P("bin", "tile", "band")
    return jax.shard_map(shards, mesh=mesh, in_specs=in_specs, out_specs=out_specs, check_vma=False)
```
